256 devices in a mesh: lat: 8 (over y, x_hi), lon: 32 (over x_lo, z, core).
Axes of the slice: x: 4 (x_hi: 2, x_lo: 2; x = x_hi * 2 + x_lo), y: 4, z: 8, core: 2. Of those that a mesh axis runs over, the one named last changes fastest.
Arguments:
- tokens: bfloat16 [192, 768, 512], P('lat', 'lon'), may hold values from -6 to 6
- cotangent: bfloat16 [192, 768, 512], P('lat', 'lon'), may hold values from -6 to 6
- norm_gain: float32 [512], replicated, may hold values from 0.5 to 1.5
- w_qkv: bfloat16 [512, 1536], replicated, may hold values from -8 to 8
- w_proj: bfloat16 [512, 512], replicated, may hold values from -0.25 to 0.25
- merge_gain: float32 [2048], replicated, may hold values from 0.5 to 1.5
- w_merge: bfloat16 [2048, 1024], replicated, may hold values from -0.125 to 0.125
- w_expand: bfloat16 [1024, 2048], replicated, may hold values from -0.1875 to 0.1875
- expand_gain: float32 [512], replicated, may hold values from 0.5 to 1.5
Outputs:
- d_tokens: bfloat16 [192, 768, 512], P('lat', 'lon')
- grad_qkv: float32 [512, 1536], P('lon')
- grad_proj: float32 [512, 512], P('lon')
The draws below stay inside these ranges and needn't reach their ends.
All inputs are finite; a program needn't handle non-finite values.
Results may differ from the reference program's by a relative error of at most 0.04.
Values may be sent and summed in bfloat16 or wider, within the bound.
No kernel may reach another device: no remote copies, remote signals or barrier semaphores. Data moves between devices by JAX's collectives and lax.ppermute only.
A program may use at most 128 MiB of HBM per device.

```python
import jax
import jax.numpy as jnp
from jax import lax

D = 512
HEADS = 8
WLAT = 6
WLON = 12
SLAT = 3
SLON = 6
LAT = 192
LON = 768


def draw_w_qkv(key, part):
    key = jax.random.fold_in(key, 11)
    first_key = jax.random.fold_in(key, 0)
    matrix = jnp.clip(jax.random.normal(first_key, (D, 3 * D), jnp.float32), -6.0, 6.0) * D ** (-0.5)
    return matrix.astype(jnp.bfloat16)


def levels(key, extent, shards, smallest, high):
    def one(position, parts):
        steps = jax.random.uniform(jax.random.fold_in(jax.random.fold_in(key, 6), position), (parts,), jnp.float32, smallest / len(shards), high / len(shards))
        return jnp.repeat(jnp.exp(steps), extent[position] // parts).reshape((-1,) + (1,) * (len(extent) - position - 1))

    gain = one(*shards[0])
    for cut in shards[1:]:
        gain = gain * one(*cut)
    return gain


def bell_draw(rng, dims, width, reach, shards=(), kind=jnp.bfloat16):
    values = jax.random.normal(rng, dims, jnp.float32) * width
    if len(shards) > 0:
        values = levels(rng, dims, shards, -0.22, 0.18) * values
    return jnp.clip(values, min=-reach, max=reach).astype(kind)


def setup_inputs(seed: int = 0) -> dict:
    key_list = jax.random.split(jax.random.key(seed), 10)
    return {
        "tokens": bell_draw(key_list[0], (LAT, LON, D), 1.0, 6.0, ((0, 8), (1, 32))),
        "cotangent": bell_draw(key_list[1], (LAT, LON, D), 1.0, 6.0, ((0, 8), (1, 32))),
        "norm_gain": jnp.clip(1.0 + 0.1 * jax.random.normal(key_list[2], (D,), jnp.float32), 0.5, 1.5),
        "w_qkv": draw_w_qkv(jax.random.fold_in(key_list[9], 71), 0),
        "w_proj": bell_draw(key_list[4], (D, D), D ** -0.5, 0.25),
        "merge_gain": jnp.clip(1.0 + 0.1 * jax.random.normal(key_list[5], (4 * D,), jnp.float32), 0.5, 1.5),
        "w_merge": bell_draw(key_list[6], (4 * D, 2 * D), (4 * D) ** -0.5, 0.125),
        "w_expand": bell_draw(key_list[7], (2 * D, 4 * D), (2 * D) ** -0.5, 0.1875),
        "expand_gain": jnp.clip(1.0 + 0.1 * jax.random.normal(key_list[8], (D,), jnp.float32), 0.5, 1.5),
    }


EPSILON = 1e-05

def layer_norm(values, norm_scale):
    average = lax.optimization_barrier(jnp.mean(values, axis=-1, keepdims=True))
    centred = values - average
    spread = lax.optimization_barrier(jnp.mean(centred * centred, axis=-1, keepdims=True))
    return centred * lax.rsqrt(spread + EPSILON) * norm_scale.astype(jnp.float32)

def pre_norm(values, norm_scale):
    return layer_norm(values, norm_scale).astype(jnp.bfloat16)

def window_attn(qkv_tile, row_class):
    tile_rows, tile_cols, channels = qkv_tile.shape
    model_width = channels // 3
    head_size = model_width // HEADS
    row_windows = tile_rows // WLAT
    col_windows = tile_cols // WLON
    split_heads = qkv_tile.reshape(row_windows, WLAT, col_windows, WLON, 3, HEADS, head_size)
    split_heads = split_heads.transpose(4, 0, 2, 5, 1, 3, 6).reshape(3, row_windows, col_windows, HEADS, WLAT * WLON, head_size)
    queries = split_heads[0]
    key_heads = split_heads[1]
    value_heads = split_heads[2]
    scores = jnp.einsum('rchqd,rchkd->rchqk', queries, key_heads, preferred_element_type=jnp.float32) * head_size ** (-0.5)
    token_class = jnp.broadcast_to(row_class.reshape(row_windows, WLAT, 1), (row_windows, WLAT, WLON)).reshape(row_windows, WLAT * WLON)
    allowed = token_class[:, :, None] == token_class[:, None, :]
    scores = jnp.where(allowed[:, None, None], scores, -1000000000.0)
    row_top = lax.optimization_barrier(jnp.max(scores, axis=-1, keepdims=True))
    weights = jnp.exp(scores - row_top)
    attn_probs = (weights / lax.optimization_barrier(jnp.sum(weights, axis=-1, keepdims=True))).astype(jnp.bfloat16)
    attended = jnp.einsum('rchqk,rchkd->rchqd', attn_probs, value_heads, preferred_element_type=jnp.float32).astype(jnp.bfloat16)
    attended = attended.reshape(row_windows, col_windows, HEADS, WLAT, WLON, head_size).transpose(0, 3, 1, 4, 2, 5)
    return attended.reshape(tile_rows, tile_cols, model_width)

def banded_attn(qkv_tile, row_class):
    tile_rows, tile_cols, channels = qkv_tile.shape
    bands = qkv_tile.reshape(tile_rows // WLAT, WLAT, tile_cols, channels)
    band_class = row_class.reshape(tile_rows // WLAT, WLAT)
    result = lax.map(lambda banded: window_attn(banded[0], banded[1]), (bands, band_class))
    return result.reshape(tile_rows, tile_cols, channels // 3)

def coarse_branch(fine_vals, merge_gain, w_merge, w_expand, expand_gain):
    tile_rows, tile_cols, model_width = fine_vals.shape
    blocks = fine_vals.astype(jnp.bfloat16).reshape(tile_rows // 2, 2, tile_cols // 2, 2, model_width)
    blocks = blocks.transpose(0, 2, 3, 1, 4).reshape(tile_rows // 2, tile_cols // 2, 4 * model_width)
    merged = layer_norm(blocks.astype(jnp.float32), merge_gain).astype(jnp.bfloat16)
    coarse = jnp.dot(merged, w_merge, preferred_element_type=jnp.float32).astype(jnp.bfloat16)
    widened = jnp.dot(coarse, w_expand, preferred_element_type=jnp.float32)
    widened = widened.reshape(tile_rows // 2, tile_cols // 2, 2, 2, model_width).transpose(0, 2, 1, 3, 4)
    return layer_norm(widened.reshape(tile_rows, tile_cols, model_width), expand_gain)

def reference(tokens, cotangent, norm_gain, w_qkv, w_proj, merge_gain, w_merge, w_expand, expand_gain):
    rolled = jnp.roll(tokens, (-SLAT, -SLON), axis=(0, 1))
    initial_rows = (jnp.arange(LAT).astype(jnp.int32) + SLAT) % LAT
    row_class = (initial_rows < SLAT).astype(jnp.int32)
    rolled_f = rolled.astype(jnp.float32)
    normed, norm_back = jax.vjp(lambda values: pre_norm(values, norm_gain), rolled_f)
    qkv = jnp.dot(normed, w_qkv, preferred_element_type=jnp.float32).astype(jnp.bfloat16)
    attn, attn_back = jax.vjp(lambda inner: banded_attn(inner, row_class), qkv)
    fine_rolled = (rolled_f + jnp.dot(attn, w_proj, preferred_element_type=jnp.float32)).astype(jnp.bfloat16)
    fine_out = jnp.roll(fine_rolled, (SLAT, SLON), axis=(0, 1))
    branch, branch_back = jax.vjp(lambda fine_vals: coarse_branch(fine_vals, merge_gain, w_merge, w_expand, expand_gain), fine_out.astype(jnp.float32))
    cot_f = cotangent.astype(jnp.float32)
    d_branch = branch_back(cot_f)[0]
    grad_fine = (cot_f + d_branch).astype(jnp.bfloat16)
    grad_rolled = jnp.roll(grad_fine, (-SLAT, -SLON), axis=(0, 1))
    d_attn = jnp.einsum('rcf,df->rcd', grad_rolled, w_proj, preferred_element_type=jnp.float32).astype(jnp.bfloat16)
    d_qkv = attn_back(d_attn)[0]
    grad_qkv = jnp.einsum('rcd,rcf->df', normed, d_qkv, preferred_element_type=jnp.float32)
    grad_proj = jnp.einsum('rcd,rcf->df', attn, grad_rolled, preferred_element_type=jnp.float32)
    d_normed = jnp.einsum('rcf,df->rcd', d_qkv, w_qkv, preferred_element_type=jnp.float32).astype(jnp.bfloat16)
    d_rolled = (grad_rolled.astype(jnp.float32) + norm_back(d_normed)[0]).astype(jnp.bfloat16)
    d_tokens = jnp.roll(d_rolled, (SLAT, SLON), axis=(0, 1))
    return (d_tokens, grad_qkv, grad_proj)
```

```python
import functools

import jax
import jax.numpy as jnp
import numpy as np
from jax import lax
from jax.experimental import pallas as pl
from jax.experimental.pallas import tpu as pltpu
from jax.sharding import Mesh, PartitionSpec as P

HEADS = 8
HEAD = 64
WLAT = 6
WLON = 12
SLAT = 3
SLON = 6
D = 512
ROWS = 24
COLS = 24
WR = WLAT * COLS
NWR = 6
XROWS = WLAT * NWR
CROWS = 28
PAIRS = 13
QROWS = 160

EPSILON = 1e-05
MASKED = -1000000000.0
OUTSIDE = -3.0e38
BF = jnp.bfloat16
F32 = jnp.float32


def to_offsets(pairs, lead, span, padded):
    out = np.zeros((4 * padded, span), np.float32)
    for a in range(pairs):
        for rp in range(2):
            for col in range(COLS):
                q = (col % 2) * 2 + rp
                out[q * padded + a * 12 + col // 2, lead + (2 * a + rp) * COLS + col] = 1
    return out.astype(jnp.bfloat16)


def from_offsets():
    out = np.zeros((4, WR, 256), np.float32)
    for k in range(1, 5):
        for t in range(WR):
            f = WLAT * k + t // COLS
            col = t % COLS
            a, rp = divmod(f - 5, 2)
            q = (col % 2) * 2 + rp
            out[k - 1, t, q * 64 + 12 * a + col // 2 - 32 * (k - 1)] = 1
    return out.astype(jnp.bfloat16)


def dot(a, b):
    return jnp.dot(a, b, preferred_element_type=F32)


def dot_nt(a, b):
    return lax.dot_general(a, b, (((1,), (1,)), ((), ())), preferred_element_type=F32)


def dot_tn(a, b):
    return lax.dot_general(a, b, (((0,), (0,)), ((), ())), preferred_element_type=F32)


def norm_parts(values):
    average = jnp.mean(values, axis=-1, keepdims=True)
    centred = values - average
    spread = jnp.mean(centred * centred, axis=-1, keepdims=True)
    scale = lax.rsqrt(spread + EPSILON)
    return centred * scale, scale


def norm_back(hat, scale, dy):
    mean_dy = jnp.mean(dy, axis=-1, keepdims=True)
    mean_dyh = jnp.mean(dy * hat, axis=-1, keepdims=True)
    return scale * (dy - mean_dy - hat * mean_dyh)


def kernel(
    place, x_ref, c_ref, ng_ref, mg_ref, eg_ref, pf_ref, pf3_ref, pc_ref, pc3_ref, pi_ref,
    wqkv_hbm, wproj_hbm, wm_hbm, we_hbm,
    dwork_ref, mine_ref, other_ref,
    wqkv, wproj, wm, we, normed, qkv, probs, attn, fine, fq, cq, mg, dw, gq, gn, dqkv, sems,
):
    lat = place[0]
    lat_size = place[1]
    core = place[2]
    loads = [
        pltpu.make_async_copy(src, dst, sems.at[i])
        for i, (src, dst) in enumerate(
            ((wqkv_hbm, wqkv), (wproj_hbm, wproj), (wm_hbm, wm), (we_hbm, we))
        )
    ]
    for load in loads:
        load.start()

    tq = lax.broadcasted_iota(jnp.int32, (WR, WR), 0)
    tk = lax.broadcasted_iota(jnp.int32, (WR, WR), 1)
    cross = ((tq % COLS) >= WLON) != ((tk % COLS) >= WLON)
    halves = (tq >= WR // 2) != (tk >= WR // 2)
    plain = jnp.where(cross, OUTSIDE, 0.0)
    edged = jnp.where(cross, OUTSIDE, jnp.where(halves, MASKED, 0.0))
    lane = lax.broadcasted_iota(jnp.int32, (1, 2 * HEAD), 1)
    low = (lane < HEAD).astype(F32)
    first_lane = lane < HEAD

    def bias_of(k):
        edge = ((k == 0) & (lat == 0)) | ((k == 4) & (lat == lat_size - 1))
        return jnp.where(edge, edged, plain)

    loads[0].wait()
    loads[1].wait()

    def forward(k, carry):
        start = pl.multiple_of(k * WR, 16)
        span = pl.ds(start, WR)
        bias = bias_of(k)
        x = x_ref[span, :].astype(F32)
        hat, _ = norm_parts(x)
        nrm = (hat * ng_ref[...]).astype(BF)
        normed[span, :] = nrm
        qkv[span, :] = dot(nrm, wqkv[...]).astype(BF)
        for hp in range(HEADS // 2):
            q2 = qkv[span, 128 * hp : 128 * hp + 128]
            k2 = qkv[span, D + 128 * hp : D + 128 * hp + 128]
            v2 = qkv[span, 2 * D + 128 * hp : 2 * D + 128 * hp + 128]
            outs = []
            for half in range(2):
                keep = (low if half == 0 else 1.0 - low) * 0.125
                s = dot_nt(q2 * keep.astype(BF), k2)
                s = jnp.where(bias == 0.0, s, bias)
                e = jnp.exp(s - jnp.max(s, axis=-1, keepdims=True))
                p = e * (1.0 / jnp.sum(e, axis=-1, keepdims=True))
                probs[k, 2 * hp + half] = p
                outs.append(dot(p.astype(BF), v2))
            attn[span, 128 * hp : 128 * hp + 128] = jnp.where(first_lane, outs[0], outs[1]).astype(BF)
        fine[span, :] = (x + dot(attn[span, :], wproj[...])).astype(BF)
        return carry

    lax.fori_loop(0, NWR, forward, 0)

    for g in range(4):
        if g < 3:
            f = dot(pf_ref[...], fine[112 + 192 * g : 112 + 192 * g + 208, :]).astype(BF)
            c = dot(pc_ref[...], c_ref[48 + 192 * g : 48 + 192 * g + 192, :]).astype(BF)
            n = 48
        else:
            f = dot(pf3_ref[...], fine[688:752, :]).astype(BF)
            c = dot(pc3_ref[...], c_ref[624:672, :]).astype(BF)
            n = 16
        for q in range(4):
            fq[q, 48 * g : 48 * g + n, :] = f[n * q : n * q + n]
            cq[q, 48 * g : 48 * g + n, :] = c[n * q : n * q + n]

    def merge_stats(rows):
        total = jnp.zeros((32, 1), F32)
        for q in range(4):
            total = total + jnp.sum(fq[q, rows, :].astype(F32), axis=-1, keepdims=True)
        average = total * (1.0 / (4 * D))
        total = jnp.zeros((32, 1), F32)
        for q in range(4):
            centred = fq[q, rows, :].astype(F32) - average
            total = total + jnp.sum(centred * centred, axis=-1, keepdims=True)
        return average, lax.rsqrt(total * (1.0 / (4 * D)) + EPSILON)

    for r in range(QROWS // 32):
        rows = slice(32 * r, 32 * r + 32)
        average, scale = merge_stats(rows)
        for q in range(4):
            hat = (fq[q, rows, :].astype(F32) - average) * scale
            mg[rows, D * q : D * q + D] = (hat * mg_ref[:, D * q : D * q + D]).astype(BF)

    loads[2].wait()
    loads[3].wait()
    coarse = dot(mg[...], wm[...]).astype(BF)
    for q in range(4):
        qq = (0, 2, 1, 3)[q]
        wide = dot(coarse, we[:, D * qq : D * qq + D])
        hat, scale = norm_parts(wide)
        dy = cq[q].astype(F32) * eg_ref[...]
        dw[:, D * qq : D * qq + D] = norm_back(hat, scale, dy).astype(BF)
    d_coarse = dot_nt(dw[...], we[...]).astype(BF)
    mg[...] = dot_nt(d_coarse, wm[...]).astype(BF)

    for r in range(QROWS // 32):
        rows = slice(32 * r, 32 * r + 32)
        average, scale = merge_stats(rows)
        sum_dy = jnp.zeros((32, 1), F32)
        sum_dyh = jnp.zeros((32, 1), F32)
        for q in range(4):
            hat = (fq[q, rows, :].astype(F32) - average) * scale
            dy = mg[rows, D * q : D * q + D].astype(F32) * mg_ref[:, D * q : D * q + D]
            sum_dy = sum_dy + jnp.sum(dy, axis=-1, keepdims=True)
            sum_dyh = sum_dyh + jnp.sum(dy * hat, axis=-1, keepdims=True)
        mean_dy = sum_dy * (1.0 / (4 * D))
        mean_dyh = sum_dyh * (1.0 / (4 * D))
        for q in range(4):
            hat = (fq[q, rows, :].astype(F32) - average) * scale
            dy = mg[rows, D * q : D * q + D].astype(F32) * mg_ref[:, D * q : D * q + D]
            back = (scale * (dy - mean_dy - hat * mean_dyh)).astype(BF)
            gq[q, rows, :] = (cq[q, rows, :].astype(F32) + back.astype(F32)).astype(BF)

    for k in range(4):
        parts = jnp.concatenate([gq[q, 32 * k : 32 * k + 64, :] for q in range(4)], axis=0)
        gn[WR * k : WR * k + WR, :] = dot(pi_ref[k], parts).astype(BF)

    def backward(k, carry):
        xspan = pl.ds(pl.multiple_of(k * WR, 16), WR)
        gspan = pl.ds(pl.multiple_of((k - 1) * WR, 16), WR)
        bias = bias_of(k)
        g = gn[gspan, :]
        d_attn = dot_nt(g, wproj[...]).astype(BF)
        for hp in range(HEADS // 2):
            q2 = qkv[xspan, 128 * hp : 128 * hp + 128]
            k2 = qkv[xspan, D + 128 * hp : D + 128 * hp + 128]
            v2 = qkv[xspan, 2 * D + 128 * hp : 2 * D + 128 * hp + 128]
            do2 = d_attn[:, 128 * hp : 128 * hp + 128]
            dqs, dks, dvs = [], [], []
            for half in range(2):
                keep = (low if half == 0 else 1.0 - low).astype(BF)
                p = probs[k, 2 * hp + half]
                dp = dot_nt(do2 * keep, v2).astype(BF).astype(F32)
                ds = p * (dp - jnp.sum(dp * p, axis=-1, keepdims=True))
                ds = jnp.where(bias == 0.0, ds, 0.0).astype(BF)
                dqs.append(dot(ds, k2))
                dks.append(dot_tn(ds, q2))
                dvs.append(dot_tn(p.astype(BF), do2))
            for part, two in enumerate((dqs, dks, dvs)):
                both = jnp.where(first_lane, two[0], two[1])
                if part < 2:
                    both = both * 0.125
                dqkv[gspan, D * part + 128 * hp : D * part + 128 * hp + 128] = both.astype(BF)
        d_normed = dot_nt(dqkv[gspan, :], wqkv[...]).astype(BF).astype(F32)
        hat, scale = norm_parts(x_ref[xspan, :].astype(F32))
        back = norm_back(hat, scale, d_normed * ng_ref[...])
        dwork_ref[gspan, :] = (g.astype(F32) + back).astype(BF)
        return carry

    lax.fori_loop(1, 5, backward, 0)

    def put(columns, block):
        pairs = block.astype(BF).reshape(mine_ref.shape[0], 2, mine_ref.shape[1], block.shape[1])
        even, odd = pairs[:, 0], pairs[:, 1]
        mine_ref[:, :, columns] = jnp.where(core == 0, even, odd)
        other_ref[:, :, columns] = jnp.where(core == 0, odd, even)

    inner = slice(WR, 5 * WR)
    for j in range(3):
        put(slice(D * j, D * j + D), dot_tn(normed[inner, :], dqkv[:, D * j : D * j + D]))
    put(slice(3 * D, 4 * D), dot_tn(attn[inner, :], gn[...]))


def compute(tiles, place, x, c, norm_gain, w_qkv, w_proj, merge_gain, w_merge, w_expand, expand_gain):
    vmem = pl.BlockSpec(memory_space=pltpu.VMEM)
    hbm = pl.BlockSpec(memory_space=pl.ANY)
    bf = lambda *shape: pltpu.VMEM(shape, BF)
    return pl.pallas_call(
        kernel,
        out_shape=(
            jax.ShapeDtypeStruct((4 * WR, D), BF),
            jax.ShapeDtypeStruct((tiles, D // (2 * tiles), 4 * D), BF),
            jax.ShapeDtypeStruct((tiles, D // (2 * tiles), 4 * D), BF),
        ),
        in_specs=[pl.BlockSpec(memory_space=pltpu.SMEM)] + [vmem] * 10 + [hbm] * 4,
        out_specs=(vmem, vmem, vmem),
        scratch_shapes=[
            bf(D, 3 * D), bf(D, D), bf(4 * D, 2 * D), bf(2 * D, 4 * D),
            bf(NWR * WR, D), bf(NWR * WR, 3 * D), pltpu.VMEM((NWR, HEADS, WR, WR), F32),
            bf(NWR * WR, D), bf(NWR * WR, D),
            bf(4, QROWS, D), bf(4, QROWS, D), bf(QROWS, 4 * D), bf(QROWS, 4 * D), bf(4, QROWS, D),
            bf(4 * WR, D), bf(4 * WR, 3 * D),
            pltpu.SemaphoreType.DMA((4,)),
        ],
        compiler_params=pltpu.CompilerParams(vmem_limit_bytes=58 * 1024 * 1024),
        name="block",
    )(
        place, x, c, norm_gain[None], merge_gain[None], expand_gain[None],
        jnp.asarray(to_offsets(4, 8, 208, 48)), jnp.asarray(to_offsets(1, 8, 64, 16)),
        jnp.asarray(to_offsets(4, 0, 192, 48)), jnp.asarray(to_offsets(1, 0, 48, 16)),
        jnp.asarray(from_offsets()),
        w_qkv, w_proj, w_merge, w_expand,
    )


def body(tokens, cotangent, norm_gain, w_qkv, w_proj, merge_gain, w_merge, w_expand, expand_gain):
    lats, tiles, cores = lax.axis_size("lat"), lax.axis_size("tile"), lax.axis_size("core")
    lons = tiles * cores
    names = ("lat", "tile", "core")

    def moved(value, dlat, dlon):
        pairs = []
        for a in range(lats):
            for b in range(lons):
                pairs.append((a * lons + b, ((a + dlat) % lats) * lons + (b + dlon) % lons))
        return lax.ppermute(value, names, pairs)

    lat = lax.axis_index("lat")
    core = lax.axis_index("core")
    place = jnp.stack([lat, jnp.int32(lats), core]).astype(jnp.int32)

    edge = moved(jnp.concatenate([tokens[:, :SLON], cotangent[:, :SLON]], axis=0), 0, -1)
    work = jnp.concatenate([tokens[:, SLON:], edge[:ROWS]], axis=1)
    cwork = jnp.concatenate([cotangent[:, SLON:], edge[ROWS:]], axis=1)
    below = moved(jnp.concatenate([work[:9], cwork[:4]], axis=0), -1, 0)
    above = moved(work[ROWS - 3 :], 1, 0)
    x = jnp.concatenate([above, work, below[:9]], axis=0).reshape(XROWS * COLS, D)
    c = jnp.concatenate([cwork, below[9:]], axis=0).reshape(CROWS * COLS, D)

    d_work, mine, other = compute(
        tiles, place, x, c, norm_gain, w_qkv, w_proj, merge_gain, w_merge, w_expand, expand_gain
    )

    theirs = lax.ppermute(other, "core", [(i, cores - 1 - i) for i in range(cores)])
    d_work = d_work.reshape(ROWS, COLS, D)
    arrived = moved(d_work[ROWS - SLAT :], 1, 0)
    d_rows = jnp.concatenate([arrived, d_work[: ROWS - SLAT]], axis=0)
    arrived = moved(d_rows[:, COLS - SLON :], 0, 1)
    d_tokens = jnp.concatenate([arrived, d_rows[:, : COLS - SLON]], axis=1)

    pair = (mine.astype(F32) + theirs.astype(F32)).astype(BF)
    spread = lax.all_to_all(pair, "tile", 0, 0, tiled=True)
    share = jnp.sum(spread.astype(F32), axis=0).astype(BF)
    copies = jnp.broadcast_to(share[None], (lats,) + share.shape)
    gathered = lax.all_to_all(copies, "lat", 0, 0, tiled=True)
    total = jnp.sum(gathered.astype(F32), axis=0)
    return (d_tokens, total[:, : 3 * D], total[:, 3 * D :])


def solution(mesh):
    lats, lons = mesh.shape["lat"], mesh.shape["lon"]
    fine_mesh = Mesh(mesh.devices.reshape(lats, lons // 2, 2), ("lat", "tile", "core"))
    lon = ("tile", "core")
    in_specs = (P("lat", lon, None), P("lat", lon, None), P(), P(), P(), P(), P(), P(), P())
    out_specs = (P("lat", lon, None), P(lon, None), P(lon, None))
    return jax.shard_map(body, mesh=fine_mesh, in_specs=in_specs, out_specs=out_specs, check_vma=False)
```

```python
import functools

import jax
import jax.numpy as jnp
import numpy as np
from jax import lax
from jax.experimental import pallas as pl
from jax.experimental.pallas import tpu as pltpu
from jax.sharding import Mesh, PartitionSpec as P

HEADS = 8
HEAD = 64
WLAT = 6
WLON = 12
SLAT = 3
SLON = 6
D = 512
ROWS = 24
COLS = 24
WR = WLAT * COLS
WIN = WLAT * WLON
WP = 80
WRP = 2 * WP
NWR = 6
XROWS = WLAT * NWR
CROWS = 28
PAIRS = 13
QROWS = 160

EPSILON = 1e-05
MASKED = -1000000000.0
OUTSIDE = -3.0e38
BF = jnp.bfloat16
F32 = jnp.float32


def window_row(i, col):
    return (col // WLON) * WP + i * WLON + col % WLON


def to_windows():
    out = np.zeros((WRP, WR), np.float32)
    for t in range(WR):
        out[window_row(t // COLS, t % COLS), t] = 1
    return out.astype(jnp.bfloat16)


def cot_offsets(pairs, padded):
    out = np.zeros((4 * padded, pairs * 2 * COLS), np.float32)
    for a in range(pairs):
        for rp in range(2):
            for col in range(COLS):
                q = (col % 2) * 2 + rp
                out[q * padded + a * 12 + col // 2, (2 * a + rp) * COLS + col] = 1
    return out.astype(jnp.bfloat16)


FINE_PARTS = ((0, 0), (0, 1), (0, 2), (1, 2), (1, 3), (2, 3), (2, 4), (3, 4), (3, 5))


def fine_offsets():
    out = np.zeros((len(FINE_PARTS), 4 * 48, WRP), np.float32)
    for n, (g, k) in enumerate(FINE_PARTS):
        padded = 48 if g < 3 else 16
        for a in range(4 * g, min(4 * g + 4, PAIRS)):
            for rp in range(2):
                f = 5 + 2 * a + rp
                if f // WLAT != k:
                    continue
                for col in range(COLS):
                    q = (col % 2) * 2 + rp
                    out[n, q * padded + (a - 4 * g) * 12 + col // 2, window_row(f % WLAT, col)] = 1
    return out.astype(jnp.bfloat16)


def from_offsets():
    out = np.zeros((4, WRP, 256), np.float32)
    for k in range(1, 5):
        for t in range(WR):
            f = WLAT * k + t // COLS
            col = t % COLS
            a, rp = divmod(f - 5, 2)
            q = (col % 2) * 2 + rp
            out[k - 1, window_row(t // COLS, col), q * 64 + 12 * a + col // 2 - 32 * (k - 1)] = 1
    return out.astype(jnp.bfloat16)


def dot(a, b):
    return jnp.dot(a, b, preferred_element_type=F32)


def dot_nt(a, b):
    return lax.dot_general(a, b, (((1,), (1,)), ((), ())), preferred_element_type=F32)


def dot_tn(a, b):
    return lax.dot_general(a, b, (((0,), (0,)), ((), ())), preferred_element_type=F32)


def norm_parts(values):
    average = jnp.mean(values, axis=-1, keepdims=True)
    centred = values - average
    spread = jnp.mean(centred * centred, axis=-1, keepdims=True)
    scale = lax.rsqrt(spread + EPSILON)
    return centred * scale, scale


def norm_back(hat, scale, dy):
    mean_dy = jnp.mean(dy, axis=-1, keepdims=True)
    mean_dyh = jnp.mean(dy * hat, axis=-1, keepdims=True)
    return scale * (dy - mean_dy - hat * mean_dyh)


def stacked(two, low):
    gap = jnp.zeros((128 - WP, 2 * HEAD), BF)
    return jnp.concatenate([two * low, gap, two * (1 - low), gap], axis=0)


def over_queries(keys_by_queries, rows, first_lane):
    both = [dot_tn(keys_by_queries[:, 128 * i : 128 * i + WP], rows) for i in range(2)]
    return jnp.where(first_lane, both[0], both[1])


def padded_keys(values):
    return jnp.concatenate([values, jnp.zeros((WP - WIN, 256), F32)], axis=0).astype(BF)


UNITS = [(w, hp) for w in range(2) for hp in range(HEADS // 2)]
GROUP = 8


def kernel(
    lat_size, x_ref, c_ref, ng_ref, mg_ref, eg_ref, px_ref, pxt_ref, pf_ref, pc_ref, pc3_ref, pi_ref,
    wqkv_hbm, wproj_hbm, wm_hbm, we_hbm,
    mine_hbm, other_hbm, gn_hbm, dqkv_hbm,
    wqkv, wproj, wm, we, xw, normed, qkv, probs, attn, fine, fq, cq, mg, dw, gq, gn, d_attn, dqkv, mine, other, sems,
):
    lat = lax.axis_index("lat")
    core = lax.axis_index("core")
    loads = [
        pltpu.make_async_copy(src, dst, sems.at[i])
        for i, (src, dst) in enumerate(
            ((wqkv_hbm, wqkv), (wproj_hbm, wproj), (wm_hbm, wm), (we_hbm, we))
        )
    ]
    for load in loads:
        load.start()

    key = lax.broadcasted_iota(jnp.int32, (WIN, 256), 0)
    query = lax.broadcasted_iota(jnp.int32, (WIN, 256), 1) % 128
    apart = (key >= WIN // 2) != (query >= WIN // 2)
    lane = lax.broadcasted_iota(jnp.int32, (1, 2 * HEAD), 1)
    first_lane = lane < HEAD
    low = first_lane.astype(F32).astype(BF)

    def masked_at(k):
        edge = ((k == 0) & (lat == 0)) | ((k == 4) & (lat == lat_size - 1))
        return apart & edge

    loads[0].wait()
    loads[1].wait()

    def prepare(k, carry):
        span = pl.ds(pl.multiple_of(k * WRP, 16), WRP)
        x = dot(px_ref[...], x_ref[pl.ds(pl.multiple_of(k * WR, 16), WR), :])
        xw[span, :] = x.astype(BF)
        hat, _ = norm_parts(x)
        normed[span, :] = (hat * ng_ref[...]).astype(BF)
        return carry

    lax.fori_loop(0, NWR, prepare, 0, unroll=3)
    for j in range(6):
        columns = slice(256 * j, 256 * j + 256)
        qkv[:, columns] = dot(normed[...], wqkv[:, columns]).astype(BF)

    def heads(base, w, hp):
        win = pl.ds(pl.multiple_of(base + WP * w, 16), WP)
        q2 = qkv[win, 128 * hp : 128 * hp + 128]
        k2 = qkv[win, D + 128 * hp : D + 128 * hp + 128]
        v2 = qkv[win, 2 * D + 128 * hp : 2 * D + 128 * hp + 128]
        return stacked(q2 * 0.125, low), k2, v2, win

    def forward(k, carry):
        start = pl.multiple_of(k * WRP, 16)
        masked = masked_at(k)
        for first in range(0, len(UNITS), GROUP):
            group = UNITS[first : first + GROUP]
            parts = [heads(start, w, hp) for w, hp in group]
            s = [dot_nt(k2, qs)[:WIN] for qs, k2, _, _ in parts]
            s = [jnp.where(masked, MASKED, v) for v in s]
            top = [jnp.max(v, axis=0, keepdims=True) for v in s]
            e = [jnp.exp(v - t) for v, t in zip(s, top)]
            total = [jnp.sum(v, axis=0, keepdims=True) for v in e]
            p = [v * (1.0 / t) for v, t in zip(e, total)]
            for (w, hp), v in zip(group, p):
                probs[k, 4 * w + hp] = v
            o = [over_queries(padded_keys(v), v2, first_lane) for v, (_, _, v2, _) in zip(p, parts)]
            for (w, hp), v, (_, _, _, win) in zip(group, o, parts):
                attn[win, 128 * hp : 128 * hp + 128] = v.astype(BF)
        return carry

    lax.fori_loop(0, NWR, forward, 0)
    for j in range(2):
        columns = slice(256 * j, 256 * j + 256)
        fine[:, columns] = (
            xw[:, columns].astype(F32) + dot(attn[...], wproj[:, columns])
        ).astype(BF)

    for g in range(4):
        n = 48 if g < 3 else 16
        f = sum(
            dot(pf_ref[m, : 4 * n, :], fine[WRP * k : WRP * k + WRP, :])
            for m, (gg, k) in enumerate(FINE_PARTS)
            if gg == g
        ).astype(BF)
        if g < 3:
            c = dot(pc_ref[...], c_ref[48 + 192 * g : 48 + 192 * g + 192, :]).astype(BF)
        else:
            c = dot(pc3_ref[...], c_ref[624:672, :]).astype(BF)
        for q in range(4):
            fq[q, 48 * g : 48 * g + n, :] = f[n * q : n * q + n]
            cq[q, 48 * g : 48 * g + n, :] = c[n * q : n * q + n]

    def merge_stats(rows):
        total = jnp.zeros((32, 1), F32)
        for q in range(4):
            total = total + jnp.sum(fq[q, rows, :].astype(F32), axis=-1, keepdims=True)
        average = total * (1.0 / (4 * D))
        total = jnp.zeros((32, 1), F32)
        for q in range(4):
            centred = fq[q, rows, :].astype(F32) - average
            total = total + jnp.sum(centred * centred, axis=-1, keepdims=True)
        return average, lax.rsqrt(total * (1.0 / (4 * D)) + EPSILON)

    for r in range(QROWS // 32):
        rows = slice(32 * r, 32 * r + 32)
        average, scale = merge_stats(rows)
        for q in range(4):
            hat = (fq[q, rows, :].astype(F32) - average) * scale
            mg[rows, D * q : D * q + D] = (hat * mg_ref[:, D * q : D * q + D]).astype(BF)

    loads[2].wait()
    loads[3].wait()
    coarse = dot(mg[...], wm[...]).astype(BF)
    for q in range(4):
        qq = (0, 2, 1, 3)[q]
        wide = dot(coarse, we[:, D * qq : D * qq + D])
        hat, scale = norm_parts(wide)
        dy = cq[q].astype(F32) * eg_ref[...]
        dw[:, D * qq : D * qq + D] = norm_back(hat, scale, dy).astype(BF)
    d_coarse = dot_nt(dw[...], we[...]).astype(BF)
    mg[...] = dot_nt(d_coarse, wm[...]).astype(BF)

    for r in range(QROWS // 32):
        rows = slice(32 * r, 32 * r + 32)
        average, scale = merge_stats(rows)
        sum_dy = jnp.zeros((32, 1), F32)
        sum_dyh = jnp.zeros((32, 1), F32)
        for q in range(4):
            hat = (fq[q, rows, :].astype(F32) - average) * scale
            dy = mg[rows, D * q : D * q + D].astype(F32) * mg_ref[:, D * q : D * q + D]
            sum_dy = sum_dy + jnp.sum(dy, axis=-1, keepdims=True)
            sum_dyh = sum_dyh + jnp.sum(dy * hat, axis=-1, keepdims=True)
        mean_dy = sum_dy * (1.0 / (4 * D))
        mean_dyh = sum_dyh * (1.0 / (4 * D))
        for q in range(4):
            hat = (fq[q, rows, :].astype(F32) - average) * scale
            dy = mg[rows, D * q : D * q + D].astype(F32) * mg_ref[:, D * q : D * q + D]
            back = (scale * (dy - mean_dy - hat * mean_dyh)).astype(BF)
            gq[q, rows, :] = (cq[q, rows, :].astype(F32) + back.astype(F32)).astype(BF)

    for k in range(4):
        parts = jnp.concatenate([gq[q, 32 * k : 32 * k + 64, :] for q in range(4)], axis=0)
        gn[WRP * k : WRP * k + WRP, :] = dot(pi_ref[k], parts).astype(BF)

    stores = []

    def store(src, dst):
        copy = pltpu.make_async_copy(src, dst, sems.at[4 + len(stores)])
        copy.start()
        stores.append(copy)

    def put(j, block):
        columns = slice(D * j, D * j + D)
        pairs = block.astype(BF).reshape(mine.shape[0], 2, mine.shape[1], D)
        even, odd = pairs[:, 0], pairs[:, 1]
        mine[:, :, columns] = jnp.where(core == 0, even, odd)
        other[:, :, columns] = jnp.where(core == 0, odd, even)
        store(other.at[:, :, columns], other_hbm.at[:, :, columns])
        store(mine.at[:, :, columns], mine_hbm.at[:, :, columns])

    inner = slice(WRP, 5 * WRP)
    store(gn, gn_hbm)
    put(3, dot_tn(attn[inner, :], gn[...]))

    for j in range(2):
        columns = slice(256 * j, 256 * j + 256)
        d_attn[:, columns] = dot_nt(gn[...], wproj[columns, :]).astype(BF)

    def backward(k, carry):
        start = pl.multiple_of(k * WRP, 16)
        gstart = pl.multiple_of((k - 1) * WRP, 16)
        masked = masked_at(k)
        for first in range(0, len(UNITS), GROUP):
            group = UNITS[first : first + GROUP]
            parts = [heads(start, w, hp) for w, hp in group]
            gwins = [pl.ds(pl.multiple_of(gstart + WP * w, 16), WP) for w, _ in group]
            do = [
                stacked(d_attn[gwin, 128 * hp : 128 * hp + 128], low)
                for gwin, (_, hp) in zip(gwins, group)
            ]
            dp = [dot_nt(v2, d)[:WIN] for d, (_, _, v2, _) in zip(do, parts)]
            p = [probs[k, 4 * w + hp] for w, hp in group]
            dv = [dot(padded_keys(v), d) for v, d in zip(p, do)]
            dp = [v.astype(BF).astype(F32) for v in dp]
            inner = [jnp.sum(a * b, axis=0, keepdims=True) for a, b in zip(dp, p)]
            ds = [b * (a - c) for a, b, c in zip(dp, p, inner)]
            ds = [padded_keys(jnp.where(masked, 0.0, v)) for v in ds]
            dk = [dot(v, qs) for v, (qs, _, _, _) in zip(ds, parts)]
            dq = [over_queries(v, k2, first_lane) * 0.125 for v, (_, k2, _, _) in zip(ds, parts)]
            for i, (gwin, (w, hp)) in enumerate(zip(gwins, group)):
                lanes = slice(128 * hp, 128 * hp + 128)
                dqkv[gwin, lanes] = dq[i].astype(BF)
                dqkv[gwin, D + lanes.start : D + lanes.stop] = dk[i].astype(BF)
                dqkv[gwin, 2 * D + lanes.start : 2 * D + lanes.stop] = dv[i].astype(BF)
        return carry

    lax.fori_loop(1, 5, backward, 0)
    store(dqkv, dqkv_hbm)
    for j in range(3):
        put(j, dot_tn(normed[inner, :], dqkv[:, D * j : D * j + D]))
    for copy in stores:
        copy.wait()


def finish_kernel(x_ref, gn_ref, dqkv_ref, wqkv_ref, ng_ref, px_ref, pxt_ref, dwork_ref, d_normed):
    for j in range(2):
        columns = slice(256 * j, 256 * j + 256)
        d_normed[:, columns] = dot_nt(dqkv_ref[...], wqkv_ref[columns, :]).astype(BF)

    def finish(k, carry):
        span = pl.ds(pl.multiple_of((k + 1) * WR, 16), WR)
        gspan = pl.ds(pl.multiple_of(k * WRP, 16), WRP)
        hat, scale = norm_parts(dot(px_ref[...], x_ref[span, :]))
        back = norm_back(hat, scale, d_normed[gspan, :].astype(F32) * ng_ref[...])
        d_work = (gn_ref[gspan, :].astype(F32) + back).astype(BF)
        dwork_ref[pl.ds(pl.multiple_of(k * WR, 16), WR), :] = dot(pxt_ref[...], d_work).astype(BF)
        return carry

    lax.fori_loop(0, 4, finish, 0, unroll=2)


VMEM = pl.BlockSpec(memory_space=pltpu.VMEM)
HBM = pl.BlockSpec(memory_space=pl.ANY)


def compute(tiles, lats, x, c, norm_gain, w_qkv, w_proj, merge_gain, w_merge, w_expand, expand_gain):
    bf = lambda *shape: pltpu.VMEM(shape, BF)
    share = (tiles, D // (2 * tiles), 4 * D)
    return pl.pallas_call(
        functools.partial(kernel, lats),
        out_shape=tuple(
            jax.ShapeDtypeStruct(shape, BF) for shape in (share, share, (4 * WRP, D), (4 * WRP, 3 * D))
        ),
        in_specs=[VMEM] * 11 + [HBM] * 4,
        out_specs=(HBM,) * 4,
        scratch_shapes=[
            bf(D, 3 * D), bf(D, D), bf(4 * D, 2 * D), bf(2 * D, 4 * D),
            bf(NWR * WRP, D), bf(NWR * WRP, D), bf(NWR * WRP, 3 * D), pltpu.VMEM((NWR, HEADS, WIN, 256), F32),
            bf(NWR * WRP, D), bf(NWR * WRP, D),
            bf(4, QROWS, D), bf(4, QROWS, D), bf(QROWS, 4 * D), bf(QROWS, 4 * D), bf(4, QROWS, D),
            bf(4 * WRP, D), bf(4 * WRP, D), bf(4 * WRP, 3 * D), bf(*share), bf(*share),
            pltpu.SemaphoreType.DMA((14,)),
        ],
        compiler_params=pltpu.CompilerParams(vmem_limit_bytes=58 * 1024 * 1024),
        cost_estimate=pl.CostEstimate(flops=7_000_000_000, bytes_accessed=18_000_000, transcendentals=0),
        name="block",
    )(
        x, c, norm_gain[None], merge_gain[None], expand_gain[None],
        jnp.asarray(to_windows()), jnp.asarray(to_windows().T), jnp.asarray(fine_offsets()),
        jnp.asarray(cot_offsets(4, 48)), jnp.asarray(cot_offsets(1, 16)), jnp.asarray(from_offsets()),
        w_qkv, w_proj, w_merge, w_expand,
    )


def finish_tokens(x, gn, dqkv, w_qkv, norm_gain):
    return pl.pallas_call(
        finish_kernel,
        out_shape=jax.ShapeDtypeStruct((4 * WR, D), BF),
        in_specs=[VMEM] * 7,
        out_specs=VMEM,
        scratch_shapes=[pltpu.VMEM((4 * WRP, D), BF)],
        compiler_params=pltpu.CompilerParams(vmem_limit_bytes=40 * 1024 * 1024),
        cost_estimate=pl.CostEstimate(flops=1_200_000_000, bytes_accessed=6_000_000, transcendentals=0),
        name="block_tokens",
    )(x, gn, dqkv, w_qkv, norm_gain[None], jnp.asarray(to_windows()), jnp.asarray(to_windows().T))


def body(tokens, cotangent, norm_gain, w_qkv, w_proj, merge_gain, w_merge, w_expand, expand_gain):
    lats, tiles, cores = lax.axis_size("lat"), lax.axis_size("tile"), lax.axis_size("core")
    lons = tiles * cores
    names = ("lat", "tile", "core")

    def moved(value, dlat, dlon):
        pairs = []
        for a in range(lats):
            for b in range(lons):
                pairs.append((a * lons + b, ((a + dlat) % lats) * lons + (b + dlon) % lons))
        return lax.ppermute(value, names, pairs)

    edge = moved(jnp.concatenate([tokens[:, :SLON], cotangent[:, :SLON]], axis=0), 0, -1)
    work = jnp.concatenate([tokens[:, SLON:], edge[:ROWS]], axis=1)
    cwork = jnp.concatenate([cotangent[:, SLON:], edge[ROWS:]], axis=1)
    below = moved(jnp.concatenate([work[:9], cwork[:4]], axis=0), -1, 0)
    above = moved(work[ROWS - 3 :], 1, 0)
    x = jnp.concatenate([above, work, below[:9]], axis=0).reshape(XROWS * COLS, D)
    c = jnp.concatenate([cwork, below[9:]], axis=0).reshape(CROWS * COLS, D)

    mine, other, gn, dqkv = compute(
        tiles, lats, x, c, norm_gain, w_qkv, w_proj, merge_gain, w_merge, w_expand, expand_gain
    )

    theirs = lax.ppermute(other, "core", [(i, cores - 1 - i) for i in range(cores)])
    pair, dqkv = lax.optimization_barrier((mine + theirs, dqkv))
    spread = lax.all_to_all(pair, "tile", 0, 0, tiled=True)

    d_work = finish_tokens(x, gn, dqkv, w_qkv, norm_gain).reshape(ROWS, COLS, D)
    arrived = moved(d_work[ROWS - SLAT :], 1, 0)
    d_rows = jnp.concatenate([arrived, d_work[: ROWS - SLAT]], axis=0)
    arrived = moved(d_rows[:, COLS - SLON :], 0, 1)
    d_tokens = jnp.concatenate([arrived, d_rows[:, : COLS - SLON]], axis=1)
    spread, d_tokens = lax.optimization_barrier((spread, d_tokens))

    share = jnp.sum(spread.astype(F32), axis=0).astype(BF)
    copies = jnp.broadcast_to(share[None], (lats,) + share.shape)
    gathered = lax.all_to_all(copies, "lat", 0, 0, tiled=True)
    grad_qkv = jnp.sum(gathered[:, :, : 3 * D].astype(F32), axis=0)
    grad_proj = jnp.sum(gathered[:, :, 3 * D :].astype(F32), axis=0)
    return (d_tokens, grad_qkv, grad_proj)


def solution(mesh):
    lats, lons = mesh.shape["lat"], mesh.shape["lon"]
    fine_mesh = Mesh(mesh.devices.reshape(lats, lons // 2, 2), ("lat", "tile", "core"))
    lon = ("tile", "core")
    in_specs = (P("lat", lon, None), P("lat", lon, None), P(), P(), P(), P(), P(), P(), P())
    out_specs = (P("lat", lon, None), P(lon, None), P(lon, None))
    return jax.shard_map(body, mesh=fine_mesh, in_specs=in_specs, out_specs=out_specs, check_vma=False)
```

```python
import functools

import jax
import jax.numpy as jnp
import numpy as np
from jax import lax
from jax.experimental import pallas as pl
from jax.experimental.pallas import tpu as pltpu
from jax.sharding import Mesh, PartitionSpec as P

HEADS = 8
HEAD = 64
WLAT = 6
WLON = 12
SLAT = 3
SLON = 6
D = 512
ROWS = 24
COLS = 24
WR = WLAT * COLS
WIN = WLAT * WLON
WP = 80
WRP = 2 * WP
NWR = 6
EARLY = 3
CROWS = 28
PAIRS = 13
QROWS = 160

EPSILON = 1e-05
GRANT = 63 * 1024 * 1024
MASKED = -1000000000.0
OUTSIDE = -3.0e38
BF = jnp.bfloat16
F32 = jnp.float32


def window_row(i, col):
    return (col // WLON) * WP + i * WLON + col % WLON


def to_windows():
    out = np.zeros((WRP, WR), np.float32)
    for t in range(WR):
        out[window_row(t // COLS, t % COLS), t] = 1
    return out.astype(jnp.bfloat16)


def cot_offsets(pairs, padded):
    out = np.zeros((4 * padded, pairs * 2 * COLS), np.float32)
    for a in range(pairs):
        for rp in range(2):
            for col in range(COLS):
                q = (col % 2) * 2 + rp
                out[q * padded + a * 12 + col // 2, (2 * a + rp) * COLS + col] = 1
    return out.astype(jnp.bfloat16)


FINE_PARTS = ((0, 0), (0, 1), (0, 2), (1, 2), (1, 3), (2, 3), (2, 4), (3, 4), (3, 5))


def fine_offsets():
    out = np.zeros((len(FINE_PARTS), 4 * 48, WRP), np.float32)
    for n, (g, k) in enumerate(FINE_PARTS):
        padded = 48 if g < 3 else 16
        for a in range(4 * g, min(4 * g + 4, PAIRS)):
            for rp in range(2):
                f = 5 + 2 * a + rp
                if f // WLAT != k:
                    continue
                for col in range(COLS):
                    q = (col % 2) * 2 + rp
                    out[n, q * padded + (a - 4 * g) * 12 + col // 2, window_row(f % WLAT, col)] = 1
    return out.astype(jnp.bfloat16)


def from_offsets():
    out = np.zeros((4, WRP, 256), np.float32)
    for k in range(1, 5):
        for t in range(WR):
            f = WLAT * k + t // COLS
            col = t % COLS
            a, rp = divmod(f - 5, 2)
            q = (col % 2) * 2 + rp
            out[k - 1, window_row(t // COLS, col), q * 64 + 12 * a + col // 2 - 32 * (k - 1)] = 1
    return out.astype(jnp.bfloat16)


def dot(a, b):
    return jnp.dot(a, b, preferred_element_type=F32)


def dot_nt(a, b):
    return lax.dot_general(a, b, (((1,), (1,)), ((), ())), preferred_element_type=F32)


def dot_tn(a, b):
    return lax.dot_general(a, b, (((0,), (0,)), ((), ())), preferred_element_type=F32)


def norm_parts(values):
    average = jnp.mean(values, axis=-1, keepdims=True)
    centred = values - average
    spread = jnp.mean(centred * centred, axis=-1, keepdims=True)
    scale = lax.rsqrt(spread + EPSILON)
    return centred * scale, scale


def norm_back(hat, scale, dy):
    mean_dy = jnp.mean(dy, axis=-1, keepdims=True)
    mean_dyh = jnp.mean(dy * hat, axis=-1, keepdims=True)
    return scale * (dy - mean_dy - hat * mean_dyh)


def stacked(two, low):
    gap = jnp.zeros((128 - WP, 2 * HEAD), BF)
    return jnp.concatenate([two * low, gap, two * (1 - low), gap], axis=0)


def over_queries(keys_by_queries, rows, first_lane):
    both = [dot_tn(keys_by_queries[:, 128 * i : 128 * i + WP], rows) for i in range(2)]
    return jnp.where(first_lane, both[0], both[1])


def padded_keys(values):
    return jnp.concatenate([values, jnp.zeros((WP - WIN, 256), F32)], axis=0).astype(BF)


UNITS = [(w, hp) for w in range(2) for hp in range(HEADS // 2)]


def lane_halves():
    first_lane = lax.broadcasted_iota(jnp.int32, (1, 2 * HEAD), 1) < HEAD
    return first_lane, first_lane.astype(F32).astype(BF)


def rows_of(start, size):
    return pl.ds(pl.multiple_of(start, 16), size)


def heads(qkv, start, w, hp, low):
    win = rows_of(start + WP * w, WP)
    q2 = qkv[win, 128 * hp : 128 * hp + 128]
    k2 = qkv[win, D + 128 * hp : D + 128 * hp + 128]
    v2 = qkv[win, 2 * D + 128 * hp : 2 * D + 128 * hp + 128]
    return stacked(q2 * 0.125, low), k2, v2, win


def attention(first, mask, x_ref, px, gain, wqkv, wproj, xw, normed, qkv, probs, attn, fine):
    first_lane, low = lane_halves()
    base = WRP * first
    span = slice(base, base + 3 * WRP)
    for k in range(3):
        rows = slice(base + WRP * k, base + WRP * k + WRP)
        x = dot(px[...], x_ref[WR * k : WR * k + WR, :])
        xw[WRP * k : WRP * k + WRP, :] = x.astype(BF)
        hat, _ = norm_parts(x)
        normed[rows, :] = (hat * gain[...]).astype(BF)
    for j in range(6):
        columns = slice(256 * j, 256 * j + 256)
        qkv[span, columns] = dot(normed[span, :], wqkv[:, columns]).astype(BF)

    def window_row(k, carry):
        masked = None if mask is None else mask(k)
        parts = [heads(qkv, k * WRP, w, hp, low) for w, hp in UNITS]
        s = [dot_nt(k2, qs)[:WIN] for qs, k2, _, _ in parts]
        if masked is not None:
            s = [jnp.where(masked, MASKED, v) for v in s]
        top = [jnp.max(v, axis=0, keepdims=True) for v in s]
        e = [jnp.exp(v - t) for v, t in zip(s, top)]
        total = [jnp.sum(v, axis=0, keepdims=True) for v in e]
        p = [v * (1.0 / t) for v, t in zip(e, total)]
        for (w, hp), v in zip(UNITS, p):
            probs[k, 4 * w + hp] = v
        o = [over_queries(padded_keys(v), v2, first_lane) for v, (_, _, v2, _) in zip(p, parts)]
        for (w, hp), v, (_, _, _, win) in zip(UNITS, o, parts):
            attn[win, 128 * hp : 128 * hp + 128] = v.astype(BF)
        return carry

    lax.fori_loop(first, first + 3, window_row, 0)
    for j in range(2):
        columns = slice(256 * j, 256 * j + 256)
        fine[span, columns] = (
            xw[:, columns].astype(F32) + dot(attn[span, :], wproj[:, columns])
        ).astype(BF)


def early_kernel(x_ref, px_ref, ng_ref, wqkv, wproj, normed, qkv, probs, attn, fine, xw):
    attention(0, None, x_ref, px_ref, ng_ref, wqkv, wproj, xw, normed, qkv, probs, attn, fine)


def kernel(
    lat_size, x_ref, c_ref, ng_ref, mg_ref, eg_ref, px_ref, pf_ref, pc_ref, pc3_ref, pi_ref,
    wqkv_hbm, wproj_hbm, wm_hbm, we_hbm, normed_hbm, qkv_hbm, probs_hbm, attn_hbm, fine_hbm,
    mine_hbm, other_hbm, gn_hbm, dqkv_hbm,
    wqkv, wproj, wm, we, xw, normed, qkv, probs, attn, fine, fq, cq, mg, dw, gq, gn, d_attn, dqkv, mine, other, sems,
):
    lat = lax.axis_index("lat")
    core = lax.axis_index("core")
    done = slice(0, EARLY * WRP)
    sources = (
        (wqkv_hbm, wqkv), (wproj_hbm, wproj), (fine_hbm, fine.at[done]), (wm_hbm, wm), (we_hbm, we),
        (probs_hbm, probs.at[0:EARLY]), (qkv_hbm, qkv.at[done]),
        (attn_hbm, attn.at[done]), (normed_hbm, normed.at[done]),
    )
    loads = [pltpu.make_async_copy(src, dst, sems.at[i]) for i, (src, dst) in enumerate(sources)]
    for load in loads:
        load.start()

    key = lax.broadcasted_iota(jnp.int32, (WIN, 256), 0)
    query = lax.broadcasted_iota(jnp.int32, (WIN, 256), 1) % 128
    apart = (key >= WIN // 2) != (query >= WIN // 2)
    first_lane, low = lane_halves()

    def masked_at(k):
        edge = ((k == NWR - 1) & (lat == 0)) | ((k == EARLY) & (lat == lat_size - 1))
        return apart & edge

    loads[0].wait()
    loads[1].wait()
    attention(EARLY, masked_at, x_ref, px_ref, ng_ref, wqkv, wproj, xw, normed, qkv, probs, attn, fine)
    loads[2].wait()

    for g in range(4):
        n = 48 if g < 3 else 16
        f = sum(
            dot(pf_ref[m, : 4 * n, :], fine[WRP * k : WRP * k + WRP, :])
            for m, (gg, k) in enumerate((g_, (k_ - 1) % NWR) for g_, k_ in FINE_PARTS)
            if gg == g
        ).astype(BF)
        if g < 3:
            c = dot(pc_ref[...], c_ref[48 + 192 * g : 48 + 192 * g + 192, :]).astype(BF)
        else:
            c = dot(pc3_ref[...], c_ref[624:672, :]).astype(BF)
        for q in range(4):
            fq[q, 48 * g : 48 * g + n, :] = f[n * q : n * q + n]
            cq[q, 48 * g : 48 * g + n, :] = c[n * q : n * q + n]

    def merge_stats(rows):
        total = jnp.zeros((32, 1), F32)
        for q in range(4):
            total = total + jnp.sum(fq[q, rows, :].astype(F32), axis=-1, keepdims=True)
        average = total * (1.0 / (4 * D))
        total = jnp.zeros((32, 1), F32)
        for q in range(4):
            centred = fq[q, rows, :].astype(F32) - average
            total = total + jnp.sum(centred * centred, axis=-1, keepdims=True)
        return average, lax.rsqrt(total * (1.0 / (4 * D)) + EPSILON)

    for r in range(QROWS // 32):
        rows = slice(32 * r, 32 * r + 32)
        average, scale = merge_stats(rows)
        for q in range(4):
            hat = (fq[q, rows, :].astype(F32) - average) * scale
            mg[rows, D * q : D * q + D] = (hat * mg_ref[:, D * q : D * q + D]).astype(BF)

    loads[3].wait()
    loads[4].wait()
    coarse = dot(mg[...], wm[...]).astype(BF)
    for q in range(4):
        qq = (0, 2, 1, 3)[q]
        wide = dot(coarse, we[:, D * qq : D * qq + D])
        hat, scale = norm_parts(wide)
        dy = cq[q].astype(F32) * eg_ref[...]
        dw[:, D * qq : D * qq + D] = norm_back(hat, scale, dy).astype(BF)
    d_coarse = dot_nt(dw[...], we[...]).astype(BF)
    mg[...] = dot_nt(d_coarse, wm[...]).astype(BF)

    for r in range(QROWS // 32):
        rows = slice(32 * r, 32 * r + 32)
        average, scale = merge_stats(rows)
        sum_dy = jnp.zeros((32, 1), F32)
        sum_dyh = jnp.zeros((32, 1), F32)
        for q in range(4):
            hat = (fq[q, rows, :].astype(F32) - average) * scale
            dy = mg[rows, D * q : D * q + D].astype(F32) * mg_ref[:, D * q : D * q + D]
            sum_dy = sum_dy + jnp.sum(dy, axis=-1, keepdims=True)
            sum_dyh = sum_dyh + jnp.sum(dy * hat, axis=-1, keepdims=True)
        mean_dy = sum_dy * (1.0 / (4 * D))
        mean_dyh = sum_dyh * (1.0 / (4 * D))
        for q in range(4):
            hat = (fq[q, rows, :].astype(F32) - average) * scale
            dy = mg[rows, D * q : D * q + D].astype(F32) * mg_ref[:, D * q : D * q + D]
            back = (scale * (dy - mean_dy - hat * mean_dyh)).astype(BF)
            gq[q, rows, :] = (cq[q, rows, :].astype(F32) + back.astype(F32)).astype(BF)

    for k in range(4):
        parts = jnp.concatenate([gq[q, 32 * k : 32 * k + 64, :] for q in range(4)], axis=0)
        gn[WRP * k : WRP * k + WRP, :] = dot(pi_ref[k], parts).astype(BF)

    stores = []

    def store(src, dst):
        copy = pltpu.make_async_copy(src, dst, sems.at[9 + len(stores)])
        copy.start()
        stores.append(copy)

    def put(j, block):
        columns = slice(D * j, D * j + D)
        pairs = block.astype(BF).reshape(mine.shape[0], 2, mine.shape[1], D)
        even, odd = pairs[:, 0], pairs[:, 1]
        mine[:, :, columns] = jnp.where(core == 0, even, odd)
        other[:, :, columns] = jnp.where(core == 0, odd, even)
        store(other.at[:, :, columns], other_hbm.at[:, :, columns])
        store(mine.at[:, :, columns], mine_hbm.at[:, :, columns])

    for load in loads[5:]:
        load.wait()
    inner = slice(0, 4 * WRP)
    store(gn, gn_hbm)
    put(3, dot_tn(attn[inner, :], gn[...]))

    for j in range(2):
        columns = slice(256 * j, 256 * j + 256)
        d_attn[:, columns] = dot_nt(gn[...], wproj[columns, :]).astype(BF)

    def backward(k, carry):
        start = pl.multiple_of(k * WRP, 16)
        masked = masked_at(k)
        parts = [heads(qkv, start, w, hp, low) for w, hp in UNITS]
        do = [
            stacked(d_attn[win, 128 * hp : 128 * hp + 128], low)
            for (_, hp), (_, _, _, win) in zip(UNITS, parts)
        ]
        dp = [dot_nt(v2, d)[:WIN] for d, (_, _, v2, _) in zip(do, parts)]
        p = [probs[k, 4 * w + hp] for w, hp in UNITS]
        dv = [dot(padded_keys(v), d) for v, d in zip(p, do)]
        dp = [v.astype(BF).astype(F32) for v in dp]
        inner = [jnp.sum(a * b, axis=0, keepdims=True) for a, b in zip(dp, p)]
        ds = [b * (a - c) for a, b, c in zip(dp, p, inner)]
        ds = [padded_keys(jnp.where(masked, 0.0, v)) for v in ds]
        dk = [dot(v, qs) for v, (qs, _, _, _) in zip(ds, parts)]
        dq = [over_queries(v, k2, first_lane) * 0.125 for v, (_, k2, _, _) in zip(ds, parts)]
        for i, ((_, hp), (_, _, _, win)) in enumerate(zip(UNITS, parts)):
            lanes = slice(128 * hp, 128 * hp + 128)
            dqkv[win, lanes] = dq[i].astype(BF)
            dqkv[win, D + lanes.start : D + lanes.stop] = dk[i].astype(BF)
            dqkv[win, 2 * D + lanes.start : 2 * D + lanes.stop] = dv[i].astype(BF)
        return carry

    lax.fori_loop(0, 4, backward, 0)
    store(dqkv, dqkv_hbm)
    for j in range(3):
        put(j, dot_tn(normed[inner, :], dqkv[:, D * j : D * j + D]))
    for copy in stores:
        copy.wait()


def finish_kernel(early_ref, late_ref, gn_ref, dqkv_ref, wqkv_ref, ng_ref, px_ref, pxt_ref, dwork_ref, d_normed):
    for j in range(2):
        columns = slice(256 * j, 256 * j + 256)
        d_normed[:, columns] = dot_nt(dqkv_ref[...], wqkv_ref[columns, :]).astype(BF)

    for k in range(4):
        rows = slice(WRP * k, WRP * k + WRP)
        x = early_ref[WR * k : WR * k + WR, :] if k < EARLY else late_ref[:WR, :]
        hat, scale = norm_parts(dot(px_ref[...], x))
        back = norm_back(hat, scale, d_normed[rows, :].astype(F32) * ng_ref[...])
        d_work = (gn_ref[rows, :].astype(F32) + back).astype(BF)
        dwork_ref[WR * k : WR * k + WR, :] = dot(pxt_ref[...], d_work).astype(BF)


VMEM = pl.BlockSpec(memory_space=pltpu.VMEM)
HBM = pl.BlockSpec(memory_space=pl.ANY)


def start_early(x, norm_gain, w_qkv, w_proj):
    rows = EARLY * WRP
    shapes = [((rows, D), BF), ((rows, 3 * D), BF), ((EARLY, HEADS, WIN, 256), F32), ((rows, D), BF), ((rows, D), BF)]
    return pl.pallas_call(
        early_kernel,
        out_shape=tuple(jax.ShapeDtypeStruct(*one) for one in shapes),
        in_specs=[VMEM] * 5,
        out_specs=(VMEM,) * 5,
        scratch_shapes=[pltpu.VMEM((rows, D), BF)],
        compiler_params=pltpu.CompilerParams(vmem_limit_bytes=GRANT),
        cost_estimate=pl.CostEstimate(flops=1_400_000_000, bytes_accessed=8_000_000, transcendentals=0),
        name="block_early",
    )(x, jnp.asarray(to_windows()), norm_gain[None], w_qkv, w_proj)


def compute(tiles, lats, early, x, c, norm_gain, w_qkv, w_proj, merge_gain, w_merge, w_expand, expand_gain):
    bf = lambda *shape: pltpu.VMEM(shape, BF)
    share = (tiles, D // (2 * tiles), 4 * D)
    return pl.pallas_call(
        functools.partial(kernel, lats),
        out_shape=tuple(
            jax.ShapeDtypeStruct(shape, BF) for shape in (share, share, (4 * WRP, D), (4 * WRP, 3 * D))
        ),
        in_specs=[VMEM] * 10 + [HBM] * 9,
        out_specs=(HBM,) * 4,
        scratch_shapes=[
            bf(D, 3 * D), bf(D, D), bf(4 * D, 2 * D), bf(2 * D, 4 * D),
            bf((NWR - EARLY) * WRP, D), bf(NWR * WRP, D), bf(NWR * WRP, 3 * D), pltpu.VMEM((NWR, HEADS, WIN, 256), F32),
            bf(NWR * WRP, D), bf(NWR * WRP, D),
            bf(4, QROWS, D), bf(4, QROWS, D), bf(QROWS, 4 * D), bf(QROWS, 4 * D), bf(4, QROWS, D),
            bf(4 * WRP, D), bf(4 * WRP, D), bf(4 * WRP, 3 * D), bf(*share), bf(*share),
            pltpu.SemaphoreType.DMA((19,)),
        ],
        compiler_params=pltpu.CompilerParams(vmem_limit_bytes=GRANT),
        cost_estimate=pl.CostEstimate(flops=7_000_000_000, bytes_accessed=18_000_000, transcendentals=0),
        name="block",
    )(
        x, c, norm_gain[None], merge_gain[None], expand_gain[None],
        jnp.asarray(to_windows()), jnp.asarray(fine_offsets()),
        jnp.asarray(cot_offsets(4, 48)), jnp.asarray(cot_offsets(1, 16)), jnp.asarray(from_offsets()),
        w_qkv, w_proj, w_merge, w_expand, *early,
    )


def finish_tokens(x_early, x, gn, dqkv, w_qkv, norm_gain):
    return pl.pallas_call(
        finish_kernel,
        out_shape=jax.ShapeDtypeStruct((4 * WR, D), BF),
        in_specs=[VMEM] * 8,
        out_specs=VMEM,
        scratch_shapes=[pltpu.VMEM((4 * WRP, D), BF)],
        compiler_params=pltpu.CompilerParams(vmem_limit_bytes=GRANT),
        cost_estimate=pl.CostEstimate(flops=1_200_000_000, bytes_accessed=6_000_000, transcendentals=0),
        name="block_tokens",
    )(x_early, x, gn, dqkv, w_qkv, norm_gain[None], jnp.asarray(to_windows()), jnp.asarray(to_windows().T))


def add_kernel(a_ref, b_ref, out_ref):
    out_ref[...] = a_ref[...] + b_ref[...]


def pair_sum(a, b):
    steps = 4 if a.shape[0] % 4 == 0 else 1
    block = pl.BlockSpec((a.shape[0] // steps,) + a.shape[1:], lambda i: (i, 0, 0))
    return pl.pallas_call(
        add_kernel,
        grid=(steps,),
        out_shape=jax.ShapeDtypeStruct(a.shape, BF),
        in_specs=[block, block],
        out_specs=block,
        compiler_params=pltpu.CompilerParams(vmem_limit_bytes=GRANT),
        name="pair_sum",
    )(a, b)


def body(tokens, cotangent, norm_gain, w_qkv, w_proj, merge_gain, w_merge, w_expand, expand_gain):
    lats, tiles, cores = lax.axis_size("lat"), lax.axis_size("tile"), lax.axis_size("core")
    lons = tiles * cores
    names = ("lat", "tile", "core")

    def moved(value, dlat, dlon):
        pairs = []
        for a in range(lats):
            for b in range(lons):
                pairs.append((a * lons + b, ((a + dlat) % lats) * lons + (b + dlon) % lons))
        return lax.ppermute(value, names, pairs)

    beside = moved(jnp.concatenate([tokens[:, :SLON], cotangent[:, :SLON]], axis=0), 0, -1)
    below = moved(jnp.concatenate([tokens[:9], cotangent[:4]], axis=0), -1, 0)
    above = moved(tokens[ROWS - 3 :], 1, 0)
    low_corner = moved(jnp.concatenate([tokens[:9, :SLON], cotangent[:4, :SLON]], axis=0), -1, -1)
    high_corner = moved(tokens[ROWS - 3 :, :SLON], 1, -1)

    first, last = SLAT, ROWS - SLAT
    x_early = jnp.concatenate([tokens[first:last, SLON:], beside[first:last]], axis=1)
    x_early = x_early.reshape(EARLY * WR, D)
    early = start_early(x_early, norm_gain, w_qkv, w_proj)
    early, below, above, low_corner, high_corner = lax.optimization_barrier(
        (early, below, above, low_corner, high_corner)
    )

    left = jnp.concatenate([tokens[last:, SLON:], below[:9, SLON:], above[:, SLON:], tokens[:first, SLON:]], axis=0)
    right = jnp.concatenate([beside[last:ROWS], low_corner[:9], high_corner, beside[:first]], axis=0)
    x = jnp.concatenate([left, right], axis=1).reshape((NWR - EARLY) * WR, D)
    left = jnp.concatenate([cotangent[:, SLON:], below[9:, SLON:]], axis=0)
    right = jnp.concatenate([beside[ROWS:], low_corner[9:]], axis=0)
    c = jnp.concatenate([left, right], axis=1).reshape(CROWS * COLS, D)

    mine, other, gn, dqkv = compute(
        tiles, lats, early, x, c, norm_gain, w_qkv, w_proj, merge_gain, w_merge, w_expand, expand_gain
    )

    theirs = lax.ppermute(other, "core", [(i, cores - 1 - i) for i in range(cores)])
    pair, dqkv = lax.optimization_barrier((pair_sum(mine, theirs), dqkv))
    spread = lax.all_to_all(pair, "tile", 0, 0, tiled=True)

    d_work = finish_tokens(x_early, x, gn, dqkv, w_qkv, norm_gain).reshape(ROWS, COLS, D)
    last_row, last_col = ROWS - SLAT, COLS - SLON
    rows = moved(d_work[last_row:, :last_col], 1, 0)
    corner = moved(d_work[last_row:, last_col:], 1, 1)
    edge = d_work[:last_row, last_col:]
    spread, rows, corner, edge = lax.optimization_barrier((spread, rows, corner, edge))
    columns = moved(edge, 0, 1)
    top = jnp.concatenate([corner, rows], axis=1)
    rest = jnp.concatenate([columns, d_work[:last_row, :last_col]], axis=1)
    d_tokens = jnp.concatenate([top, rest], axis=0)

    share = jnp.sum(spread.astype(F32), axis=0).astype(BF)
    copies = jnp.broadcast_to(share[None], (lats,) + share.shape)
    gathered = lax.all_to_all(copies, "lat", 0, 0, tiled=True)
    grad_qkv = jnp.sum(gathered[:, :, : 3 * D].astype(F32), axis=0)
    grad_proj = jnp.sum(gathered[:, :, 3 * D :].astype(F32), axis=0)
    return (d_tokens, grad_qkv, grad_proj)


def solution(mesh):
    lats, lons = mesh.shape["lat"], mesh.shape["lon"]
    fine_mesh = Mesh(mesh.devices.reshape(lats, lons // 2, 2), ("lat", "tile", "core"))
    lon = ("tile", "core")
    in_specs = (P("lat", lon, None), P("lat", lon, None), P(), P(), P(), P(), P(), P(), P())
    out_specs = (P("lat", lon, None), P(lon, None), P(lon, None))
    return jax.shard_map(body, mesh=fine_mesh, in_specs=in_specs, out_specs=out_specs, check_vma=False)
```

```python
import functools

import jax
import jax.numpy as jnp
import numpy as np
from jax import lax
from jax.experimental import pallas as pl
from jax.experimental.pallas import tpu as pltpu
from jax.sharding import Mesh, PartitionSpec as P

HEADS = 8
HEAD = 64
WLAT = 6
WLON = 12
SLAT = 3
SLON = 6
D = 512
ROWS = 24
COLS = 24
WR = WLAT * COLS
WIN = WLAT * WLON
WP = 80
WRP = 2 * WP
NWR = 6
EARLY = 3
CROWS = 28
PAIRS = 13
QROWS = 160

EPSILON = 1e-05
GRANT = 63 * 1024 * 1024
SMALL_GRANT = 24 * 1024 * 1024
MASKED = -1000000000.0
OUTSIDE = -3.0e38
BF = jnp.bfloat16
F32 = jnp.float32


def window_row(i, col):
    return (col // WLON) * WP + i * WLON + col % WLON


def to_windows():
    out = np.zeros((WRP, WR), np.float32)
    for t in range(WR):
        out[window_row(t // COLS, t % COLS), t] = 1
    return out.astype(jnp.bfloat16)


def cot_offsets(pairs, padded):
    out = np.zeros((4 * padded, pairs * 2 * COLS), np.float32)
    for a in range(pairs):
        for rp in range(2):
            for col in range(COLS):
                q = (col % 2) * 2 + rp
                out[q * padded + a * 12 + col // 2, (2 * a + rp) * COLS + col] = 1
    return out.astype(jnp.bfloat16)


FINE_PARTS = ((0, 0), (0, 1), (0, 2), (1, 2), (1, 3), (2, 3), (2, 4), (3, 4), (3, 5))


def fine_offsets():
    out = np.zeros((len(FINE_PARTS), 4 * 48, WRP), np.float32)
    for n, (g, k) in enumerate(FINE_PARTS):
        padded = 48 if g < 3 else 16
        for a in range(4 * g, min(4 * g + 4, PAIRS)):
            for rp in range(2):
                f = 5 + 2 * a + rp
                if f // WLAT != k:
                    continue
                for col in range(COLS):
                    q = (col % 2) * 2 + rp
                    out[n, q * padded + (a - 4 * g) * 12 + col // 2, window_row(f % WLAT, col)] = 1
    return out.astype(jnp.bfloat16)


def from_offsets():
    out = np.zeros((4, WRP, 256), np.float32)
    for k in range(1, 5):
        for t in range(WR):
            f = WLAT * k + t // COLS
            col = t % COLS
            a, rp = divmod(f - 5, 2)
            q = (col % 2) * 2 + rp
            out[k - 1, window_row(t // COLS, col), q * 64 + 12 * a + col // 2 - 32 * (k - 1)] = 1
    return out.astype(jnp.bfloat16)


def dot(a, b):
    return jnp.dot(a, b, preferred_element_type=F32)


def dot_nt(a, b):
    return lax.dot_general(a, b, (((1,), (1,)), ((), ())), preferred_element_type=F32)


def dot_tn(a, b):
    return lax.dot_general(a, b, (((0,), (0,)), ((), ())), preferred_element_type=F32)


def norm_parts(values):
    average = jnp.mean(values, axis=-1, keepdims=True)
    centred = values - average
    spread = jnp.mean(centred * centred, axis=-1, keepdims=True)
    scale = lax.rsqrt(spread + EPSILON)
    return centred * scale, scale


def norm_back(hat, scale, dy):
    mean_dy = jnp.mean(dy, axis=-1, keepdims=True)
    mean_dyh = jnp.mean(dy * hat, axis=-1, keepdims=True)
    return scale * (dy - mean_dy - hat * mean_dyh)


def stacked(two, low):
    gap = jnp.zeros((128 - WP, 2 * HEAD), BF)
    return jnp.concatenate([two * low, gap, two * (1 - low), gap], axis=0)


def over_queries(keys_by_queries, rows, first_lane):
    both = [dot_tn(keys_by_queries[:, 128 * i : 128 * i + WP], rows) for i in range(2)]
    return jnp.where(first_lane, both[0], both[1])


def padded_keys(values):
    return jnp.concatenate([values, jnp.zeros((WP - WIN, 256), F32)], axis=0).astype(BF)


UNITS = [(w, hp) for w in range(2) for hp in range(HEADS // 2)]


def lane_halves():
    first_lane = lax.broadcasted_iota(jnp.int32, (1, 2 * HEAD), 1) < HEAD
    return first_lane, first_lane.astype(F32).astype(BF)


def rows_of(start, size):
    return pl.ds(pl.multiple_of(start, 16), size)


def heads(qkv, start, w, hp, low):
    win = rows_of(start + WP * w, WP)
    q2 = qkv[win, 128 * hp : 128 * hp + 128]
    k2 = qkv[win, D + 128 * hp : D + 128 * hp + 128]
    v2 = qkv[win, 2 * D + 128 * hp : 2 * D + 128 * hp + 128]
    return stacked(q2 * 0.125, low), k2, v2, win


def attention(first, mask, x_ref, px, gain, wqkv, wproj, xw, normed, qkv, probs, attn, fine):
    first_lane, low = lane_halves()
    base = WRP * first
    span = slice(base, base + 3 * WRP)
    for k in range(3):
        rows = slice(base + WRP * k, base + WRP * k + WRP)
        x = dot(px[...], x_ref[WR * k : WR * k + WR, :])
        xw[WRP * k : WRP * k + WRP, :] = x.astype(BF)
        hat, _ = norm_parts(x)
        normed[rows, :] = (hat * gain[...]).astype(BF)
    for j in range(6):
        columns = slice(256 * j, 256 * j + 256)
        qkv[span, columns] = dot(normed[span, :], wqkv[:, columns]).astype(BF)

    def window_row(k, carry):
        masked = None if mask is None else mask(k)
        parts = [heads(qkv, k * WRP, w, hp, low) for w, hp in UNITS]
        s = [dot_nt(k2, qs)[:WIN] for qs, k2, _, _ in parts]
        if masked is not None:
            s = [jnp.where(masked, MASKED, v) for v in s]
        top = [jnp.max(v, axis=0, keepdims=True) for v in s]
        e = [jnp.exp(v - t) for v, t in zip(s, top)]
        total = [jnp.sum(v, axis=0, keepdims=True) for v in e]
        p = [v * (1.0 / t) for v, t in zip(e, total)]
        for (w, hp), v in zip(UNITS, p):
            probs[k, 4 * w + hp] = v
        o = [over_queries(padded_keys(v), v2, first_lane) for v, (_, _, v2, _) in zip(p, parts)]
        for (w, hp), v, (_, _, _, win) in zip(UNITS, o, parts):
            attn[win, 128 * hp : 128 * hp + 128] = v.astype(BF)
        return carry

    lax.fori_loop(first, first + 3, window_row, 0)
    for j in range(2):
        columns = slice(256 * j, 256 * j + 256)
        fine[span, columns] = (
            xw[:, columns].astype(F32) + dot(attn[span, :], wproj[:, columns])
        ).astype(BF)


def early_kernel(x_ref, px_ref, ng_ref, wqkv, wproj, normed, qkv, probs, attn, fine, xw):
    attention(0, None, x_ref, px_ref, ng_ref, wqkv, wproj, xw, normed, qkv, probs, attn, fine)


def kernel(
    lat_size, x_ref, c_ref, ng_ref, mg_ref, eg_ref, px_ref, pf_ref, pc_ref, pc3_ref, pi_ref,
    wqkv_hbm, wproj_hbm, wm_hbm, we_hbm, normed_hbm, qkv_hbm, probs_hbm, attn_hbm, fine_hbm,
    mine_hbm, other_hbm, gn_hbm, dqkv_hbm,
    wqkv, wproj, wm, we, xw, normed, qkv, probs, attn, fine, fq, cq, mg, dw, gq, gn, d_attn, dqkv, mine, other, sems,
):
    lat = lax.axis_index("lat")
    core = lax.axis_index("core")
    done = slice(0, EARLY * WRP)
    sources = (
        (wqkv_hbm, wqkv), (wproj_hbm, wproj), (fine_hbm, fine.at[done]), (wm_hbm, wm), (we_hbm, we),
        (probs_hbm, probs.at[0:EARLY]), (qkv_hbm, qkv.at[done]),
        (attn_hbm, attn.at[done]), (normed_hbm, normed.at[done]),
    )
    loads = [pltpu.make_async_copy(src, dst, sems.at[i]) for i, (src, dst) in enumerate(sources)]
    for load in loads:
        load.start()

    key = lax.broadcasted_iota(jnp.int32, (WIN, 256), 0)
    query = lax.broadcasted_iota(jnp.int32, (WIN, 256), 1) % 128
    apart = (key >= WIN // 2) != (query >= WIN // 2)
    first_lane, low = lane_halves()

    def masked_at(k):
        edge = ((k == NWR - 1) & (lat == 0)) | ((k == EARLY) & (lat == lat_size - 1))
        return apart & edge

    loads[0].wait()
    loads[1].wait()
    attention(EARLY, masked_at, x_ref, px_ref, ng_ref, wqkv, wproj, xw, normed, qkv, probs, attn, fine)
    loads[2].wait()

    for g in range(4):
        n = 48 if g < 3 else 16
        f = sum(
            dot(pf_ref[m, : 4 * n, :], fine[WRP * k : WRP * k + WRP, :])
            for m, (gg, k) in enumerate((g_, (k_ - 1) % NWR) for g_, k_ in FINE_PARTS)
            if gg == g
        ).astype(BF)
        if g < 3:
            c = dot(pc_ref[...], c_ref[48 + 192 * g : 48 + 192 * g + 192, :]).astype(BF)
        else:
            c = dot(pc3_ref[...], c_ref[624:672, :]).astype(BF)
        for q in range(4):
            fq[q, 48 * g : 48 * g + n, :] = f[n * q : n * q + n]
            cq[q, 48 * g : 48 * g + n, :] = c[n * q : n * q + n]

    def merge_stats(rows):
        total = jnp.zeros((32, 1), F32)
        for q in range(4):
            total = total + jnp.sum(fq[q, rows, :].astype(F32), axis=-1, keepdims=True)
        average = total * (1.0 / (4 * D))
        total = jnp.zeros((32, 1), F32)
        for q in range(4):
            centred = fq[q, rows, :].astype(F32) - average
            total = total + jnp.sum(centred * centred, axis=-1, keepdims=True)
        return average, lax.rsqrt(total * (1.0 / (4 * D)) + EPSILON)

    for r in range(QROWS // 32):
        rows = slice(32 * r, 32 * r + 32)
        average, scale = merge_stats(rows)
        for q in range(4):
            hat = (fq[q, rows, :].astype(F32) - average) * scale
            mg[rows, D * q : D * q + D] = (hat * mg_ref[:, D * q : D * q + D]).astype(BF)

    loads[3].wait()
    loads[4].wait()
    coarse = dot(mg[...], wm[...]).astype(BF)
    for q in range(4):
        qq = (0, 2, 1, 3)[q]
        wide = dot(coarse, we[:, D * qq : D * qq + D])
        hat, scale = norm_parts(wide)
        dy = cq[q].astype(F32) * eg_ref[...]
        dw[:, D * qq : D * qq + D] = norm_back(hat, scale, dy).astype(BF)
    d_coarse = dot_nt(dw[...], we[...]).astype(BF)
    mg[...] = dot_nt(d_coarse, wm[...]).astype(BF)

    for r in range(QROWS // 32):
        rows = slice(32 * r, 32 * r + 32)
        average, scale = merge_stats(rows)
        sum_dy = jnp.zeros((32, 1), F32)
        sum_dyh = jnp.zeros((32, 1), F32)
        for q in range(4):
            hat = (fq[q, rows, :].astype(F32) - average) * scale
            dy = mg[rows, D * q : D * q + D].astype(F32) * mg_ref[:, D * q : D * q + D]
            sum_dy = sum_dy + jnp.sum(dy, axis=-1, keepdims=True)
            sum_dyh = sum_dyh + jnp.sum(dy * hat, axis=-1, keepdims=True)
        mean_dy = sum_dy * (1.0 / (4 * D))
        mean_dyh = sum_dyh * (1.0 / (4 * D))
        for q in range(4):
            hat = (fq[q, rows, :].astype(F32) - average) * scale
            dy = mg[rows, D * q : D * q + D].astype(F32) * mg_ref[:, D * q : D * q + D]
            back = (scale * (dy - mean_dy - hat * mean_dyh)).astype(BF)
            gq[q, rows, :] = (cq[q, rows, :].astype(F32) + back.astype(F32)).astype(BF)

    for k in range(4):
        parts = jnp.concatenate([gq[q, 32 * k : 32 * k + 64, :] for q in range(4)], axis=0)
        gn[WRP * k : WRP * k + WRP, :] = dot(pi_ref[k], parts).astype(BF)

    stores = []

    def store(src, dst):
        copy = pltpu.make_async_copy(src, dst, sems.at[9 + len(stores)])
        copy.start()
        stores.append(copy)

    def put(j, block):
        columns = slice(D * j, D * j + D)
        pairs = block.astype(BF).reshape(mine.shape[0], 2, mine.shape[1], D)
        even, odd = pairs[:, 0], pairs[:, 1]
        mine[:, :, columns] = jnp.where(core == 0, even, odd)
        other[:, :, columns] = jnp.where(core == 0, odd, even)
        store(other.at[:, :, columns], other_hbm.at[:, :, columns])
        store(mine.at[:, :, columns], mine_hbm.at[:, :, columns])

    for load in loads[5:]:
        load.wait()
    inner = slice(0, 4 * WRP)
    store(gn, gn_hbm)
    put(3, dot_tn(attn[inner, :], gn[...]))

    for j in range(2):
        columns = slice(256 * j, 256 * j + 256)
        d_attn[:, columns] = dot_nt(gn[...], wproj[columns, :]).astype(BF)

    def backward(k, carry):
        start = pl.multiple_of(k * WRP, 16)
        masked = masked_at(k)
        parts = [heads(qkv, start, w, hp, low) for w, hp in UNITS]
        do = [
            stacked(d_attn[win, 128 * hp : 128 * hp + 128], low)
            for (_, hp), (_, _, _, win) in zip(UNITS, parts)
        ]
        dp = [dot_nt(v2, d)[:WIN] for d, (_, _, v2, _) in zip(do, parts)]
        p = [probs[k, 4 * w + hp] for w, hp in UNITS]
        dv = [dot(padded_keys(v), d) for v, d in zip(p, do)]
        dp = [v.astype(BF).astype(F32) for v in dp]
        inner = [jnp.sum(a * b, axis=0, keepdims=True) for a, b in zip(dp, p)]
        ds = [b * (a - c) for a, b, c in zip(dp, p, inner)]
        ds = [padded_keys(jnp.where(masked, 0.0, v)) for v in ds]
        dk = [dot(v, qs) for v, (qs, _, _, _) in zip(ds, parts)]
        dq = [over_queries(v, k2, first_lane) * 0.125 for v, (_, k2, _, _) in zip(ds, parts)]
        for i, ((_, hp), (_, _, _, win)) in enumerate(zip(UNITS, parts)):
            lanes = slice(128 * hp, 128 * hp + 128)
            dqkv[win, lanes] = dq[i].astype(BF)
            dqkv[win, D + lanes.start : D + lanes.stop] = dk[i].astype(BF)
            dqkv[win, 2 * D + lanes.start : 2 * D + lanes.stop] = dv[i].astype(BF)
        return carry

    lax.fori_loop(0, 4, backward, 0)
    store(dqkv, dqkv_hbm)
    for j in range(3):
        put(j, dot_tn(normed[inner, :], dqkv[:, D * j : D * j + D]))
    for copy in stores:
        copy.wait()


def finish_kernel(early_ref, late_ref, gn_ref, dqkv_ref, wqkv_ref, ng_ref, px_ref, pxt_ref, dwork_ref, d_normed):
    for j in range(2):
        columns = slice(256 * j, 256 * j + 256)
        d_normed[:, columns] = dot_nt(dqkv_ref[...], wqkv_ref[columns, :]).astype(BF)

    for k in range(4):
        rows = slice(WRP * k, WRP * k + WRP)
        x = early_ref[WR * k : WR * k + WR, :] if k < EARLY else late_ref[:WR, :]
        hat, scale = norm_parts(dot(px_ref[...], x))
        back = norm_back(hat, scale, d_normed[rows, :].astype(F32) * ng_ref[...])
        d_work = (gn_ref[rows, :].astype(F32) + back).astype(BF)
        dwork_ref[WR * k : WR * k + WR, :] = dot(pxt_ref[...], d_work).astype(BF)


VMEM = pl.BlockSpec(memory_space=pltpu.VMEM)
HBM = pl.BlockSpec(memory_space=pl.ANY)


def start_early(x, norm_gain, w_qkv, w_proj):
    rows = EARLY * WRP
    shapes = [((rows, D), BF), ((rows, 3 * D), BF), ((EARLY, HEADS, WIN, 256), F32), ((rows, D), BF), ((rows, D), BF)]
    return pl.pallas_call(
        early_kernel,
        out_shape=tuple(jax.ShapeDtypeStruct(*one) for one in shapes),
        in_specs=[VMEM] * 5,
        out_specs=(VMEM,) * 5,
        scratch_shapes=[pltpu.VMEM((rows, D), BF)],
        compiler_params=pltpu.CompilerParams(vmem_limit_bytes=SMALL_GRANT),
        cost_estimate=pl.CostEstimate(flops=1_400_000_000, bytes_accessed=8_000_000, transcendentals=0),
        name="block_early",
    )(x, jnp.asarray(to_windows()), norm_gain[None], w_qkv, w_proj)


def compute(tiles, lats, early, x, c, norm_gain, w_qkv, w_proj, merge_gain, w_merge, w_expand, expand_gain):
    bf = lambda *shape: pltpu.VMEM(shape, BF)
    share = (tiles, D // (2 * tiles), 4 * D)
    return pl.pallas_call(
        functools.partial(kernel, lats),
        out_shape=tuple(
            jax.ShapeDtypeStruct(shape, BF) for shape in (share, share, (4 * WRP, D), (4 * WRP, 3 * D))
        ),
        in_specs=[VMEM] * 10 + [HBM] * 9,
        out_specs=(HBM,) * 4,
        scratch_shapes=[
            bf(D, 3 * D), bf(D, D), bf(4 * D, 2 * D), bf(2 * D, 4 * D),
            bf((NWR - EARLY) * WRP, D), bf(NWR * WRP, D), bf(NWR * WRP, 3 * D), pltpu.VMEM((NWR, HEADS, WIN, 256), F32),
            bf(NWR * WRP, D), bf(NWR * WRP, D),
            bf(4, QROWS, D), bf(4, QROWS, D), bf(QROWS, 4 * D), bf(QROWS, 4 * D), bf(4, QROWS, D),
            bf(4 * WRP, D), bf(4 * WRP, D), bf(4 * WRP, 3 * D), bf(*share), bf(*share),
            pltpu.SemaphoreType.DMA((19,)),
        ],
        compiler_params=pltpu.CompilerParams(vmem_limit_bytes=GRANT),
        cost_estimate=pl.CostEstimate(flops=7_000_000_000, bytes_accessed=18_000_000, transcendentals=0),
        name="block",
    )(
        x, c, norm_gain[None], merge_gain[None], expand_gain[None],
        jnp.asarray(to_windows()), jnp.asarray(fine_offsets()),
        jnp.asarray(cot_offsets(4, 48)), jnp.asarray(cot_offsets(1, 16)), jnp.asarray(from_offsets()),
        w_qkv, w_proj, w_merge, w_expand, *early,
    )


def finish_tokens(x_early, x, gn, dqkv, w_qkv, norm_gain):
    return pl.pallas_call(
        finish_kernel,
        out_shape=jax.ShapeDtypeStruct((4 * WR, D), BF),
        in_specs=[VMEM] * 8,
        out_specs=VMEM,
        scratch_shapes=[pltpu.VMEM((4 * WRP, D), BF)],
        compiler_params=pltpu.CompilerParams(vmem_limit_bytes=SMALL_GRANT),
        cost_estimate=pl.CostEstimate(flops=1_200_000_000, bytes_accessed=6_000_000, transcendentals=0),
        name="block_tokens",
    )(x_early, x, gn, dqkv, w_qkv, norm_gain[None], jnp.asarray(to_windows()), jnp.asarray(to_windows().T))


def body(tokens, cotangent, norm_gain, w_qkv, w_proj, merge_gain, w_merge, w_expand, expand_gain):
    lats, tiles, cores = lax.axis_size("lat"), lax.axis_size("tile"), lax.axis_size("core")
    lons = tiles * cores
    names = ("lat", "tile", "core")

    def moved(value, dlat, dlon):
        pairs = []
        for a in range(lats):
            for b in range(lons):
                pairs.append((a * lons + b, ((a + dlat) % lats) * lons + (b + dlon) % lons))
        return lax.ppermute(value, names, pairs)

    beside = moved(jnp.concatenate([tokens[:, :SLON], cotangent[:, :SLON]], axis=0), 0, -1)
    work = jnp.concatenate([tokens[:, SLON:], beside[:ROWS]], axis=1)
    cwork = jnp.concatenate([cotangent[:, SLON:], beside[ROWS:]], axis=1)
    first, last = SLAT, ROWS - SLAT
    below = moved(jnp.concatenate([work[:9], cwork[:4]], axis=0), -1, 0)
    above = moved(work[last:], 1, 0)

    x_early = work[first:last].reshape(EARLY * WR, D)
    early = start_early(x_early, norm_gain, w_qkv, w_proj)
    early, below, above = lax.optimization_barrier((early, below, above))

    x = jnp.concatenate([work[last:], below[:9], above, work[:first]], axis=0)
    x = x.reshape((NWR - EARLY) * WR, D)
    c = jnp.concatenate([cwork, below[9:]], axis=0).reshape(CROWS * COLS, D)

    mine, other, gn, dqkv = compute(
        tiles, lats, early, x, c, norm_gain, w_qkv, w_proj, merge_gain, w_merge, w_expand, expand_gain
    )

    theirs = lax.ppermute(other, "core", [(i, cores - 1 - i) for i in range(cores)])
    pair, dqkv = lax.optimization_barrier((mine + theirs, dqkv))
    spread = lax.all_to_all(pair, "tile", 0, 0, tiled=True)

    d_work = finish_tokens(x_early, x, gn, dqkv, w_qkv, norm_gain).reshape(ROWS, COLS, D)
    last_row, last_col = ROWS - SLAT, COLS - SLON
    rows = moved(d_work[last_row:, :last_col], 1, 0)
    corner = moved(d_work[last_row:, last_col:], 1, 1)
    edge = d_work[:last_row, last_col:]
    spread, rows, corner, edge = lax.optimization_barrier((spread, rows, corner, edge))
    columns = moved(edge, 0, 1)
    top = jnp.concatenate([corner, rows], axis=1)
    rest = jnp.concatenate([columns, d_work[:last_row, :last_col]], axis=1)
    d_tokens = jnp.concatenate([top, rest], axis=0)

    share = jnp.sum(spread.astype(F32), axis=0).astype(BF)
    copies = jnp.broadcast_to(share[None], (lats,) + share.shape)
    gathered = lax.all_to_all(copies, "lat", 0, 0, tiled=True)
    grad_qkv = jnp.sum(gathered[:, :, : 3 * D].astype(F32), axis=0)
    grad_proj = jnp.sum(gathered[:, :, 3 * D :].astype(F32), axis=0)
    return (d_tokens, grad_qkv, grad_proj)


def solution(mesh):
    lats, lons = mesh.shape["lat"], mesh.shape["lon"]
    fine_mesh = Mesh(mesh.devices.reshape(lats, lons // 2, 2), ("lat", "tile", "core"))
    lon = ("tile", "core")
    in_specs = (P("lat", lon, None), P("lat", lon, None), P(), P(), P(), P(), P(), P(), P())
    out_specs = (P("lat", lon, None), P(lon, None), P(lon, None))
    return jax.shard_map(body, mesh=fine_mesh, in_specs=in_specs, out_specs=out_specs, check_vma=False)
```

```python
import functools

import jax
import jax.numpy as jnp
import numpy as np
from jax import lax
from jax.experimental import pallas as pl
from jax.experimental.pallas import tpu as pltpu
from jax.sharding import Mesh, PartitionSpec as P

HEADS = 8
HEAD = 64
WLAT = 6
WLON = 12
SLAT = 3
SLON = 6
D = 512
ROWS = 24
COLS = 24
WR = WLAT * COLS
WIN = WLAT * WLON
WP = 80
WRP = 2 * WP
NWR = 6
EARLY = 3
CROWS = 28
PAIRS = 13
QROWS = 160

EPSILON = 1e-05
GRANT = 40 * 1024 * 1024
SMALL_GRANT = 24 * 1024 * 1024
MASKED = -1000000000.0
OUTSIDE = -3.0e38
BF = jnp.bfloat16
F32 = jnp.float32


def window_row(i, col):
    return (col // WLON) * WP + i * WLON + col % WLON


def to_windows():
    out = np.zeros((WRP, WR), np.float32)
    for t in range(WR):
        out[window_row(t // COLS, t % COLS), t] = 1
    return out.astype(jnp.bfloat16)


def cot_offsets(pairs, padded):
    out = np.zeros((4 * padded, pairs * 2 * COLS), np.float32)
    for a in range(pairs):
        for rp in range(2):
            for col in range(COLS):
                q = (col % 2) * 2 + rp
                out[q * padded + a * 12 + col // 2, (2 * a + rp) * COLS + col] = 1
    return out.astype(jnp.bfloat16)


FINE_PARTS = ((0, 0), (0, 1), (0, 2), (1, 2), (1, 3), (2, 3), (2, 4), (3, 4), (3, 5))


def fine_offsets():
    out = np.zeros((len(FINE_PARTS), 4 * 48, WRP), np.float32)
    for n, (g, k) in enumerate(FINE_PARTS):
        padded = 48 if g < 3 else 16
        for a in range(4 * g, min(4 * g + 4, PAIRS)):
            for rp in range(2):
                f = 5 + 2 * a + rp
                if f // WLAT != k:
                    continue
                for col in range(COLS):
                    q = (col % 2) * 2 + rp
                    out[n, q * padded + (a - 4 * g) * 12 + col // 2, window_row(f % WLAT, col)] = 1
    return out.astype(jnp.bfloat16)


def from_offsets():
    out = np.zeros((4, WRP, 256), np.float32)
    for k in range(1, 5):
        for t in range(WR):
            f = WLAT * k + t // COLS
            col = t % COLS
            a, rp = divmod(f - 5, 2)
            q = (col % 2) * 2 + rp
            out[k - 1, window_row(t // COLS, col), q * 64 + 12 * a + col // 2 - 32 * (k - 1)] = 1
    return out.astype(jnp.bfloat16)


def dot(a, b):
    return jnp.dot(a, b, preferred_element_type=F32)


def dot_nt(a, b):
    return lax.dot_general(a, b, (((1,), (1,)), ((), ())), preferred_element_type=F32)


def dot_tn(a, b):
    return lax.dot_general(a, b, (((0,), (0,)), ((), ())), preferred_element_type=F32)


def norm_parts(values):
    average = jnp.mean(values, axis=-1, keepdims=True)
    centred = values - average
    spread = jnp.mean(centred * centred, axis=-1, keepdims=True)
    scale = lax.rsqrt(spread + EPSILON)
    return centred * scale, scale


def norm_back(hat, scale, dy):
    mean_dy = jnp.mean(dy, axis=-1, keepdims=True)
    mean_dyh = jnp.mean(dy * hat, axis=-1, keepdims=True)
    return scale * (dy - mean_dy - hat * mean_dyh)


def stacked(two, low):
    gap = jnp.zeros((128 - WP, 2 * HEAD), BF)
    return jnp.concatenate([two * low, gap, two * (1 - low), gap], axis=0)


def over_queries(keys_by_queries, rows, first_lane):
    both = [dot_tn(keys_by_queries[:, 128 * i : 128 * i + WP], rows) for i in range(2)]
    return jnp.where(first_lane, both[0], both[1])


def padded_keys(values):
    return jnp.concatenate([values, jnp.zeros((WP - WIN, 256), F32)], axis=0).astype(BF)


UNITS = [(w, hp) for w in range(2) for hp in range(HEADS // 2)]


def lane_halves():
    first_lane = lax.broadcasted_iota(jnp.int32, (1, 2 * HEAD), 1) < HEAD
    return first_lane, first_lane.astype(F32).astype(BF)


def rows_of(start, size):
    return pl.ds(pl.multiple_of(start, 16), size)


def heads(qkv, start, w, hp, low):
    win = rows_of(start + WP * w, WP)
    q2 = qkv[win, 128 * hp : 128 * hp + 128]
    k2 = qkv[win, D + 128 * hp : D + 128 * hp + 128]
    v2 = qkv[win, 2 * D + 128 * hp : 2 * D + 128 * hp + 128]
    return stacked(q2 * 0.125, low), k2, v2, win


def attention(first, mask, x_ref, px, gain, wqkv, wproj, xw, normed, qkv, probs, attn, fine):
    first_lane, low = lane_halves()
    base = WRP * first
    span = slice(base, base + 3 * WRP)
    for k in range(3):
        rows = slice(base + WRP * k, base + WRP * k + WRP)
        x = dot(px[...], x_ref[WR * k : WR * k + WR, :])
        xw[WRP * k : WRP * k + WRP, :] = x.astype(BF)
        hat, _ = norm_parts(x)
        normed[rows, :] = (hat * gain[...]).astype(BF)
    for j in range(6):
        columns = slice(256 * j, 256 * j + 256)
        qkv[span, columns] = dot(normed[span, :], wqkv[:, columns]).astype(BF)

    def window_row(k, carry):
        masked = None if mask is None else mask(k)
        parts = [heads(qkv, k * WRP, w, hp, low) for w, hp in UNITS]
        s = [dot_nt(k2, qs)[:WIN] for qs, k2, _, _ in parts]
        if masked is not None:
            s = [jnp.where(masked, MASKED, v) for v in s]
        top = [jnp.max(v, axis=0, keepdims=True) for v in s]
        e = [jnp.exp(v - t) for v, t in zip(s, top)]
        total = [jnp.sum(v, axis=0, keepdims=True) for v in e]
        p = [v * (1.0 / t) for v, t in zip(e, total)]
        for (w, hp), v in zip(UNITS, p):
            probs[k, 4 * w + hp] = v
        o = [over_queries(padded_keys(v), v2, first_lane) for v, (_, _, v2, _) in zip(p, parts)]
        for (w, hp), v, (_, _, _, win) in zip(UNITS, o, parts):
            attn[win, 128 * hp : 128 * hp + 128] = v.astype(BF)
        return carry

    lax.fori_loop(first, first + 3, window_row, 0)
    for j in range(2):
        columns = slice(256 * j, 256 * j + 256)
        fine[span, columns] = (
            xw[:, columns].astype(F32) + dot(attn[span, :], wproj[:, columns])
        ).astype(BF)


def early_kernel(x_ref, px_ref, ng_ref, wqkv, wproj, normed, qkv, probs, attn, fine, xw):
    attention(0, None, x_ref, px_ref, ng_ref, wqkv, wproj, xw, normed, qkv, probs, attn, fine)


def kernel(
    lat_size, x_ref, c_ref, ng_ref, mg_ref, eg_ref, px_ref, pf_ref, pc_ref, pc3_ref, pi_ref,
    wqkv_hbm, wproj_hbm, wm_hbm, we_hbm, normed_hbm, qkv_hbm, probs_hbm, attn_hbm, fine_hbm,
    mine_hbm, other_hbm, gn_hbm, dqkv_hbm,
    wqkv, wproj, wm, we, xw, normed, qkv, probs, attn, fine, fq, cq, mg, dw, gq, gn, d_attn, dqkv, mine, other, sems,
):
    lat = lax.axis_index("lat")
    core = lax.axis_index("core")
    done = slice(0, EARLY * WRP)
    sources = (
        (wqkv_hbm, wqkv), (wproj_hbm, wproj), (fine_hbm, fine.at[done]), (wm_hbm, wm), (we_hbm, we),
        (probs_hbm, probs.at[0:EARLY]), (qkv_hbm, qkv.at[done]),
        (attn_hbm, attn.at[done]), (normed_hbm, normed.at[done]),
    )
    loads = [pltpu.make_async_copy(src, dst, sems.at[i]) for i, (src, dst) in enumerate(sources)]
    for load in loads:
        load.start()

    key = lax.broadcasted_iota(jnp.int32, (WIN, 256), 0)
    query = lax.broadcasted_iota(jnp.int32, (WIN, 256), 1) % 128
    apart = (key >= WIN // 2) != (query >= WIN // 2)
    first_lane, low = lane_halves()

    def masked_at(k):
        edge = ((k == NWR - 1) & (lat == 0)) | ((k == EARLY) & (lat == lat_size - 1))
        return apart & edge

    loads[0].wait()
    loads[1].wait()
    attention(EARLY, masked_at, x_ref, px_ref, ng_ref, wqkv, wproj, xw, normed, qkv, probs, attn, fine)
    loads[2].wait()

    for g in range(4):
        n = 48 if g < 3 else 16
        f = sum(
            dot(pf_ref[m, : 4 * n, :], fine[WRP * k : WRP * k + WRP, :])
            for m, (gg, k) in enumerate((g_, (k_ - 1) % NWR) for g_, k_ in FINE_PARTS)
            if gg == g
        ).astype(BF)
        if g < 3:
            c = dot(pc_ref[...], c_ref[48 + 192 * g : 48 + 192 * g + 192, :]).astype(BF)
        else:
            c = dot(pc3_ref[...], c_ref[624:672, :]).astype(BF)
        for q in range(4):
            fq[q, 48 * g : 48 * g + n, :] = f[n * q : n * q + n]
            cq[q, 48 * g : 48 * g + n, :] = c[n * q : n * q + n]

    def merge_stats(rows):
        total = jnp.zeros((32, 1), F32)
        for q in range(4):
            total = total + jnp.sum(fq[q, rows, :].astype(F32), axis=-1, keepdims=True)
        average = total * (1.0 / (4 * D))
        total = jnp.zeros((32, 1), F32)
        for q in range(4):
            centred = fq[q, rows, :].astype(F32) - average
            total = total + jnp.sum(centred * centred, axis=-1, keepdims=True)
        return average, lax.rsqrt(total * (1.0 / (4 * D)) + EPSILON)

    for r in range(QROWS // 32):
        rows = slice(32 * r, 32 * r + 32)
        average, scale = merge_stats(rows)
        for q in range(4):
            hat = (fq[q, rows, :].astype(F32) - average) * scale
            mg[rows, D * q : D * q + D] = (hat * mg_ref[:, D * q : D * q + D]).astype(BF)

    loads[3].wait()
    loads[4].wait()
    coarse = dot(mg[...], wm[...]).astype(BF)
    for q in range(4):
        qq = (0, 2, 1, 3)[q]
        wide = dot(coarse, we[:, D * qq : D * qq + D])
        hat, scale = norm_parts(wide)
        dy = cq[q].astype(F32) * eg_ref[...]
        dw[:, D * qq : D * qq + D] = norm_back(hat, scale, dy).astype(BF)
    d_coarse = dot_nt(dw[...], we[...]).astype(BF)
    mg[...] = dot_nt(d_coarse, wm[...]).astype(BF)

    for r in range(QROWS // 32):
        rows = slice(32 * r, 32 * r + 32)
        average, scale = merge_stats(rows)
        sum_dy = jnp.zeros((32, 1), F32)
        sum_dyh = jnp.zeros((32, 1), F32)
        for q in range(4):
            hat = (fq[q, rows, :].astype(F32) - average) * scale
            dy = mg[rows, D * q : D * q + D].astype(F32) * mg_ref[:, D * q : D * q + D]
            sum_dy = sum_dy + jnp.sum(dy, axis=-1, keepdims=True)
            sum_dyh = sum_dyh + jnp.sum(dy * hat, axis=-1, keepdims=True)
        mean_dy = sum_dy * (1.0 / (4 * D))
        mean_dyh = sum_dyh * (1.0 / (4 * D))
        for q in range(4):
            hat = (fq[q, rows, :].astype(F32) - average) * scale
            dy = mg[rows, D * q : D * q + D].astype(F32) * mg_ref[:, D * q : D * q + D]
            back = (scale * (dy - mean_dy - hat * mean_dyh)).astype(BF)
            gq[q, rows, :] = (cq[q, rows, :].astype(F32) + back.astype(F32)).astype(BF)

    for k in range(4):
        parts = jnp.concatenate([gq[q, 32 * k : 32 * k + 64, :] for q in range(4)], axis=0)
        gn[WRP * k : WRP * k + WRP, :] = dot(pi_ref[k], parts).astype(BF)

    stores = []

    def store(src, dst):
        copy = pltpu.make_async_copy(src, dst, sems.at[9 + len(stores)])
        copy.start()
        stores.append(copy)

    def put(j, block):
        columns = slice(D * j, D * j + D)
        pairs = block.astype(BF).reshape(mine.shape[0], 2, mine.shape[1], D)
        even, odd = pairs[:, 0], pairs[:, 1]
        mine[:, :, columns] = jnp.where(core == 0, even, odd)
        other[:, :, columns] = jnp.where(core == 0, odd, even)
        store(other.at[:, :, columns], other_hbm.at[:, :, columns])
        store(mine.at[:, :, columns], mine_hbm.at[:, :, columns])

    for load in loads[5:]:
        load.wait()
    inner = slice(0, 4 * WRP)
    store(gn, gn_hbm)
    put(3, dot_tn(attn[inner, :], gn[...]))

    for j in range(2):
        columns = slice(256 * j, 256 * j + 256)
        d_attn[:, columns] = dot_nt(gn[...], wproj[columns, :]).astype(BF)

    def backward(k, carry):
        start = pl.multiple_of(k * WRP, 16)
        masked = masked_at(k)
        parts = [heads(qkv, start, w, hp, low) for w, hp in UNITS]
        do = [
            stacked(d_attn[win, 128 * hp : 128 * hp + 128], low)
            for (_, hp), (_, _, _, win) in zip(UNITS, parts)
        ]
        dp = [dot_nt(v2, d)[:WIN] for d, (_, _, v2, _) in zip(do, parts)]
        p = [probs[k, 4 * w + hp] for w, hp in UNITS]
        dv = [dot(padded_keys(v), d) for v, d in zip(p, do)]
        dp = [v.astype(BF).astype(F32) for v in dp]
        inner = [jnp.sum(a * b, axis=0, keepdims=True) for a, b in zip(dp, p)]
        ds = [b * (a - c) for a, b, c in zip(dp, p, inner)]
        ds = [padded_keys(jnp.where(masked, 0.0, v)) for v in ds]
        dk = [dot(v, qs) for v, (qs, _, _, _) in zip(ds, parts)]
        dq = [over_queries(v, k2, first_lane) * 0.125 for v, (_, k2, _, _) in zip(ds, parts)]
        for i, ((_, hp), (_, _, _, win)) in enumerate(zip(UNITS, parts)):
            lanes = slice(128 * hp, 128 * hp + 128)
            dqkv[win, lanes] = dq[i].astype(BF)
            dqkv[win, D + lanes.start : D + lanes.stop] = dk[i].astype(BF)
            dqkv[win, 2 * D + lanes.start : 2 * D + lanes.stop] = dv[i].astype(BF)
        return carry

    lax.fori_loop(0, 4, backward, 0)
    store(dqkv, dqkv_hbm)
    for j in range(3):
        put(j, dot_tn(normed[inner, :], dqkv[:, D * j : D * j + D]))
    for copy in stores:
        copy.wait()


def finish_kernel(early_ref, late_ref, gn_ref, dqkv_ref, wqkv_ref, ng_ref, px_ref, pxt_ref, dwork_ref, d_normed):
    for j in range(2):
        columns = slice(256 * j, 256 * j + 256)
        d_normed[:, columns] = dot_nt(dqkv_ref[...], wqkv_ref[columns, :]).astype(BF)

    for k in range(4):
        rows = slice(WRP * k, WRP * k + WRP)
        x = early_ref[WR * k : WR * k + WR, :] if k < EARLY else late_ref[:WR, :]
        hat, scale = norm_parts(dot(px_ref[...], x))
        back = norm_back(hat, scale, d_normed[rows, :].astype(F32) * ng_ref[...])
        d_work = (gn_ref[rows, :].astype(F32) + back).astype(BF)
        dwork_ref[WR * k : WR * k + WR, :] = dot(pxt_ref[...], d_work).astype(BF)


VMEM = pl.BlockSpec(memory_space=pltpu.VMEM)
HBM = pl.BlockSpec(memory_space=pl.ANY)


def start_early(x, norm_gain, w_qkv, w_proj):
    rows = EARLY * WRP
    shapes = [((rows, D), BF), ((rows, 3 * D), BF), ((EARLY, HEADS, WIN, 256), F32), ((rows, D), BF), ((rows, D), BF)]
    return pl.pallas_call(
        early_kernel,
        out_shape=tuple(jax.ShapeDtypeStruct(*one) for one in shapes),
        in_specs=[VMEM] * 5,
        out_specs=(VMEM,) * 5,
        scratch_shapes=[pltpu.VMEM((rows, D), BF)],
        compiler_params=pltpu.CompilerParams(vmem_limit_bytes=SMALL_GRANT),
        cost_estimate=pl.CostEstimate(flops=1_400_000_000, bytes_accessed=8_000_000, transcendentals=0),
        name="block_early",
    )(x, jnp.asarray(to_windows()), norm_gain[None], w_qkv, w_proj)


def compute(tiles, lats, early, x, c, norm_gain, w_qkv, w_proj, merge_gain, w_merge, w_expand, expand_gain):
    bf = lambda *shape: pltpu.VMEM(shape, BF)
    share = (tiles, D // (2 * tiles), 4 * D)
    return pl.pallas_call(
        functools.partial(kernel, lats),
        out_shape=tuple(
            jax.ShapeDtypeStruct(shape, BF) for shape in (share, share, (4 * WRP, D), (4 * WRP, 3 * D))
        ),
        in_specs=[VMEM] * 10 + [HBM] * 9,
        out_specs=(HBM,) * 4,
        scratch_shapes=[
            bf(D, 3 * D), bf(D, D), bf(4 * D, 2 * D), bf(2 * D, 4 * D),
            bf((NWR - EARLY) * WRP, D), bf(NWR * WRP, D), bf(NWR * WRP, 3 * D), pltpu.VMEM((NWR, HEADS, WIN, 256), F32),
            bf(NWR * WRP, D), bf(NWR * WRP, D),
            bf(4, QROWS, D), bf(4, QROWS, D), bf(QROWS, 4 * D), bf(QROWS, 4 * D), bf(4, QROWS, D),
            bf(4 * WRP, D), bf(4 * WRP, D), bf(4 * WRP, 3 * D), bf(*share), bf(*share),
            pltpu.SemaphoreType.DMA((19,)),
        ],
        compiler_params=pltpu.CompilerParams(vmem_limit_bytes=GRANT),
        cost_estimate=pl.CostEstimate(flops=7_000_000_000, bytes_accessed=18_000_000, transcendentals=0),
        name="block",
    )(
        x, c, norm_gain[None], merge_gain[None], expand_gain[None],
        jnp.asarray(to_windows()), jnp.asarray(fine_offsets()),
        jnp.asarray(cot_offsets(4, 48)), jnp.asarray(cot_offsets(1, 16)), jnp.asarray(from_offsets()),
        w_qkv, w_proj, w_merge, w_expand, *early,
    )


def finish_tokens(x_early, x, gn, dqkv, w_qkv, norm_gain):
    return pl.pallas_call(
        finish_kernel,
        out_shape=jax.ShapeDtypeStruct((4 * WR, D), BF),
        in_specs=[VMEM] * 8,
        out_specs=VMEM,
        scratch_shapes=[pltpu.VMEM((4 * WRP, D), BF)],
        compiler_params=pltpu.CompilerParams(vmem_limit_bytes=SMALL_GRANT),
        cost_estimate=pl.CostEstimate(flops=1_200_000_000, bytes_accessed=6_000_000, transcendentals=0),
        name="block_tokens",
    )(x_early, x, gn, dqkv, w_qkv, norm_gain[None], jnp.asarray(to_windows()), jnp.asarray(to_windows().T))


def body(tokens, cotangent, norm_gain, w_qkv, w_proj, merge_gain, w_merge, w_expand, expand_gain):
    lats, tiles, cores = lax.axis_size("lat"), lax.axis_size("tile"), lax.axis_size("core")
    lons = tiles * cores
    names = ("lat", "tile", "core")

    def moved(value, dlat, dlon):
        pairs = []
        for a in range(lats):
            for b in range(lons):
                pairs.append((a * lons + b, ((a + dlat) % lats) * lons + (b + dlon) % lons))
        return lax.ppermute(value, names, pairs)

    beside = moved(jnp.concatenate([tokens[:, :SLON], cotangent[:, :SLON]], axis=0), 0, -1)
    work = jnp.concatenate([tokens[:, SLON:], beside[:ROWS]], axis=1)
    cwork = jnp.concatenate([cotangent[:, SLON:], beside[ROWS:]], axis=1)
    first, last = SLAT, ROWS - SLAT
    below = moved(jnp.concatenate([work[:9], cwork[:4]], axis=0), -1, 0)
    above = moved(work[last:], 1, 0)

    x_early = work[first:last].reshape(EARLY * WR, D)
    early = start_early(x_early, norm_gain, w_qkv, w_proj)
    early, below, above = lax.optimization_barrier((early, below, above))

    x = jnp.concatenate([work[last:], below[:9], above, work[:first]], axis=0)
    x = x.reshape((NWR - EARLY) * WR, D)
    c = jnp.concatenate([cwork, below[9:]], axis=0).reshape(CROWS * COLS, D)

    mine, other, gn, dqkv = compute(
        tiles, lats, early, x, c, norm_gain, w_qkv, w_proj, merge_gain, w_merge, w_expand, expand_gain
    )

    theirs = lax.ppermute(other, "core", [(i, cores - 1 - i) for i in range(cores)])
    pair, dqkv = lax.optimization_barrier((mine + theirs, dqkv))
    spread = lax.all_to_all(pair, "tile", 0, 0, tiled=True)

    d_work = finish_tokens(x_early, x, gn, dqkv, w_qkv, norm_gain).reshape(ROWS, COLS, D)
    last_row, last_col = ROWS - SLAT, COLS - SLON
    rows = moved(d_work[last_row:, :last_col], 1, 0)
    corner = moved(d_work[last_row:, last_col:], 1, 1)
    edge = d_work[:last_row, last_col:]
    spread, rows, corner, edge = lax.optimization_barrier((spread, rows, corner, edge))
    columns = moved(edge, 0, 1)
    top = jnp.concatenate([corner, rows], axis=1)
    rest = jnp.concatenate([columns, d_work[:last_row, :last_col]], axis=1)
    d_tokens = jnp.concatenate([top, rest], axis=0)

    share = jnp.sum(spread.astype(F32), axis=0).astype(BF)
    copies = jnp.broadcast_to(share[None], (lats,) + share.shape)
    gathered = lax.all_to_all(copies, "lat", 0, 0, tiled=True)
    grad_qkv = jnp.sum(gathered[:, :, : 3 * D].astype(F32), axis=0)
    grad_proj = jnp.sum(gathered[:, :, 3 * D :].astype(F32), axis=0)
    return (d_tokens, grad_qkv, grad_proj)


def solution(mesh):
    lats, lons = mesh.shape["lat"], mesh.shape["lon"]
    fine_mesh = Mesh(mesh.devices.reshape(lats, lons // 2, 2), ("lat", "tile", "core"))
    lon = ("tile", "core")
    in_specs = (P("lat", lon, None), P("lat", lon, None), P(), P(), P(), P(), P(), P(), P())
    out_specs = (P("lat", lon, None), P(lon, None), P(lon, None))
    return jax.shard_map(body, mesh=fine_mesh, in_specs=in_specs, out_specs=out_specs, check_vma=False)
```

```python
import functools

import jax
import jax.numpy as jnp
import numpy as np
from jax import lax
from jax.experimental import pallas as pl
from jax.experimental.pallas import tpu as pltpu
from jax.sharding import Mesh, PartitionSpec as P

HEADS = 8
HEAD = 64
WLAT = 6
WLON = 12
SLAT = 3
SLON = 6
D = 512
ROWS = 24
COLS = 24
WR = WLAT * COLS
WIN = WLAT * WLON
WP = 80
WRP = 2 * WP
NWR = 6
EARLY = 3
CROWS = 28
PAIRS = 13
QROWS = 160

EPSILON = 1e-05
GRANT = 40 * 1024 * 1024
SMALL_GRANT = 24 * 1024 * 1024
MASKED = -1000000000.0
OUTSIDE = -3.0e38
BF = jnp.bfloat16
F32 = jnp.float32


def window_row(i, col):
    return (col // WLON) * WP + i * WLON + col % WLON


def to_windows():
    out = np.zeros((WRP, WR), np.float32)
    for t in range(WR):
        out[window_row(t // COLS, t % COLS), t] = 1
    return out.astype(jnp.bfloat16)


def cot_offsets(pairs, padded):
    out = np.zeros((4 * padded, pairs * 2 * COLS), np.float32)
    for a in range(pairs):
        for rp in range(2):
            for col in range(COLS):
                q = (col % 2) * 2 + rp
                out[q * padded + a * 12 + col // 2, (2 * a + rp) * COLS + col] = 1
    return out.astype(jnp.bfloat16)


FINE_PARTS = ((0, 0), (0, 1), (0, 2), (1, 2), (1, 3), (2, 3), (2, 4), (3, 4), (3, 5))


def fine_offsets():
    out = np.zeros((len(FINE_PARTS), 4 * 48, WRP), np.float32)
    for n, (g, k) in enumerate(FINE_PARTS):
        padded = 48 if g < 3 else 16
        for a in range(4 * g, min(4 * g + 4, PAIRS)):
            for rp in range(2):
                f = 5 + 2 * a + rp
                if f // WLAT != k:
                    continue
                for col in range(COLS):
                    q = (col % 2) * 2 + rp
                    out[n, q * padded + (a - 4 * g) * 12 + col // 2, window_row(f % WLAT, col)] = 1
    return out.astype(jnp.bfloat16)


def from_offsets():
    out = np.zeros((4, WRP, 256), np.float32)
    for k in range(1, 5):
        for t in range(WR):
            f = WLAT * k + t // COLS
            col = t % COLS
            a, rp = divmod(f - 5, 2)
            q = (col % 2) * 2 + rp
            out[k - 1, window_row(t // COLS, col), q * 64 + 12 * a + col // 2 - 32 * (k - 1)] = 1
    return out.astype(jnp.bfloat16)


def dot(a, b):
    return jnp.dot(a, b, preferred_element_type=F32)


def dot_nt(a, b):
    return lax.dot_general(a, b, (((1,), (1,)), ((), ())), preferred_element_type=F32)


def dot_tn(a, b):
    return lax.dot_general(a, b, (((0,), (0,)), ((), ())), preferred_element_type=F32)


def norm_parts(values):
    average = jnp.mean(values, axis=-1, keepdims=True)
    centred = values - average
    spread = jnp.mean(centred * centred, axis=-1, keepdims=True)
    scale = lax.rsqrt(spread + EPSILON)
    return centred * scale, scale


def norm_back(hat, scale, dy):
    mean_dy = jnp.mean(dy, axis=-1, keepdims=True)
    mean_dyh = jnp.mean(dy * hat, axis=-1, keepdims=True)
    return scale * (dy - mean_dy - hat * mean_dyh)


def stacked(two, low):
    gap = jnp.zeros((128 - WP, 2 * HEAD), BF)
    return jnp.concatenate([two * low, gap, two * (1 - low), gap], axis=0)


def over_queries(keys_by_queries, rows, first_lane):
    both = [dot_tn(keys_by_queries[:, 128 * i : 128 * i + WP], rows) for i in range(2)]
    return jnp.where(first_lane, both[0], both[1])


def padded_keys(values):
    return jnp.concatenate([values, jnp.zeros((WP - WIN, 256), F32)], axis=0).astype(BF)


UNITS = [(w, hp) for w in range(2) for hp in range(HEADS // 2)]


def lane_halves():
    first_lane = lax.broadcasted_iota(jnp.int32, (1, 2 * HEAD), 1) < HEAD
    return first_lane, first_lane.astype(F32).astype(BF)


def rows_of(start, size):
    return pl.ds(pl.multiple_of(start, 16), size)


def heads(qkv, start, w, hp, low):
    win = rows_of(start + WP * w, WP)
    q2 = qkv[win, 128 * hp : 128 * hp + 128]
    k2 = qkv[win, D + 128 * hp : D + 128 * hp + 128]
    v2 = qkv[win, 2 * D + 128 * hp : 2 * D + 128 * hp + 128]
    return stacked(q2 * 0.125, low), k2, v2, win


def attention(first, mask, x_ref, px, gain, wqkv, wproj, xw, normed, qkv, probs, attn, fine):
    first_lane, low = lane_halves()
    base = WRP * first
    span = slice(base, base + 3 * WRP)
    for k in range(3):
        rows = slice(base + WRP * k, base + WRP * k + WRP)
        x = dot(px[...], x_ref[WR * k : WR * k + WR, :])
        xw[WRP * k : WRP * k + WRP, :] = x.astype(BF)
        hat, _ = norm_parts(x)
        normed[rows, :] = (hat * gain[...]).astype(BF)
    for j in range(6):
        columns = slice(256 * j, 256 * j + 256)
        qkv[span, columns] = dot(normed[span, :], wqkv[:, columns]).astype(BF)

    def window_row(k, carry):
        masked = None if mask is None else mask(k)
        parts = [heads(qkv, k * WRP, w, hp, low) for w, hp in UNITS]
        s = [dot_nt(k2, qs)[:WIN] for qs, k2, _, _ in parts]
        if masked is not None:
            s = [jnp.where(masked, MASKED, v) for v in s]
        top = [jnp.max(v, axis=0, keepdims=True) for v in s]
        e = [jnp.exp(v - t) for v, t in zip(s, top)]
        total = [jnp.sum(v, axis=0, keepdims=True) for v in e]
        p = [v * (1.0 / t) for v, t in zip(e, total)]
        for (w, hp), v in zip(UNITS, p):
            probs[k, 4 * w + hp] = v
        o = [over_queries(padded_keys(v), v2, first_lane) for v, (_, _, v2, _) in zip(p, parts)]
        for (w, hp), v, (_, _, _, win) in zip(UNITS, o, parts):
            attn[win, 128 * hp : 128 * hp + 128] = v.astype(BF)
        return carry

    lax.fori_loop(first, first + 3, window_row, 0)
    for j in range(2):
        columns = slice(256 * j, 256 * j + 256)
        fine[span, columns] = (
            xw[:, columns].astype(F32) + dot(attn[span, :], wproj[:, columns])
        ).astype(BF)


def early_kernel(x_ref, px_ref, ng_ref, wqkv, wproj, normed, qkv, probs, attn, fine, xw):
    attention(0, None, x_ref, px_ref, ng_ref, wqkv, wproj, xw, normed, qkv, probs, attn, fine)


def kernel(
    lat_size, x_ref, c_ref, ng_ref, mg_ref, eg_ref, px_ref, pf_ref, pc_ref, pc3_ref, pi_ref,
    wqkv_hbm, wproj_hbm, wm_hbm, we_hbm, normed_hbm, qkv_hbm, probs_hbm, attn_hbm, fine_hbm,
    mine_hbm, other_hbm, gn_hbm, dqkv_hbm,
    wqkv, wproj, wm, we, xw, normed, qkv, probs, attn, fine, fq, cq, mg, dw, gq, gn, d_attn, dqkv, mine, other, sems,
):
    lat = lax.axis_index("lat")
    core = lax.axis_index("core")
    done = slice(0, EARLY * WRP)
    sources = (
        (wqkv_hbm, wqkv), (wproj_hbm, wproj), (fine_hbm, fine.at[done]), (wm_hbm, wm), (we_hbm, we),
        (probs_hbm, probs.at[0:EARLY]), (qkv_hbm, qkv.at[done]),
        (attn_hbm, attn.at[done]), (normed_hbm, normed.at[done]),
    )
    loads = [pltpu.make_async_copy(src, dst, sems.at[i]) for i, (src, dst) in enumerate(sources)]
    for load in loads:
        load.start()

    key = lax.broadcasted_iota(jnp.int32, (WIN, 256), 0)
    query = lax.broadcasted_iota(jnp.int32, (WIN, 256), 1) % 128
    apart = (key >= WIN // 2) != (query >= WIN // 2)
    first_lane, low = lane_halves()

    def masked_at(k):
        edge = ((k == NWR - 1) & (lat == 0)) | ((k == EARLY) & (lat == lat_size - 1))
        return apart & edge

    loads[0].wait()
    loads[1].wait()
    attention(EARLY, masked_at, x_ref, px_ref, ng_ref, wqkv, wproj, xw, normed, qkv, probs, attn, fine)
    loads[2].wait()

    for g in range(4):
        n = 48 if g < 3 else 16
        f = sum(
            dot(pf_ref[m, : 4 * n, :], fine[WRP * k : WRP * k + WRP, :])
            for m, (gg, k) in enumerate((g_, (k_ - 1) % NWR) for g_, k_ in FINE_PARTS)
            if gg == g
        ).astype(BF)
        if g < 3:
            c = dot(pc_ref[...], c_ref[48 + 192 * g : 48 + 192 * g + 192, :]).astype(BF)
        else:
            c = dot(pc3_ref[...], c_ref[624:672, :]).astype(BF)
        for q in range(4):
            fq[q, 48 * g : 48 * g + n, :] = f[n * q : n * q + n]
            cq[q, 48 * g : 48 * g + n, :] = c[n * q : n * q + n]

    def merge_stats(rows):
        total = jnp.zeros((32, 1), F32)
        for q in range(4):
            total = total + jnp.sum(fq[q, rows, :].astype(F32), axis=-1, keepdims=True)
        average = total * (1.0 / (4 * D))
        total = jnp.zeros((32, 1), F32)
        for q in range(4):
            centred = fq[q, rows, :].astype(F32) - average
            total = total + jnp.sum(centred * centred, axis=-1, keepdims=True)
        return average, lax.rsqrt(total * (1.0 / (4 * D)) + EPSILON)

    for r in range(QROWS // 32):
        rows = slice(32 * r, 32 * r + 32)
        average, scale = merge_stats(rows)
        for q in range(4):
            hat = (fq[q, rows, :].astype(F32) - average) * scale
            mg[rows, D * q : D * q + D] = (hat * mg_ref[:, D * q : D * q + D]).astype(BF)

    loads[3].wait()
    loads[4].wait()
    coarse = dot(mg[...], wm[...]).astype(BF)
    for q in range(4):
        qq = (0, 2, 1, 3)[q]
        wide = dot(coarse, we[:, D * qq : D * qq + D])
        hat, scale = norm_parts(wide)
        dy = cq[q].astype(F32) * eg_ref[...]
        dw[:, D * qq : D * qq + D] = norm_back(hat, scale, dy).astype(BF)
    d_coarse = dot_nt(dw[...], we[...]).astype(BF)
    mg[...] = dot_nt(d_coarse, wm[...]).astype(BF)

    for r in range(QROWS // 32):
        rows = slice(32 * r, 32 * r + 32)
        average, scale = merge_stats(rows)
        sum_dy = jnp.zeros((32, 1), F32)
        sum_dyh = jnp.zeros((32, 1), F32)
        for q in range(4):
            hat = (fq[q, rows, :].astype(F32) - average) * scale
            dy = mg[rows, D * q : D * q + D].astype(F32) * mg_ref[:, D * q : D * q + D]
            sum_dy = sum_dy + jnp.sum(dy, axis=-1, keepdims=True)
            sum_dyh = sum_dyh + jnp.sum(dy * hat, axis=-1, keepdims=True)
        mean_dy = sum_dy * (1.0 / (4 * D))
        mean_dyh = sum_dyh * (1.0 / (4 * D))
        for q in range(4):
            hat = (fq[q, rows, :].astype(F32) - average) * scale
            dy = mg[rows, D * q : D * q + D].astype(F32) * mg_ref[:, D * q : D * q + D]
            back = (scale * (dy - mean_dy - hat * mean_dyh)).astype(BF)
            gq[q, rows, :] = (cq[q, rows, :].astype(F32) + back.astype(F32)).astype(BF)

    for k in range(4):
        parts = jnp.concatenate([gq[q, 32 * k : 32 * k + 64, :] for q in range(4)], axis=0)
        gn[WRP * k : WRP * k + WRP, :] = dot(pi_ref[k], parts).astype(BF)

    stores = []

    def store(src, dst):
        copy = pltpu.make_async_copy(src, dst, sems.at[9 + len(stores)])
        copy.start()
        stores.append(copy)

    def put(j, block):
        columns = slice(D * j, D * j + D)
        pairs = block.astype(BF).reshape(mine.shape[0], 2, mine.shape[1], D)
        even, odd = pairs[:, 0], pairs[:, 1]
        mine[:, :, columns] = jnp.where(core == 0, even, odd)
        other[:, :, columns] = jnp.where(core == 0, odd, even)
        store(other.at[:, :, columns], other_hbm.at[:, :, columns])
        store(mine.at[:, :, columns], mine_hbm.at[:, :, columns])

    for load in loads[5:]:
        load.wait()
    inner = slice(0, 4 * WRP)
    store(gn, gn_hbm)
    put(3, dot_tn(attn[inner, :], gn[...]))

    for j in range(2):
        columns = slice(256 * j, 256 * j + 256)
        d_attn[:, columns] = dot_nt(gn[...], wproj[columns, :]).astype(BF)

    def backward(k, carry):
        start = pl.multiple_of(k * WRP, 16)
        masked = masked_at(k)
        parts = [heads(qkv, start, w, hp, low) for w, hp in UNITS]
        do = [
            stacked(d_attn[win, 128 * hp : 128 * hp + 128], low)
            for (_, hp), (_, _, _, win) in zip(UNITS, parts)
        ]
        dp = [dot_nt(v2, d)[:WIN] for d, (_, _, v2, _) in zip(do, parts)]
        p = [probs[k, 4 * w + hp] for w, hp in UNITS]
        dv = [dot(padded_keys(v), d) for v, d in zip(p, do)]
        dp = [v.astype(BF).astype(F32) for v in dp]
        inner = [jnp.sum(a * b, axis=0, keepdims=True) for a, b in zip(dp, p)]
        ds = [b * (a - c) for a, b, c in zip(dp, p, inner)]
        ds = [padded_keys(jnp.where(masked, 0.0, v)) for v in ds]
        dk = [dot(v, qs) for v, (qs, _, _, _) in zip(ds, parts)]
        dq = [over_queries(v, k2, first_lane) * 0.125 for v, (_, k2, _, _) in zip(ds, parts)]
        for i, ((_, hp), (_, _, _, win)) in enumerate(zip(UNITS, parts)):
            lanes = slice(128 * hp, 128 * hp + 128)
            dqkv[win, lanes] = dq[i].astype(BF)
            dqkv[win, D + lanes.start : D + lanes.stop] = dk[i].astype(BF)
            dqkv[win, 2 * D + lanes.start : 2 * D + lanes.stop] = dv[i].astype(BF)
        return carry

    lax.fori_loop(0, 4, backward, 0)
    store(dqkv, dqkv_hbm)
    for j in range(3):
        put(j, dot_tn(normed[inner, :], dqkv[:, D * j : D * j + D]))
    for copy in stores:
        copy.wait()


def finish_kernel(early_ref, late_ref, gn_ref, dqkv_ref, wqkv_ref, ng_ref, px_ref, pxt_ref, dwork_ref, d_normed):
    for j in range(2):
        columns = slice(256 * j, 256 * j + 256)
        d_normed[:, columns] = dot_nt(dqkv_ref[...], wqkv_ref[columns, :]).astype(BF)

    for k in range(4):
        rows = slice(WRP * k, WRP * k + WRP)
        x = early_ref[WR * k : WR * k + WR, :] if k < EARLY else late_ref[:WR, :]
        hat, scale = norm_parts(dot(px_ref[...], x))
        back = norm_back(hat, scale, d_normed[rows, :].astype(F32) * ng_ref[...])
        d_work = (gn_ref[rows, :].astype(F32) + back).astype(BF)
        dwork_ref[WR * k : WR * k + WR, :] = dot(pxt_ref[...], d_work).astype(BF)


VMEM = pl.BlockSpec(memory_space=pltpu.VMEM)
HBM = pl.BlockSpec(memory_space=pl.ANY)


def start_early(x, norm_gain, w_qkv, w_proj):
    rows = EARLY * WRP
    shapes = [((rows, D), BF), ((rows, 3 * D), BF), ((EARLY, HEADS, WIN, 256), F32), ((rows, D), BF), ((rows, D), BF)]
    return pl.pallas_call(
        early_kernel,
        out_shape=tuple(jax.ShapeDtypeStruct(*one) for one in shapes),
        in_specs=[VMEM] * 5,
        out_specs=(VMEM,) * 5,
        scratch_shapes=[pltpu.VMEM((rows, D), BF)],
        compiler_params=pltpu.CompilerParams(vmem_limit_bytes=SMALL_GRANT),
        cost_estimate=pl.CostEstimate(flops=1_400_000_000, bytes_accessed=8_000_000, transcendentals=0),
        name="block_early",
    )(x, jnp.asarray(to_windows()), norm_gain[None], w_qkv, w_proj)


def compute(tiles, lats, early, x, c, norm_gain, w_qkv, w_proj, merge_gain, w_merge, w_expand, expand_gain):
    bf = lambda *shape: pltpu.VMEM(shape, BF)
    share = (tiles, D // (2 * tiles), 4 * D)
    return pl.pallas_call(
        functools.partial(kernel, lats),
        out_shape=tuple(
            jax.ShapeDtypeStruct(shape, BF) for shape in (share, share, (4 * WRP, D), (4 * WRP, 3 * D))
        ),
        in_specs=[VMEM] * 10 + [HBM] * 9,
        out_specs=(HBM,) * 4,
        scratch_shapes=[
            bf(D, 3 * D), bf(D, D), bf(4 * D, 2 * D), bf(2 * D, 4 * D),
            bf((NWR - EARLY) * WRP, D), bf(NWR * WRP, D), bf(NWR * WRP, 3 * D), pltpu.VMEM((NWR, HEADS, WIN, 256), F32),
            bf(NWR * WRP, D), bf(NWR * WRP, D),
            bf(4, QROWS, D), bf(4, QROWS, D), bf(QROWS, 4 * D), bf(QROWS, 4 * D), bf(4, QROWS, D),
            bf(4 * WRP, D), bf(4 * WRP, D), bf(4 * WRP, 3 * D), bf(*share), bf(*share),
            pltpu.SemaphoreType.DMA((19,)),
        ],
        compiler_params=pltpu.CompilerParams(vmem_limit_bytes=GRANT),
        cost_estimate=pl.CostEstimate(flops=7_000_000_000, bytes_accessed=18_000_000, transcendentals=0),
        name="block",
    )(
        x, c, norm_gain[None], merge_gain[None], expand_gain[None],
        jnp.asarray(to_windows()), jnp.asarray(fine_offsets()),
        jnp.asarray(cot_offsets(4, 48)), jnp.asarray(cot_offsets(1, 16)), jnp.asarray(from_offsets()),
        w_qkv, w_proj, w_merge, w_expand, *early,
    )


def finish_tokens(x_early, x, gn, dqkv, w_qkv, norm_gain):
    return pl.pallas_call(
        finish_kernel,
        out_shape=jax.ShapeDtypeStruct((4 * WR, D), BF),
        in_specs=[VMEM] * 8,
        out_specs=VMEM,
        scratch_shapes=[pltpu.VMEM((4 * WRP, D), BF)],
        compiler_params=pltpu.CompilerParams(vmem_limit_bytes=SMALL_GRANT),
        cost_estimate=pl.CostEstimate(flops=1_200_000_000, bytes_accessed=6_000_000, transcendentals=0),
        name="block_tokens",
    )(x_early, x, gn, dqkv, w_qkv, norm_gain[None], jnp.asarray(to_windows()), jnp.asarray(to_windows().T))


def copies_kernel(in_ref, out_ref):
    for j in range(in_ref.shape[2] // D):
        columns = slice(D * j, D * j + D)
        total = in_ref[0, :, columns].astype(F32)
        for i in range(1, in_ref.shape[0]):
            total = total + in_ref[i, :, columns].astype(F32)
        for i in range(out_ref.shape[0]):
            out_ref[i, :, columns] = total.astype(BF)


def share_copies(spread, copies):
    return pl.pallas_call(
        copies_kernel,
        out_shape=jax.ShapeDtypeStruct((copies,) + spread.shape[1:], BF),
        in_specs=[VMEM],
        out_specs=VMEM,
        compiler_params=pltpu.CompilerParams(vmem_limit_bytes=SMALL_GRANT),
        name="share_copies",
    )(spread)


def body(tokens, cotangent, norm_gain, w_qkv, w_proj, merge_gain, w_merge, w_expand, expand_gain):
    lats, tiles, cores = lax.axis_size("lat"), lax.axis_size("tile"), lax.axis_size("core")
    lons = tiles * cores
    names = ("lat", "tile", "core")

    def moved(value, dlat, dlon):
        pairs = []
        for a in range(lats):
            for b in range(lons):
                pairs.append((a * lons + b, ((a + dlat) % lats) * lons + (b + dlon) % lons))
        return lax.ppermute(value, names, pairs)

    beside = moved(jnp.concatenate([tokens[:, :SLON], cotangent[:, :SLON]], axis=0), 0, -1)
    work = jnp.concatenate([tokens[:, SLON:], beside[:ROWS]], axis=1)
    cwork = jnp.concatenate([cotangent[:, SLON:], beside[ROWS:]], axis=1)
    first, last = SLAT, ROWS - SLAT
    below = moved(jnp.concatenate([work[:9], cwork[:4]], axis=0), -1, 0)
    above = moved(work[last:], 1, 0)

    x_early = work[first:last].reshape(EARLY * WR, D)
    early = start_early(x_early, norm_gain, w_qkv, w_proj)
    early, below, above = lax.optimization_barrier((early, below, above))

    x = jnp.concatenate([work[last:], below[:9], above, work[:first]], axis=0)
    x = x.reshape((NWR - EARLY) * WR, D)
    c = jnp.concatenate([cwork, below[9:]], axis=0).reshape(CROWS * COLS, D)

    mine, other, gn, dqkv = compute(
        tiles, lats, early, x, c, norm_gain, w_qkv, w_proj, merge_gain, w_merge, w_expand, expand_gain
    )

    theirs = lax.ppermute(other, "core", [(i, cores - 1 - i) for i in range(cores)])
    pair, dqkv = lax.optimization_barrier((mine + theirs, dqkv))
    spread = lax.all_to_all(pair, "tile", 0, 0, tiled=True)

    d_work = finish_tokens(x_early, x, gn, dqkv, w_qkv, norm_gain).reshape(ROWS, COLS, D)
    last_row, last_col = ROWS - SLAT, COLS - SLON
    spread, d_work = lax.optimization_barrier((spread, d_work))
    rows = moved(d_work[last_row:, :last_col], 1, 0)
    corner = moved(d_work[last_row:, last_col:], 1, 1)
    columns = moved(d_work[:last_row, last_col:], 0, 1)
    top = jnp.concatenate([corner, rows], axis=1)
    rest = jnp.concatenate([columns, d_work[:last_row, :last_col]], axis=1)
    d_tokens = jnp.concatenate([top, rest], axis=0)

    gathered = lax.all_to_all(share_copies(spread, lats), "lat", 0, 0, tiled=True)
    grad_qkv = jnp.sum(gathered[:, :, : 3 * D].astype(F32), axis=0)
    grad_proj = jnp.sum(gathered[:, :, 3 * D :].astype(F32), axis=0)
    return (d_tokens, grad_qkv, grad_proj)


def solution(mesh):
    lats, lons = mesh.shape["lat"], mesh.shape["lon"]
    fine_mesh = Mesh(mesh.devices.reshape(lats, lons // 2, 2), ("lat", "tile", "core"))
    lon = ("tile", "core")
    in_specs = (P("lat", lon, None), P("lat", lon, None), P(), P(), P(), P(), P(), P(), P())
    out_specs = (P("lat", lon, None), P(lon, None), P(lon, None))
    return jax.shard_map(body, mesh=fine_mesh, in_specs=in_specs, out_specs=out_specs, check_vma=False)
```

```python
import functools

import jax
import jax.numpy as jnp
import numpy as np
from jax import lax
from jax.experimental import pallas as pl
from jax.experimental.pallas import tpu as pltpu
from jax.sharding import Mesh, PartitionSpec as P

HEADS = 8
HEAD = 64
WLAT = 6
WLON = 12
SLAT = 3
SLON = 6
D = 512
ROWS = 24
COLS = 24
WR = WLAT * COLS
WIN = WLAT * WLON
WP = 80
WRP = 2 * WP
NWR = 6
EARLY = 3
CROWS = 28
PAIRS = 13
QROWS = 160

EPSILON = 1e-05
GRANT = 40 * 1024 * 1024
SMALL_GRANT = 24 * 1024 * 1024
MASKED = -1000000000.0
OUTSIDE = -3.0e38
BF = jnp.bfloat16
F32 = jnp.float32


def window_row(i, col):
    return (col // WLON) * WP + i * WLON + col % WLON


def to_windows(upward=False):
    out = np.zeros((WRP, WR), np.float32)
    for t in range(WR):
        i = t // COLS
        out[window_row(WLAT - 1 - i if upward else i, t % COLS), t] = 1
    return out.astype(jnp.bfloat16)


def cot_offsets(pairs, padded):
    out = np.zeros((4 * padded, pairs * 2 * COLS), np.float32)
    for a in range(pairs):
        for rp in range(2):
            for col in range(COLS):
                q = (col % 2) * 2 + rp
                out[q * padded + a * 12 + col // 2, (2 * a + rp) * COLS + col] = 1
    return out.astype(jnp.bfloat16)


FINE_PARTS = ((0, 0), (0, 1), (0, 2), (1, 2), (1, 3), (2, 3), (2, 4), (3, 4), (3, 5))


def fine_offsets():
    out = np.zeros((len(FINE_PARTS), 4 * 48, WRP), np.float32)
    for n, (g, k) in enumerate(FINE_PARTS):
        padded = 48 if g < 3 else 16
        for a in range(4 * g, min(4 * g + 4, PAIRS)):
            for rp in range(2):
                f = 5 + 2 * a + rp
                if f // WLAT != k:
                    continue
                i = f % WLAT if k > 0 else WLAT - 1 - f
                for col in range(COLS):
                    q = (col % 2) * 2 + rp
                    out[n, q * padded + (a - 4 * g) * 12 + col // 2, window_row(i, col)] = 1
    return out.astype(jnp.bfloat16)


def from_offsets():
    out = np.zeros((4, WRP, 256), np.float32)
    for k in range(1, 5):
        for t in range(WR):
            f = WLAT * k + t // COLS
            col = t % COLS
            a, rp = divmod(f - 5, 2)
            q = (col % 2) * 2 + rp
            out[k - 1, window_row(t // COLS, col), q * 64 + 12 * a + col // 2 - 32 * (k - 1)] = 1
    return out.astype(jnp.bfloat16)


def dot(a, b):
    return jnp.dot(a, b, preferred_element_type=F32)


def dot_nt(a, b):
    return lax.dot_general(a, b, (((1,), (1,)), ((), ())), preferred_element_type=F32)


def dot_tn(a, b):
    return lax.dot_general(a, b, (((0,), (0,)), ((), ())), preferred_element_type=F32)


def norm_parts(values):
    average = jnp.mean(values, axis=-1, keepdims=True)
    centred = values - average
    spread = jnp.mean(centred * centred, axis=-1, keepdims=True)
    scale = lax.rsqrt(spread + EPSILON)
    return centred * scale, scale


def norm_back(hat, scale, dy):
    mean_dy = jnp.mean(dy, axis=-1, keepdims=True)
    mean_dyh = jnp.mean(dy * hat, axis=-1, keepdims=True)
    return scale * (dy - mean_dy - hat * mean_dyh)


def stacked(two, low):
    gap = jnp.zeros((128 - WP, 2 * HEAD), BF)
    return jnp.concatenate([two * low, gap, two * (1 - low), gap], axis=0)


def over_queries(keys_by_queries, rows, first_lane):
    both = [dot_tn(keys_by_queries[:, 128 * i : 128 * i + WP], rows) for i in range(2)]
    return jnp.where(first_lane, both[0], both[1])


def padded_keys(values):
    return jnp.concatenate([values, jnp.zeros((WP - WIN, 256), F32)], axis=0).astype(BF)


UNITS = [(w, hp) for w in range(2) for hp in range(HEADS // 2)]


def lane_halves():
    first_lane = lax.broadcasted_iota(jnp.int32, (1, 2 * HEAD), 1) < HEAD
    return first_lane, first_lane.astype(F32).astype(BF)


def rows_of(start, size):
    return pl.ds(pl.multiple_of(start, 16), size)


def heads(qkv, start, w, hp, low):
    win = rows_of(start + WP * w, WP)
    q2 = qkv[win, 128 * hp : 128 * hp + 128]
    k2 = qkv[win, D + 128 * hp : D + 128 * hp + 128]
    v2 = qkv[win, 2 * D + 128 * hp : 2 * D + 128 * hp + 128]
    return stacked(q2 * 0.125, low), k2, v2, win


def first_row_attention(qkv, attn, start, masked):
    win, top = slice(start, start + WP), slice(start, start + 16)
    head = lax.broadcasted_iota(jnp.int32, (1, D), 1) // HEAD
    mine = [head == h for h in range(HEADS)]
    q = qkv[top, :D] * 0.125
    qs = jnp.concatenate([q * m.astype(F32).astype(BF) for m in mine], axis=0)
    s = dot_nt(qkv[win, D : 2 * D], qs)[:WIN]
    if masked is not None:
        s = jnp.where(masked, MASKED, s)
    e = jnp.exp(s - jnp.max(s, axis=0, keepdims=True))
    p = e * (1.0 / jnp.sum(e, axis=0, keepdims=True))
    p = jnp.concatenate([p, jnp.zeros((WP - WIN, p.shape[1]), F32)], axis=0).astype(BF)
    o = dot_tn(p, qkv[win, 2 * D :])
    total = jnp.zeros((16, D), F32)
    for h, m in enumerate(mine):
        total = jnp.where(m, o[16 * h : 16 * h + 16], total)
    attn[top, :] = total.astype(BF)
    attn[start + 16 : start + WP, :] = jnp.zeros((WP - 16, D), BF)


def attention(first, whole, mask, edge, x_ref, px, gain, wqkv, wproj, xw, normed, qkv, probs, attn, fine):
    first_lane, low = lane_halves()
    base = WRP * first
    span = slice(base, base + 3 * WRP)
    for k in range(3):
        rows = slice(base + WRP * k, base + WRP * k + WRP)
        x = dot(px[k][...], x_ref[WR * k : WR * k + WR, :])
        xw[WRP * k : WRP * k + WRP, :] = x.astype(BF)
        hat, _ = norm_parts(x)
        normed[rows, :] = (hat * gain[...]).astype(BF)
    for j in range(6):
        columns = slice(256 * j, 256 * j + 256)
        qkv[span, columns] = dot(normed[span, :], wqkv[:, columns]).astype(BF)

    def window_row(k, carry):
        masked = None if mask is None else mask(k)
        parts = [heads(qkv, k * WRP, w, hp, low) for w, hp in UNITS]
        s = [dot_nt(k2, qs)[:WIN] for qs, k2, _, _ in parts]
        if masked is not None:
            s = [jnp.where(masked, MASKED, v) for v in s]
        top = [jnp.max(v, axis=0, keepdims=True) for v in s]
        e = [jnp.exp(v - t) for v, t in zip(s, top)]
        total = [jnp.sum(v, axis=0, keepdims=True) for v in e]
        p = [v * (1.0 / t) for v, t in zip(e, total)]
        for (w, hp), v in zip(UNITS, p):
            probs[k, 4 * w + hp] = v
        o = [over_queries(padded_keys(v), v2, first_lane) for v, (_, _, v2, _) in zip(p, parts)]
        for (w, hp), v, (_, _, _, win) in zip(UNITS, o, parts):
            attn[win, 128 * hp : 128 * hp + 128] = v.astype(BF)
        return carry

    lax.fori_loop(first, first + whole, window_row, 0)
    for k in range(first + whole, first + 3):
        for w in range(2):
            first_row_attention(qkv, attn, WRP * k + WP * w, edge if k == NWR - 1 else None)
    for j in range(2):
        columns = slice(256 * j, 256 * j + 256)
        fine[span, columns] = (
            xw[:, columns].astype(F32) + dot(attn[span, :], wproj[:, columns])
        ).astype(BF)


def early_kernel(x_ref, px_ref, ng_ref, wqkv, wproj, normed, qkv, probs, attn, fine, xw):
    attention(0, 3, None, None, x_ref, (px_ref,) * 3, ng_ref, wqkv, wproj, xw, normed, qkv, probs, attn, fine)


def kernel(
    lat_size, x_ref, c_ref, ng_ref, mg_ref, eg_ref, px_ref, pxu_ref, pf_ref, pc_ref, pc3_ref, pi_ref,
    wqkv_hbm, wproj_hbm, wm_hbm, we_hbm, normed_hbm, qkv_hbm, probs_hbm, attn_hbm, fine_hbm,
    mine_hbm, other_hbm, gn_hbm, dqkv_hbm,
    wqkv, wproj, wm, we, xw, normed, qkv, probs, attn, fine, fq, cq, mg, dw, gq, gn, d_attn, dqkv, mine, other, sems,
):
    lat = lax.axis_index("lat")
    core = lax.axis_index("core")
    done = slice(0, EARLY * WRP)
    sources = (
        (wqkv_hbm, wqkv), (wproj_hbm, wproj), (fine_hbm, fine.at[done]), (wm_hbm, wm), (we_hbm, we),
        (probs_hbm, probs.at[0:EARLY]), (qkv_hbm, qkv.at[done]),
        (attn_hbm, attn.at[done]), (normed_hbm, normed.at[done]),
    )
    loads = [pltpu.make_async_copy(src, dst, sems.at[i]) for i, (src, dst) in enumerate(sources)]
    for load in loads:
        load.start()

    key = lax.broadcasted_iota(jnp.int32, (WIN, 256), 0)
    query = lax.broadcasted_iota(jnp.int32, (WIN, 256), 1) % 128
    apart = (key >= WIN // 2) != (query >= WIN // 2)
    first_lane, low = lane_halves()

    def masked_at(k):
        edge = (k == EARLY) & (lat == lat_size - 1)
        return apart & edge

    upper = (key[:, : 16 * HEADS] >= WIN // 2) & (lat == 0)

    loads[0].wait()
    loads[1].wait()
    attention(EARLY, 1, masked_at, upper, x_ref, (px_ref, px_ref, pxu_ref), ng_ref, wqkv, wproj, xw, normed, qkv, probs, attn, fine)
    loads[2].wait()

    for g in range(4):
        n = 48 if g < 3 else 16
        f = sum(
            dot(pf_ref[m, : 4 * n, :], fine[WRP * k : WRP * k + WRP, :])
            for m, (gg, k) in enumerate((g_, (k_ - 1) % NWR) for g_, k_ in FINE_PARTS)
            if gg == g
        ).astype(BF)
        if g < 3:
            c = dot(pc_ref[...], c_ref[48 + 192 * g : 48 + 192 * g + 192, :]).astype(BF)
        else:
            c = dot(pc3_ref[...], c_ref[624:672, :]).astype(BF)
        for q in range(4):
            fq[q, 48 * g : 48 * g + n, :] = f[n * q : n * q + n]
            cq[q, 48 * g : 48 * g + n, :] = c[n * q : n * q + n]

    def merge_stats(rows):
        total = jnp.zeros((32, 1), F32)
        for q in range(4):
            total = total + jnp.sum(fq[q, rows, :].astype(F32), axis=-1, keepdims=True)
        average = total * (1.0 / (4 * D))
        total = jnp.zeros((32, 1), F32)
        for q in range(4):
            centred = fq[q, rows, :].astype(F32) - average
            total = total + jnp.sum(centred * centred, axis=-1, keepdims=True)
        return average, lax.rsqrt(total * (1.0 / (4 * D)) + EPSILON)

    for r in range(QROWS // 32):
        rows = slice(32 * r, 32 * r + 32)
        average, scale = merge_stats(rows)
        for q in range(4):
            hat = (fq[q, rows, :].astype(F32) - average) * scale
            mg[rows, D * q : D * q + D] = (hat * mg_ref[:, D * q : D * q + D]).astype(BF)

    loads[3].wait()
    loads[4].wait()
    coarse = dot(mg[...], wm[...]).astype(BF)
    for q in range(4):
        qq = (0, 2, 1, 3)[q]
        wide = dot(coarse, we[:, D * qq : D * qq + D])
        hat, scale = norm_parts(wide)
        dy = cq[q].astype(F32) * eg_ref[...]
        dw[:, D * qq : D * qq + D] = norm_back(hat, scale, dy).astype(BF)
    d_coarse = dot_nt(dw[...], we[...]).astype(BF)
    mg[...] = dot_nt(d_coarse, wm[...]).astype(BF)

    for r in range(QROWS // 32):
        rows = slice(32 * r, 32 * r + 32)
        average, scale = merge_stats(rows)
        sum_dy = jnp.zeros((32, 1), F32)
        sum_dyh = jnp.zeros((32, 1), F32)
        for q in range(4):
            hat = (fq[q, rows, :].astype(F32) - average) * scale
            dy = mg[rows, D * q : D * q + D].astype(F32) * mg_ref[:, D * q : D * q + D]
            sum_dy = sum_dy + jnp.sum(dy, axis=-1, keepdims=True)
            sum_dyh = sum_dyh + jnp.sum(dy * hat, axis=-1, keepdims=True)
        mean_dy = sum_dy * (1.0 / (4 * D))
        mean_dyh = sum_dyh * (1.0 / (4 * D))
        for q in range(4):
            hat = (fq[q, rows, :].astype(F32) - average) * scale
            dy = mg[rows, D * q : D * q + D].astype(F32) * mg_ref[:, D * q : D * q + D]
            back = (scale * (dy - mean_dy - hat * mean_dyh)).astype(BF)
            gq[q, rows, :] = (cq[q, rows, :].astype(F32) + back.astype(F32)).astype(BF)

    for k in range(4):
        parts = jnp.concatenate([gq[q, 32 * k : 32 * k + 64, :] for q in range(4)], axis=0)
        gn[WRP * k : WRP * k + WRP, :] = dot(pi_ref[k], parts).astype(BF)

    stores = []

    def store(src, dst):
        copy = pltpu.make_async_copy(src, dst, sems.at[9 + len(stores)])
        copy.start()
        stores.append(copy)

    def put(j, block):
        columns = slice(D * j, D * j + D)
        pairs = block.astype(BF).reshape(mine.shape[0], 2, mine.shape[1], D)
        even, odd = pairs[:, 0], pairs[:, 1]
        mine[:, :, columns] = jnp.where(core == 0, even, odd)
        other[:, :, columns] = jnp.where(core == 0, odd, even)
        store(other.at[:, :, columns], other_hbm.at[:, :, columns])
        store(mine.at[:, :, columns], mine_hbm.at[:, :, columns])

    for load in loads[5:]:
        load.wait()
    inner = slice(0, 4 * WRP)
    store(gn, gn_hbm)
    put(3, dot_tn(attn[inner, :], gn[...]))

    for j in range(2):
        columns = slice(256 * j, 256 * j + 256)
        d_attn[:, columns] = dot_nt(gn[...], wproj[columns, :]).astype(BF)

    def backward(k, carry):
        start = pl.multiple_of(k * WRP, 16)
        masked = masked_at(k)
        parts = [heads(qkv, start, w, hp, low) for w, hp in UNITS]
        do = [
            stacked(d_attn[win, 128 * hp : 128 * hp + 128], low)
            for (_, hp), (_, _, _, win) in zip(UNITS, parts)
        ]
        dp = [dot_nt(v2, d)[:WIN] for d, (_, _, v2, _) in zip(do, parts)]
        p = [probs[k, 4 * w + hp] for w, hp in UNITS]
        dv = [dot(padded_keys(v), d) for v, d in zip(p, do)]
        dp = [v.astype(BF).astype(F32) for v in dp]
        inner = [jnp.sum(a * b, axis=0, keepdims=True) for a, b in zip(dp, p)]
        ds = [b * (a - c) for a, b, c in zip(dp, p, inner)]
        ds = [padded_keys(jnp.where(masked, 0.0, v)) for v in ds]
        dk = [dot(v, qs) for v, (qs, _, _, _) in zip(ds, parts)]
        dq = [over_queries(v, k2, first_lane) * 0.125 for v, (_, k2, _, _) in zip(ds, parts)]
        for i, ((_, hp), (_, _, _, win)) in enumerate(zip(UNITS, parts)):
            lanes = slice(128 * hp, 128 * hp + 128)
            dqkv[win, lanes] = dq[i].astype(BF)
            dqkv[win, D + lanes.start : D + lanes.stop] = dk[i].astype(BF)
            dqkv[win, 2 * D + lanes.start : 2 * D + lanes.stop] = dv[i].astype(BF)
        return carry

    lax.fori_loop(0, 4, backward, 0)
    store(dqkv, dqkv_hbm)
    for j in range(3):
        put(j, dot_tn(normed[inner, :], dqkv[:, D * j : D * j + D]))
    for copy in stores:
        copy.wait()


def finish_kernel(early_ref, late_ref, gn_ref, dqkv_ref, wqkv_ref, ng_ref, px_ref, pxt_ref, dwork_ref, d_normed):
    for j in range(2):
        columns = slice(256 * j, 256 * j + 256)
        d_normed[:, columns] = dot_nt(dqkv_ref[...], wqkv_ref[columns, :]).astype(BF)

    for k in range(4):
        rows = slice(WRP * k, WRP * k + WRP)
        x = early_ref[WR * k : WR * k + WR, :] if k < EARLY else late_ref[:WR, :]
        hat, scale = norm_parts(dot(px_ref[...], x))
        back = norm_back(hat, scale, d_normed[rows, :].astype(F32) * ng_ref[...])
        d_work = (gn_ref[rows, :].astype(F32) + back).astype(BF)
        dwork_ref[WR * k : WR * k + WR, :] = dot(pxt_ref[...], d_work).astype(BF)


VMEM = pl.BlockSpec(memory_space=pltpu.VMEM)
HBM = pl.BlockSpec(memory_space=pl.ANY)


def start_early(x, norm_gain, w_qkv, w_proj):
    rows = EARLY * WRP
    shapes = [((rows, D), BF), ((rows, 3 * D), BF), ((EARLY, HEADS, WIN, 256), F32), ((rows, D), BF), ((rows, D), BF)]
    return pl.pallas_call(
        early_kernel,
        out_shape=tuple(jax.ShapeDtypeStruct(*one) for one in shapes),
        in_specs=[VMEM] * 5,
        out_specs=(VMEM,) * 5,
        scratch_shapes=[pltpu.VMEM((rows, D), BF)],
        compiler_params=pltpu.CompilerParams(vmem_limit_bytes=SMALL_GRANT),
        cost_estimate=pl.CostEstimate(flops=1_400_000_000, bytes_accessed=8_000_000, transcendentals=0),
        name="block_early",
    )(x, jnp.asarray(to_windows()), norm_gain[None], w_qkv, w_proj)


def compute(tiles, lats, early, x, c, norm_gain, w_qkv, w_proj, merge_gain, w_merge, w_expand, expand_gain):
    bf = lambda *shape: pltpu.VMEM(shape, BF)
    share = (tiles, D // (2 * tiles), 4 * D)
    return pl.pallas_call(
        functools.partial(kernel, lats),
        out_shape=tuple(
            jax.ShapeDtypeStruct(shape, BF) for shape in (share, share, (4 * WRP, D), (4 * WRP, 3 * D))
        ),
        in_specs=[VMEM] * 11 + [HBM] * 9,
        out_specs=(HBM,) * 4,
        scratch_shapes=[
            bf(D, 3 * D), bf(D, D), bf(4 * D, 2 * D), bf(2 * D, 4 * D),
            bf((NWR - EARLY) * WRP, D), bf(NWR * WRP, D), bf(NWR * WRP, 3 * D), pltpu.VMEM((EARLY + 1, HEADS, WIN, 256), F32),
            bf(NWR * WRP, D), bf(NWR * WRP, D),
            bf(4, QROWS, D), bf(4, QROWS, D), bf(QROWS, 4 * D), bf(QROWS, 4 * D), bf(4, QROWS, D),
            bf(4 * WRP, D), bf(4 * WRP, D), bf(4 * WRP, 3 * D), bf(*share), bf(*share),
            pltpu.SemaphoreType.DMA((19,)),
        ],
        compiler_params=pltpu.CompilerParams(vmem_limit_bytes=GRANT),
        cost_estimate=pl.CostEstimate(flops=7_000_000_000, bytes_accessed=18_000_000, transcendentals=0),
        name="block",
    )(
        x, c, norm_gain[None], merge_gain[None], expand_gain[None],
        jnp.asarray(to_windows()), jnp.asarray(to_windows(True)), jnp.asarray(fine_offsets()),
        jnp.asarray(cot_offsets(4, 48)), jnp.asarray(cot_offsets(1, 16)), jnp.asarray(from_offsets()),
        w_qkv, w_proj, w_merge, w_expand, *early,
    )


def finish_tokens(x_early, x, gn, dqkv, w_qkv, norm_gain):
    return pl.pallas_call(
        finish_kernel,
        out_shape=jax.ShapeDtypeStruct((4 * WR, D), BF),
        in_specs=[VMEM] * 8,
        out_specs=VMEM,
        scratch_shapes=[pltpu.VMEM((4 * WRP, D), BF)],
        compiler_params=pltpu.CompilerParams(vmem_limit_bytes=SMALL_GRANT),
        cost_estimate=pl.CostEstimate(flops=1_200_000_000, bytes_accessed=6_000_000, transcendentals=0),
        name="block_tokens",
    )(x_early, x, gn, dqkv, w_qkv, norm_gain[None], jnp.asarray(to_windows()), jnp.asarray(to_windows().T))


def copies_kernel(in_ref, out_ref):
    for j in range(in_ref.shape[2] // D):
        columns = slice(D * j, D * j + D)
        total = in_ref[0, :, columns].astype(F32)
        for i in range(1, in_ref.shape[0]):
            total = total + in_ref[i, :, columns].astype(F32)
        for i in range(out_ref.shape[0]):
            out_ref[i, :, columns] = total.astype(BF)


def share_copies(spread, copies):
    return pl.pallas_call(
        copies_kernel,
        out_shape=jax.ShapeDtypeStruct((copies,) + spread.shape[1:], BF),
        in_specs=[VMEM],
        out_specs=VMEM,
        compiler_params=pltpu.CompilerParams(vmem_limit_bytes=SMALL_GRANT),
        name="share_copies",
    )(spread)


def body(tokens, cotangent, norm_gain, w_qkv, w_proj, merge_gain, w_merge, w_expand, expand_gain):
    lats, tiles, cores = lax.axis_size("lat"), lax.axis_size("tile"), lax.axis_size("core")
    lons = tiles * cores
    names = ("lat", "tile", "core")

    def moved(value, dlat, dlon):
        pairs = []
        for a in range(lats):
            for b in range(lons):
                pairs.append((a * lons + b, ((a + dlat) % lats) * lons + (b + dlon) % lons))
        return lax.ppermute(value, names, pairs)

    beside = moved(jnp.concatenate([tokens[:, :SLON], cotangent[:, :SLON]], axis=0), 0, -1)
    work = jnp.concatenate([tokens[:, SLON:], beside[:ROWS]], axis=1)
    cwork = jnp.concatenate([cotangent[:, SLON:], beside[ROWS:]], axis=1)
    first, last = SLAT, ROWS - SLAT
    below = moved(jnp.concatenate([work[:9], cwork[:4]], axis=0), -1, 0)
    above = moved(work[last:], 1, 0)

    x_early = work[first:last].reshape(EARLY * WR, D)
    early = start_early(x_early, norm_gain, w_qkv, w_proj)
    early, below, above = lax.optimization_barrier((early, below, above))

    x = jnp.concatenate([work[last:], below[:9], above, work[:first]], axis=0)
    x = x.reshape((NWR - EARLY) * WR, D)
    c = jnp.concatenate([cwork, below[9:]], axis=0).reshape(CROWS * COLS, D)

    mine, other, gn, dqkv = compute(
        tiles, lats, early, x, c, norm_gain, w_qkv, w_proj, merge_gain, w_merge, w_expand, expand_gain
    )

    theirs = lax.ppermute(other, "core", [(i, cores - 1 - i) for i in range(cores)])
    pair, dqkv = lax.optimization_barrier((mine + theirs, dqkv))
    spread = lax.all_to_all(pair, "tile", 0, 0, tiled=True)

    d_work = finish_tokens(x_early, x, gn, dqkv, w_qkv, norm_gain).reshape(ROWS, COLS, D)
    last_row, last_col = ROWS - SLAT, COLS - SLON
    rows = moved(d_work[last_row:, :last_col], 1, 0)
    corner = moved(d_work[last_row:, last_col:], 1, 1)
    edge = d_work[:last_row, last_col:]
    spread, rows, corner, edge = lax.optimization_barrier((spread, rows, corner, edge))
    columns = moved(edge, 0, 1)
    top = jnp.concatenate([corner, rows], axis=1)
    rest = jnp.concatenate([columns, d_work[:last_row, :last_col]], axis=1)
    d_tokens = jnp.concatenate([top, rest], axis=0)

    gathered = lax.all_to_all(share_copies(spread, lats), "lat", 0, 0, tiled=True)
    grad_qkv = jnp.sum(gathered[:, :, : 3 * D].astype(F32), axis=0)
    grad_proj = jnp.sum(gathered[:, :, 3 * D :].astype(F32), axis=0)
    return (d_tokens, grad_qkv, grad_proj)


def solution(mesh):
    lats, lons = mesh.shape["lat"], mesh.shape["lon"]
    fine_mesh = Mesh(mesh.devices.reshape(lats, lons // 2, 2), ("lat", "tile", "core"))
    lon = ("tile", "core")
    in_specs = (P("lat", lon, None), P("lat", lon, None), P(), P(), P(), P(), P(), P(), P())
    out_specs = (P("lat", lon, None), P(lon, None), P(lon, None))
    return jax.shard_map(body, mesh=fine_mesh, in_specs=in_specs, out_specs=out_specs, check_vma=False)
```

```python
import functools

import jax
import jax.numpy as jnp
import numpy as np
from jax import lax
from jax.experimental import pallas as pl
from jax.experimental.pallas import tpu as pltpu
from jax.sharding import Mesh, PartitionSpec as P

HEADS = 8
HEAD = 64
WLAT = 6
WLON = 12
SLAT = 3
SLON = 6
D = 512
ROWS = 24
COLS = 24
WR = WLAT * COLS
WIN = WLAT * WLON
WP = 80
WRP = 2 * WP
NWR = 6
EARLY = 3
CROWS = 28
PAIRS = 13
QROWS = 160

EPSILON = 1e-05
GRANT = 40 * 1024 * 1024
SMALL_GRANT = 24 * 1024 * 1024
MASKED = -1000000000.0
OUTSIDE = -3.0e38
BF = jnp.bfloat16
F32 = jnp.float32


def window_row(i, col):
    return (col // WLON) * WP + i * WLON + col % WLON


def to_windows(upward=False):
    out = np.zeros((WRP, WR), np.float32)
    for t in range(WR):
        i = t // COLS
        out[window_row(WLAT - 1 - i if upward else i, t % COLS), t] = 1
    return out.astype(jnp.bfloat16)


def cot_offsets(pairs, padded):
    out = np.zeros((4 * padded, pairs * 2 * COLS), np.float32)
    for a in range(pairs):
        for rp in range(2):
            for col in range(COLS):
                q = (col % 2) * 2 + rp
                out[q * padded + a * 12 + col // 2, (2 * a + rp) * COLS + col] = 1
    return out.astype(jnp.bfloat16)


FINE_PARTS = ((0, 0), (0, 1), (0, 2), (1, 2), (1, 3), (2, 3), (2, 4), (3, 4), (3, 5))


def fine_offsets():
    out = np.zeros((len(FINE_PARTS), 4 * 48, WRP), np.float32)
    for n, (g, k) in enumerate(FINE_PARTS):
        padded = 48 if g < 3 else 16
        for a in range(4 * g, min(4 * g + 4, PAIRS)):
            for rp in range(2):
                f = 5 + 2 * a + rp
                if f // WLAT != k:
                    continue
                i = f % WLAT if k > 0 else WLAT - 1 - f
                for col in range(COLS):
                    q = (col % 2) * 2 + rp
                    out[n, q * padded + (a - 4 * g) * 12 + col // 2, window_row(i, col)] = 1
    return out.astype(jnp.bfloat16)


def from_offsets():
    out = np.zeros((4, WRP, 256), np.float32)
    for k in range(1, 5):
        for t in range(WR):
            f = WLAT * k + t // COLS
            col = t % COLS
            a, rp = divmod(f - 5, 2)
            q = (col % 2) * 2 + rp
            out[k - 1, window_row(t // COLS, col), q * 64 + 12 * a + col // 2 - 32 * (k - 1)] = 1
    return out.astype(jnp.bfloat16)


def dot(a, b):
    return jnp.dot(a, b, preferred_element_type=F32)


def dot_nt(a, b):
    return lax.dot_general(a, b, (((1,), (1,)), ((), ())), preferred_element_type=F32)


def dot_tn(a, b):
    return lax.dot_general(a, b, (((0,), (0,)), ((), ())), preferred_element_type=F32)


def norm_parts(values):
    average = jnp.mean(values, axis=-1, keepdims=True)
    centred = values - average
    spread = jnp.mean(centred * centred, axis=-1, keepdims=True)
    scale = lax.rsqrt(spread + EPSILON)
    return centred * scale, scale


def norm_back(hat, scale, dy):
    mean_dy = jnp.mean(dy, axis=-1, keepdims=True)
    mean_dyh = jnp.mean(dy * hat, axis=-1, keepdims=True)
    return scale * (dy - mean_dy - hat * mean_dyh)


def stacked(two, low):
    gap = jnp.zeros((128 - WP, 2 * HEAD), BF)
    return jnp.concatenate([two * low, gap, two * (1 - low), gap], axis=0)


def over_queries(keys_by_queries, rows, first_lane):
    both = [dot_tn(keys_by_queries[:, 128 * i : 128 * i + WP], rows) for i in range(2)]
    return jnp.where(first_lane, both[0], both[1])


def padded_keys(values):
    return jnp.concatenate([values, jnp.zeros((WP - WIN, 256), F32)], axis=0).astype(BF)


UNITS = [(w, hp) for w in range(2) for hp in range(HEADS // 2)]


def lane_halves():
    first_lane = lax.broadcasted_iota(jnp.int32, (1, 2 * HEAD), 1) < HEAD
    return first_lane, first_lane.astype(F32).astype(BF)


def rows_of(start, size):
    return pl.ds(pl.multiple_of(start, 16), size)


def heads(qkv, start, w, hp, low):
    win = rows_of(start + WP * w, WP)
    q2 = qkv[win, 128 * hp : 128 * hp + 128]
    k2 = qkv[win, D + 128 * hp : D + 128 * hp + 128]
    v2 = qkv[win, 2 * D + 128 * hp : 2 * D + 128 * hp + 128]
    return stacked(q2 * 0.125, low), k2, v2, win


def first_row_attention(qkv, attn, start, masked):
    win, top = slice(start, start + WP), slice(start, start + 16)
    head = lax.broadcasted_iota(jnp.int32, (1, D), 1) // HEAD
    mine = [head == h for h in range(HEADS)]
    q = qkv[top, :D] * 0.125
    qs = jnp.concatenate([q * m.astype(F32).astype(BF) for m in mine], axis=0)
    s = dot_nt(qkv[win, D : 2 * D], qs)[:WIN]
    if masked is not None:
        s = jnp.where(masked, MASKED, s)
    e = jnp.exp(s - jnp.max(s, axis=0, keepdims=True))
    p = e * (1.0 / jnp.sum(e, axis=0, keepdims=True))
    p = jnp.concatenate([p, jnp.zeros((WP - WIN, p.shape[1]), F32)], axis=0).astype(BF)
    o = dot_tn(p, qkv[win, 2 * D :])
    total = jnp.zeros((16, D), F32)
    for h, m in enumerate(mine):
        total = jnp.where(m, o[16 * h : 16 * h + 16], total)
    attn[top, :] = total.astype(BF)
    attn[start + 16 : start + WP, :] = jnp.zeros((WP - 16, D), BF)


def attention(first, whole, mask, edge, x_ref, px, gain, wqkv, wproj, xw, normed, qkv, probs, attn, fine):
    first_lane, low = lane_halves()
    base = WRP * first
    span = slice(base, base + 3 * WRP)
    for k in range(3):
        rows = slice(base + WRP * k, base + WRP * k + WRP)
        x = dot(px[k][...], x_ref[WR * k : WR * k + WR, :])
        xw[WRP * k : WRP * k + WRP, :] = x.astype(BF)
        hat, _ = norm_parts(x)
        normed[rows, :] = (hat * gain[...]).astype(BF)
    for j in range(6):
        columns = slice(256 * j, 256 * j + 256)
        qkv[span, columns] = dot(normed[span, :], wqkv[:, columns]).astype(BF)

    def window_row(k, carry):
        masked = None if mask is None else mask(k)
        parts = [heads(qkv, k * WRP, w, hp, low) for w, hp in UNITS]
        s = [dot_nt(k2, qs)[:WIN] for qs, k2, _, _ in parts]
        if masked is not None:
            s = [jnp.where(masked, MASKED, v) for v in s]
        top = [jnp.max(v, axis=0, keepdims=True) for v in s]
        e = [jnp.exp(v - t) for v, t in zip(s, top)]
        total = [jnp.sum(v, axis=0, keepdims=True) for v in e]
        p = [v * (1.0 / t) for v, t in zip(e, total)]
        for (w, hp), v in zip(UNITS, p):
            probs[k, 4 * w + hp] = v
        o = [over_queries(padded_keys(v), v2, first_lane) for v, (_, _, v2, _) in zip(p, parts)]
        for (w, hp), v, (_, _, _, win) in zip(UNITS, o, parts):
            attn[win, 128 * hp : 128 * hp + 128] = v.astype(BF)
        return carry

    lax.fori_loop(first, first + whole, window_row, 0)
    for k in range(first + whole, first + 3):
        for w in range(2):
            first_row_attention(qkv, attn, WRP * k + WP * w, edge if k == NWR - 1 else None)
    for j in range(2):
        columns = slice(256 * j, 256 * j + 256)
        fine[span, columns] = (
            xw[:, columns].astype(F32) + dot(attn[span, :], wproj[:, columns])
        ).astype(BF)


def early_kernel(x_ref, px_ref, ng_ref, wqkv, wproj, normed, qkv, probs, attn, fine, xw):
    attention(0, 3, None, None, x_ref, (px_ref,) * 3, ng_ref, wqkv, wproj, xw, normed, qkv, probs, attn, fine)


def kernel(
    lat_size, x_ref, c_ref, ng_ref, mg_ref, eg_ref, px_ref, pxu_ref, pf_ref, pc_ref, pc3_ref, pi_ref,
    wqkv_hbm, wproj_hbm, wm_hbm, we_hbm, normed_hbm, qkv_hbm, probs_hbm, attn_hbm, fine_hbm,
    mine_hbm, other_hbm, gn_hbm, dqkv_hbm,
    wqkv, wproj, wm, we, xw, normed, qkv, probs, attn, fine, fq, hats, cq, mg, dw, gq, gn, d_attn, dqkv, mine, other, sems,
):
    lat = lax.axis_index("lat")
    core = lax.axis_index("core")
    done = slice(0, EARLY * WRP)
    sources = (
        (wqkv_hbm, wqkv), (wproj_hbm, wproj), (fine_hbm, fine.at[done]), (wm_hbm, wm), (we_hbm, we),
        (probs_hbm, probs.at[0:EARLY]), (qkv_hbm, qkv.at[done]),
        (attn_hbm, attn.at[done]), (normed_hbm, normed.at[done]),
    )
    loads = [pltpu.make_async_copy(src, dst, sems.at[i]) for i, (src, dst) in enumerate(sources)]
    for load in loads:
        load.start()

    key = lax.broadcasted_iota(jnp.int32, (WIN, 256), 0)
    query = lax.broadcasted_iota(jnp.int32, (WIN, 256), 1) % 128
    apart = (key >= WIN // 2) != (query >= WIN // 2)
    first_lane, low = lane_halves()

    def masked_at(k):
        edge = (k == EARLY) & (lat == lat_size - 1)
        return apart & edge

    upper = (key[:, : 16 * HEADS] >= WIN // 2) & (lat == 0)

    loads[0].wait()
    loads[1].wait()
    attention(EARLY, 1, masked_at, upper, x_ref, (px_ref, px_ref, pxu_ref), ng_ref, wqkv, wproj, xw, normed, qkv, probs, attn, fine)
    loads[2].wait()

    for g in range(4):
        n = 48 if g < 3 else 16
        f = sum(
            dot(pf_ref[m, : 4 * n, :], fine[WRP * k : WRP * k + WRP, :])
            for m, (gg, k) in enumerate((g_, (k_ - 1) % NWR) for g_, k_ in FINE_PARTS)
            if gg == g
        ).astype(BF)
        if g < 3:
            c = dot(pc_ref[...], c_ref[48 + 192 * g : 48 + 192 * g + 192, :]).astype(BF)
        else:
            c = dot(pc3_ref[...], c_ref[624:672, :]).astype(BF)
        for q in range(4):
            fq[q, 48 * g : 48 * g + n, :] = f[n * q : n * q + n]
            cq[q, 48 * g : 48 * g + n, :] = c[n * q : n * q + n]

    def merge_stats(rows):
        total = jnp.zeros((32, 1), F32)
        for q in range(4):
            total = total + jnp.sum(fq[q, rows, :].astype(F32), axis=-1, keepdims=True)
        average = total * (1.0 / (4 * D))
        total = jnp.zeros((32, 1), F32)
        for q in range(4):
            centred = fq[q, rows, :].astype(F32) - average
            total = total + jnp.sum(centred * centred, axis=-1, keepdims=True)
        return average, lax.rsqrt(total * (1.0 / (4 * D)) + EPSILON)

    scales = []
    for r in range(QROWS // 32):
        rows = slice(32 * r, 32 * r + 32)
        average, scale = merge_stats(rows)
        scales.append(scale)
        for q in range(4):
            hat = (fq[q, rows, :].astype(F32) - average) * scale
            hats[q, rows, :] = hat
            mg[rows, D * q : D * q + D] = (hat * mg_ref[:, D * q : D * q + D]).astype(BF)

    loads[3].wait()
    loads[4].wait()
    coarse = dot(mg[...], wm[...]).astype(BF)
    for q in range(4):
        qq = (0, 2, 1, 3)[q]
        wide = dot(coarse, we[:, D * qq : D * qq + D])
        hat, scale = norm_parts(wide)
        dy = cq[q].astype(F32) * eg_ref[...]
        dw[:, D * qq : D * qq + D] = norm_back(hat, scale, dy).astype(BF)
    d_coarse = dot_nt(dw[...], we[...]).astype(BF)
    mg[...] = dot_nt(d_coarse, wm[...]).astype(BF)

    for r in range(QROWS // 32):
        rows = slice(32 * r, 32 * r + 32)
        scale = scales[r]
        sum_dy = jnp.zeros((32, 1), F32)
        sum_dyh = jnp.zeros((32, 1), F32)
        for q in range(4):
            hat = hats[q, rows, :]
            dy = mg[rows, D * q : D * q + D].astype(F32) * mg_ref[:, D * q : D * q + D]
            sum_dy = sum_dy + jnp.sum(dy, axis=-1, keepdims=True)
            sum_dyh = sum_dyh + jnp.sum(dy * hat, axis=-1, keepdims=True)
        mean_dy = sum_dy * (1.0 / (4 * D))
        mean_dyh = sum_dyh * (1.0 / (4 * D))
        for q in range(4):
            hat = hats[q, rows, :]
            dy = mg[rows, D * q : D * q + D].astype(F32) * mg_ref[:, D * q : D * q + D]
            back = (scale * (dy - mean_dy - hat * mean_dyh)).astype(BF)
            gq[q, rows, :] = (cq[q, rows, :].astype(F32) + back.astype(F32)).astype(BF)

    for k in range(4):
        parts = jnp.concatenate([gq[q, 32 * k : 32 * k + 64, :] for q in range(4)], axis=0)
        gn[WRP * k : WRP * k + WRP, :] = dot(pi_ref[k], parts).astype(BF)

    stores = []

    def store(src, dst):
        copy = pltpu.make_async_copy(src, dst, sems.at[9 + len(stores)])
        copy.start()
        stores.append(copy)

    def put(j, block):
        columns = slice(D * j, D * j + D)
        pairs = block.astype(BF).reshape(mine.shape[0], 2, mine.shape[1], D)
        even, odd = pairs[:, 0], pairs[:, 1]
        mine[:, :, columns] = jnp.where(core == 0, even, odd)
        other[:, :, columns] = jnp.where(core == 0, odd, even)
        store(other.at[:, :, columns], other_hbm.at[:, :, columns])
        store(mine.at[:, :, columns], mine_hbm.at[:, :, columns])

    for load in loads[5:]:
        load.wait()
    inner = slice(0, 4 * WRP)
    store(gn, gn_hbm)
    put(3, dot_tn(attn[inner, :], gn[...]))

    for j in range(2):
        columns = slice(256 * j, 256 * j + 256)
        d_attn[:, columns] = dot_nt(gn[...], wproj[columns, :]).astype(BF)

    def backward(k, carry):
        start = pl.multiple_of(k * WRP, 16)
        masked = masked_at(k)
        parts = [heads(qkv, start, w, hp, low) for w, hp in UNITS]
        do = [
            stacked(d_attn[win, 128 * hp : 128 * hp + 128], low)
            for (_, hp), (_, _, _, win) in zip(UNITS, parts)
        ]
        dp = [dot_nt(v2, d)[:WIN] for d, (_, _, v2, _) in zip(do, parts)]
        p = [probs[k, 4 * w + hp] for w, hp in UNITS]
        dv = [dot(padded_keys(v), d) for v, d in zip(p, do)]
        dp = [v.astype(BF).astype(F32) for v in dp]
        inner = [jnp.sum(a * b, axis=0, keepdims=True) for a, b in zip(dp, p)]
        ds = [b * (a - c) for a, b, c in zip(dp, p, inner)]
        ds = [padded_keys(jnp.where(masked, 0.0, v)) for v in ds]
        dk = [dot(v, qs) for v, (qs, _, _, _) in zip(ds, parts)]
        dq = [over_queries(v, k2, first_lane) * 0.125 for v, (_, k2, _, _) in zip(ds, parts)]
        for i, ((_, hp), (_, _, _, win)) in enumerate(zip(UNITS, parts)):
            lanes = slice(128 * hp, 128 * hp + 128)
            dqkv[win, lanes] = dq[i].astype(BF)
            dqkv[win, D + lanes.start : D + lanes.stop] = dk[i].astype(BF)
            dqkv[win, 2 * D + lanes.start : 2 * D + lanes.stop] = dv[i].astype(BF)
        return carry

    lax.fori_loop(0, 4, backward, 0, unroll=2)
    store(dqkv, dqkv_hbm)
    for j in range(3):
        put(j, dot_tn(normed[inner, :], dqkv[:, D * j : D * j + D]))
    for copy in stores:
        copy.wait()


def finish_kernel(early_ref, late_ref, gn_ref, dqkv_ref, wqkv_ref, ng_ref, px_ref, pxt_ref, dwork_ref, d_normed):
    for j in range(2):
        columns = slice(256 * j, 256 * j + 256)
        d_normed[:, columns] = dot_nt(dqkv_ref[...], wqkv_ref[columns, :]).astype(BF)

    for k in range(4):
        rows = slice(WRP * k, WRP * k + WRP)
        x = early_ref[WR * k : WR * k + WR, :] if k < EARLY else late_ref[:WR, :]
        hat, scale = norm_parts(dot(px_ref[...], x))
        back = norm_back(hat, scale, d_normed[rows, :].astype(F32) * ng_ref[...])
        d_work = (gn_ref[rows, :].astype(F32) + back).astype(BF)
        dwork_ref[WR * k : WR * k + WR, :] = dot(pxt_ref[...], d_work).astype(BF)


VMEM = pl.BlockSpec(memory_space=pltpu.VMEM)
HBM = pl.BlockSpec(memory_space=pl.ANY)


def start_early(x, norm_gain, w_qkv, w_proj):
    rows = EARLY * WRP
    shapes = [((rows, D), BF), ((rows, 3 * D), BF), ((EARLY, HEADS, WIN, 256), F32), ((rows, D), BF), ((rows, D), BF)]
    return pl.pallas_call(
        early_kernel,
        out_shape=tuple(jax.ShapeDtypeStruct(*one) for one in shapes),
        in_specs=[VMEM] * 5,
        out_specs=(VMEM,) * 5,
        scratch_shapes=[pltpu.VMEM((rows, D), BF)],
        compiler_params=pltpu.CompilerParams(vmem_limit_bytes=SMALL_GRANT),
        cost_estimate=pl.CostEstimate(flops=1_400_000_000, bytes_accessed=8_000_000, transcendentals=0),
        name="block_early",
    )(x, jnp.asarray(to_windows()), norm_gain[None], w_qkv, w_proj)


def compute(tiles, lats, early, x, c, norm_gain, w_qkv, w_proj, merge_gain, w_merge, w_expand, expand_gain):
    bf = lambda *shape: pltpu.VMEM(shape, BF)
    share = (tiles, D // (2 * tiles), 4 * D)
    return pl.pallas_call(
        functools.partial(kernel, lats),
        out_shape=tuple(
            jax.ShapeDtypeStruct(shape, BF) for shape in (share, share, (4 * WRP, D), (4 * WRP, 3 * D))
        ),
        in_specs=[VMEM] * 11 + [HBM] * 9,
        out_specs=(HBM,) * 4,
        scratch_shapes=[
            bf(D, 3 * D), bf(D, D), bf(4 * D, 2 * D), bf(2 * D, 4 * D),
            bf((NWR - EARLY) * WRP, D), bf(NWR * WRP, D), bf(NWR * WRP, 3 * D), pltpu.VMEM((EARLY + 1, HEADS, WIN, 256), F32),
            bf(NWR * WRP, D), bf(NWR * WRP, D),
            bf(4, QROWS, D), pltpu.VMEM((4, QROWS, D), F32), bf(4, QROWS, D), bf(QROWS, 4 * D), bf(QROWS, 4 * D), bf(4, QROWS, D),
            bf(4 * WRP, D), bf(4 * WRP, D), bf(4 * WRP, 3 * D), bf(*share), bf(*share),
            pltpu.SemaphoreType.DMA((19,)),
        ],
        compiler_params=pltpu.CompilerParams(vmem_limit_bytes=GRANT),
        cost_estimate=pl.CostEstimate(flops=7_000_000_000, bytes_accessed=18_000_000, transcendentals=0),
        name="block",
    )(
        x, c, norm_gain[None], merge_gain[None], expand_gain[None],
        jnp.asarray(to_windows()), jnp.asarray(to_windows(True)), jnp.asarray(fine_offsets()),
        jnp.asarray(cot_offsets(4, 48)), jnp.asarray(cot_offsets(1, 16)), jnp.asarray(from_offsets()),
        w_qkv, w_proj, w_merge, w_expand, *early,
    )


def finish_tokens(x_early, x, gn, dqkv, w_qkv, norm_gain):
    return pl.pallas_call(
        finish_kernel,
        out_shape=jax.ShapeDtypeStruct((4 * WR, D), BF),
        in_specs=[VMEM] * 8,
        out_specs=VMEM,
        scratch_shapes=[pltpu.VMEM((4 * WRP, D), BF)],
        compiler_params=pltpu.CompilerParams(vmem_limit_bytes=SMALL_GRANT),
        cost_estimate=pl.CostEstimate(flops=1_200_000_000, bytes_accessed=6_000_000, transcendentals=0),
        name="block_tokens",
    )(x_early, x, gn, dqkv, w_qkv, norm_gain[None], jnp.asarray(to_windows()), jnp.asarray(to_windows().T))


def copies_kernel(in_ref, out_ref):
    for j in range(in_ref.shape[2] // D):
        columns = slice(D * j, D * j + D)
        total = in_ref[0, :, columns].astype(F32)
        for i in range(1, in_ref.shape[0]):
            total = total + in_ref[i, :, columns].astype(F32)
        for i in range(out_ref.shape[0]):
            out_ref[i, :, columns] = total.astype(BF)


def share_copies(spread, copies):
    return pl.pallas_call(
        copies_kernel,
        out_shape=jax.ShapeDtypeStruct((copies,) + spread.shape[1:], BF),
        in_specs=[VMEM],
        out_specs=VMEM,
        compiler_params=pltpu.CompilerParams(vmem_limit_bytes=SMALL_GRANT),
        name="share_copies",
    )(spread)


def body(tokens, cotangent, norm_gain, w_qkv, w_proj, merge_gain, w_merge, w_expand, expand_gain):
    lats, tiles, cores = lax.axis_size("lat"), lax.axis_size("tile"), lax.axis_size("core")
    lons = tiles * cores
    names = ("lat", "tile", "core")

    def moved(value, dlat, dlon):
        pairs = []
        for a in range(lats):
            for b in range(lons):
                pairs.append((a * lons + b, ((a + dlat) % lats) * lons + (b + dlon) % lons))
        return lax.ppermute(value, names, pairs)

    beside = moved(jnp.concatenate([tokens[:, :SLON], cotangent[:, :SLON]], axis=0), 0, -1)
    work = jnp.concatenate([tokens[:, SLON:], beside[:ROWS]], axis=1)
    cwork = jnp.concatenate([cotangent[:, SLON:], beside[ROWS:]], axis=1)
    first, last = SLAT, ROWS - SLAT
    below = moved(jnp.concatenate([work[:9], cwork[:4]], axis=0), -1, 0)
    above = moved(work[last:], 1, 0)

    x_early = work[first:last].reshape(EARLY * WR, D)
    early = start_early(x_early, norm_gain, w_qkv, w_proj)
    early, below, above = lax.optimization_barrier((early, below, above))

    x = jnp.concatenate([work[last:], below[:9], above, work[:first]], axis=0)
    x = x.reshape((NWR - EARLY) * WR, D)
    c = jnp.concatenate([cwork, below[9:]], axis=0).reshape(CROWS * COLS, D)

    mine, other, gn, dqkv = compute(
        tiles, lats, early, x, c, norm_gain, w_qkv, w_proj, merge_gain, w_merge, w_expand, expand_gain
    )

    theirs = lax.ppermute(other, "core", [(i, cores - 1 - i) for i in range(cores)])
    pair, dqkv = lax.optimization_barrier((mine + theirs, dqkv))
    spread = lax.all_to_all(pair, "tile", 0, 0, tiled=True)

    d_work = finish_tokens(x_early, x, gn, dqkv, w_qkv, norm_gain).reshape(ROWS, COLS, D)
    last_row, last_col = ROWS - SLAT, COLS - SLON
    rows = moved(d_work[last_row:, :last_col], 1, 0)
    corner = moved(d_work[last_row:, last_col:], 1, 1)
    edge = d_work[:last_row, last_col:]
    spread, rows, corner, edge = lax.optimization_barrier((spread, rows, corner, edge))
    columns = moved(edge, 0, 1)
    top = jnp.concatenate([corner, rows], axis=1)
    rest = jnp.concatenate([columns, d_work[:last_row, :last_col]], axis=1)
    d_tokens = jnp.concatenate([top, rest], axis=0)

    gathered = lax.all_to_all(share_copies(spread, lats), "lat", 0, 0, tiled=True)
    grad_qkv = jnp.sum(gathered[:, :, : 3 * D].astype(F32), axis=0)
    grad_proj = jnp.sum(gathered[:, :, 3 * D :].astype(F32), axis=0)
    return (d_tokens, grad_qkv, grad_proj)


def solution(mesh):
    lats, lons = mesh.shape["lat"], mesh.shape["lon"]
    fine_mesh = Mesh(mesh.devices.reshape(lats, lons // 2, 2), ("lat", "tile", "core"))
    lon = ("tile", "core")
    in_specs = (P("lat", lon, None), P("lat", lon, None), P(), P(), P(), P(), P(), P(), P())
    out_specs = (P("lat", lon, None), P(lon, None), P(lon, None))
    return jax.shard_map(body, mesh=fine_mesh, in_specs=in_specs, out_specs=out_specs, check_vma=False)
```

```python
import functools

import jax
import jax.numpy as jnp
import numpy as np
from jax import lax
from jax.experimental import pallas as pl
from jax.experimental.pallas import tpu as pltpu
from jax.sharding import Mesh, PartitionSpec as P

HEADS = 8
HEAD = 64
WLAT = 6
WLON = 12
SLAT = 3
SLON = 6
D = 512
ROWS = 24
COLS = 24
WR = WLAT * COLS
WIN = WLAT * WLON
WP = 80
WRP = 2 * WP
NWR = 6
EARLY = 3
CROWS = 28
PAIRS = 13
QROWS = 160

EPSILON = 1e-05
GRANT = 40 * 1024 * 1024
SMALL_GRANT = 24 * 1024 * 1024
MASKED = -1000000000.0
OUTSIDE = -3.0e38
BF = jnp.bfloat16
F32 = jnp.float32


def window_row(i, col):
    return (col // WLON) * WP + i * WLON + col % WLON


def to_windows(upward=False):
    out = np.zeros((WRP, WR), np.float32)
    for t in range(WR):
        i = t // COLS
        out[window_row(WLAT - 1 - i if upward else i, t % COLS), t] = 1
    return out.astype(jnp.bfloat16)


def cot_offsets(pairs, padded):
    out = np.zeros((4 * padded, pairs * 2 * COLS), np.float32)
    for a in range(pairs):
        for rp in range(2):
            for col in range(COLS):
                q = (col % 2) * 2 + rp
                out[q * padded + a * 12 + col // 2, (2 * a + rp) * COLS + col] = 1
    return out.astype(jnp.bfloat16)


FINE_PARTS = ((0, 0), (0, 1), (0, 2), (1, 2), (1, 3), (2, 3), (2, 4), (3, 4), (3, 5))


def fine_offsets():
    out = np.zeros((len(FINE_PARTS), 4 * 48, WRP), np.float32)
    for n, (g, k) in enumerate(FINE_PARTS):
        padded = 48 if g < 3 else 16
        for a in range(4 * g, min(4 * g + 4, PAIRS)):
            for rp in range(2):
                f = 5 + 2 * a + rp
                if f // WLAT != k:
                    continue
                i = f % WLAT if k > 0 else WLAT - 1 - f
                for col in range(COLS):
                    q = (col % 2) * 2 + rp
                    out[n, q * padded + (a - 4 * g) * 12 + col // 2, window_row(i, col)] = 1
    return out.astype(jnp.bfloat16)


def from_offsets():
    out = np.zeros((4, WRP, 256), np.float32)
    for k in range(1, 5):
        for t in range(WR):
            f = WLAT * k + t // COLS
            col = t % COLS
            a, rp = divmod(f - 5, 2)
            q = (col % 2) * 2 + rp
            out[k - 1, window_row(t // COLS, col), q * 64 + 12 * a + col // 2 - 32 * (k - 1)] = 1
    return out.astype(jnp.bfloat16)


def dot(a, b):
    return jnp.dot(a, b, preferred_element_type=F32)


def dot_nt(a, b):
    return lax.dot_general(a, b, (((1,), (1,)), ((), ())), preferred_element_type=F32)


def dot_tn(a, b):
    return lax.dot_general(a, b, (((0,), (0,)), ((), ())), preferred_element_type=F32)


def norm_parts(values):
    average = jnp.mean(values, axis=-1, keepdims=True)
    centred = values - average
    spread = jnp.mean(centred * centred, axis=-1, keepdims=True)
    scale = lax.rsqrt(spread + EPSILON)
    return centred * scale, scale


def norm_back(hat, scale, dy):
    mean_dy = jnp.mean(dy, axis=-1, keepdims=True)
    mean_dyh = jnp.mean(dy * hat, axis=-1, keepdims=True)
    return scale * (dy - mean_dy - hat * mean_dyh)


def stacked(two, low):
    gap = jnp.zeros((128 - WP, 2 * HEAD), BF)
    return jnp.concatenate([two * low, gap, two * (1 - low), gap], axis=0)


def over_queries(keys_by_queries, rows, first_lane):
    both = [dot_tn(keys_by_queries[:, 128 * i : 128 * i + WP], rows) for i in range(2)]
    return jnp.where(first_lane, both[0], both[1])


def padded_keys(values):
    return jnp.concatenate([values, jnp.zeros((WP - WIN, 256), F32)], axis=0).astype(BF)


UNITS = [(w, hp) for w in range(2) for hp in range(HEADS // 2)]


def lane_halves():
    first_lane = lax.broadcasted_iota(jnp.int32, (1, 2 * HEAD), 1) < HEAD
    return first_lane, first_lane.astype(F32).astype(BF)


def rows_of(start, size):
    return pl.ds(pl.multiple_of(start, 16), size)


def heads(qkv, start, w, hp, low):
    win = rows_of(start + WP * w, WP)
    q2 = qkv[win, 128 * hp : 128 * hp + 128]
    k2 = qkv[win, D + 128 * hp : D + 128 * hp + 128]
    v2 = qkv[win, 2 * D + 128 * hp : 2 * D + 128 * hp + 128]
    return stacked(q2 * 0.125, low), k2, v2, win


def first_row_attention(qkv, attn, start, masked):
    win, top = slice(start, start + WP), slice(start, start + 16)
    head = lax.broadcasted_iota(jnp.int32, (1, D), 1) // HEAD
    mine = [head == h for h in range(HEADS)]
    q = qkv[top, :D] * 0.125
    qs = jnp.concatenate([q * m.astype(F32).astype(BF) for m in mine], axis=0)
    s = dot_nt(qkv[win, D : 2 * D], qs)[:WIN]
    if masked is not None:
        s = jnp.where(masked, MASKED, s)
    e = jnp.exp(s - jnp.max(s, axis=0, keepdims=True))
    p = e * (1.0 / jnp.sum(e, axis=0, keepdims=True))
    p = jnp.concatenate([p, jnp.zeros((WP - WIN, p.shape[1]), F32)], axis=0).astype(BF)
    o = dot_tn(p, qkv[win, 2 * D :])
    total = jnp.zeros((16, D), F32)
    for h, m in enumerate(mine):
        total = jnp.where(m, o[16 * h : 16 * h + 16], total)
    attn[top, :] = total.astype(BF)
    attn[start + 16 : start + WP, :] = jnp.zeros((WP - 16, D), BF)


def attention(first, whole, mask, edge, x_ref, px, gain, wqkv, wproj, xw, normed, qkv, probs, attn, fine):
    first_lane, low = lane_halves()
    base = WRP * first
    span = slice(base, base + 3 * WRP)
    for k in range(3):
        rows = slice(base + WRP * k, base + WRP * k + WRP)
        x = dot(px[k][...], x_ref[WR * k : WR * k + WR, :])
        xw[WRP * k : WRP * k + WRP, :] = x.astype(BF)
        hat, _ = norm_parts(x)
        normed[rows, :] = (hat * gain[...]).astype(BF)
    for j in range(6):
        columns = slice(256 * j, 256 * j + 256)
        qkv[span, columns] = dot(normed[span, :], wqkv[:, columns]).astype(BF)

    def window_row(k, carry):
        masked = None if mask is None else mask(k)
        parts = [heads(qkv, k * WRP, w, hp, low) for w, hp in UNITS]
        s = [dot_nt(k2, qs)[:WIN] for qs, k2, _, _ in parts]
        if masked is not None:
            s = [jnp.where(masked, MASKED, v) for v in s]
        top = [jnp.max(v, axis=0, keepdims=True) for v in s]
        e = [jnp.exp(v - t) for v, t in zip(s, top)]
        total = [jnp.sum(v, axis=0, keepdims=True) for v in e]
        p = [v * (1.0 / t) for v, t in zip(e, total)]
        for (w, hp), v in zip(UNITS, p):
            probs[k, 4 * w + hp] = v
        o = [over_queries(padded_keys(v), v2, first_lane) for v, (_, _, v2, _) in zip(p, parts)]
        for (w, hp), v, (_, _, _, win) in zip(UNITS, o, parts):
            attn[win, 128 * hp : 128 * hp + 128] = v.astype(BF)
        return carry

    lax.fori_loop(first, first + whole, window_row, 0)
    for k in range(first + whole, first + 3):
        for w in range(2):
            first_row_attention(qkv, attn, WRP * k + WP * w, edge if k == NWR - 1 else None)
    for j in range(2):
        columns = slice(256 * j, 256 * j + 256)
        fine[span, columns] = (
            xw[:, columns].astype(F32) + dot(attn[span, :], wproj[:, columns])
        ).astype(BF)


def early_kernel(x_ref, px_ref, ng_ref, wqkv, wproj, normed, qkv, probs, attn, fine, xw):
    attention(0, 3, None, None, x_ref, (px_ref,) * 3, ng_ref, wqkv, wproj, xw, normed, qkv, probs, attn, fine)


def kernel(
    lat_size, x_ref, c_ref, ng_ref, mg_ref, eg_ref, px_ref, pxu_ref, pf_ref, pc_ref, pc3_ref, pi_ref,
    wqkv_hbm, wproj_hbm, wm_hbm, we_hbm, normed_hbm, qkv_hbm, probs_hbm, attn_hbm, fine_hbm,
    mine_hbm, other_hbm, gn_hbm, dqkv_hbm,
    wqkv, wproj, wm, we, xw, normed, qkv, probs, attn, fine, fq, hats, cq, mg, dw, gq, gn, d_attn, dqkv, mine, other, sems,
):
    lat = lax.axis_index("lat")
    core = lax.axis_index("core")
    done = slice(0, EARLY * WRP)
    sources = (
        (wqkv_hbm, wqkv), (wproj_hbm, wproj), (fine_hbm, fine.at[done]), (wm_hbm, wm), (we_hbm, we),
        (probs_hbm, probs.at[0:EARLY]), (qkv_hbm, qkv.at[done]),
        (attn_hbm, attn.at[done]), (normed_hbm, normed.at[done]),
    )
    loads = [pltpu.make_async_copy(src, dst, sems.at[i]) for i, (src, dst) in enumerate(sources)]
    for load in loads:
        load.start()

    key = lax.broadcasted_iota(jnp.int32, (WIN, 256), 0)
    query = lax.broadcasted_iota(jnp.int32, (WIN, 256), 1) % 128
    apart = (key >= WIN // 2) != (query >= WIN // 2)
    first_lane, low = lane_halves()

    def masked_at(k):
        edge = (k == EARLY) & (lat == lat_size - 1)
        return apart & edge

    upper = (key[:, : 16 * HEADS] >= WIN // 2) & (lat == 0)

    loads[0].wait()
    loads[1].wait()
    attention(EARLY, 1, masked_at, upper, x_ref, (px_ref, px_ref, pxu_ref), ng_ref, wqkv, wproj, xw, normed, qkv, probs, attn, fine)
    loads[2].wait()

    for g in range(4):
        n = 48 if g < 3 else 16
        f = sum(
            dot(pf_ref[m, : 4 * n, :], fine[WRP * k : WRP * k + WRP, :])
            for m, (gg, k) in enumerate((g_, (k_ - 1) % NWR) for g_, k_ in FINE_PARTS)
            if gg == g
        ).astype(BF)
        if g < 3:
            c = dot(pc_ref[...], c_ref[48 + 192 * g : 48 + 192 * g + 192, :]).astype(BF)
        else:
            c = dot(pc3_ref[...], c_ref[624:672, :]).astype(BF)
        for q in range(4):
            fq[q, 48 * g : 48 * g + n, :] = f[n * q : n * q + n]
            cq[q, 48 * g : 48 * g + n, :] = c[n * q : n * q + n]

    def merge_stats(rows):
        total = jnp.zeros((32, 1), F32)
        for q in range(4):
            total = total + jnp.sum(fq[q, rows, :].astype(F32), axis=-1, keepdims=True)
        average = total * (1.0 / (4 * D))
        total = jnp.zeros((32, 1), F32)
        for q in range(4):
            centred = fq[q, rows, :].astype(F32) - average
            total = total + jnp.sum(centred * centred, axis=-1, keepdims=True)
        return average, lax.rsqrt(total * (1.0 / (4 * D)) + EPSILON)

    scales = []
    for r in range(QROWS // 32):
        rows = slice(32 * r, 32 * r + 32)
        average, scale = merge_stats(rows)
        scales.append(scale)
        for q in range(4):
            hat = (fq[q, rows, :].astype(F32) - average) * scale
            hats[q, rows, :] = hat
            mg[rows, D * q : D * q + D] = (hat * mg_ref[:, D * q : D * q + D]).astype(BF)

    loads[3].wait()
    loads[4].wait()
    coarse = dot(mg[...], wm[...]).astype(BF)
    for q in range(4):
        qq = (0, 2, 1, 3)[q]
        wide = dot(coarse, we[:, D * qq : D * qq + D])
        hat, scale = norm_parts(wide)
        dy = cq[q].astype(F32) * eg_ref[...]
        dw[:, D * qq : D * qq + D] = norm_back(hat, scale, dy).astype(BF)
    d_coarse = dot_nt(dw[...], we[...]).astype(BF)
    mg[...] = dot_nt(d_coarse, wm[...]).astype(BF)

    for r in range(QROWS // 32):
        rows = slice(32 * r, 32 * r + 32)
        scale = scales[r]
        sum_dy = jnp.zeros((32, 1), F32)
        sum_dyh = jnp.zeros((32, 1), F32)
        for q in range(4):
            hat = hats[q, rows, :]
            dy = mg[rows, D * q : D * q + D].astype(F32) * mg_ref[:, D * q : D * q + D]
            sum_dy = sum_dy + jnp.sum(dy, axis=-1, keepdims=True)
            sum_dyh = sum_dyh + jnp.sum(dy * hat, axis=-1, keepdims=True)
        mean_dy = sum_dy * (1.0 / (4 * D))
        mean_dyh = sum_dyh * (1.0 / (4 * D))
        for q in range(4):
            hat = hats[q, rows, :]
            dy = mg[rows, D * q : D * q + D].astype(F32) * mg_ref[:, D * q : D * q + D]
            back = (scale * (dy - mean_dy - hat * mean_dyh)).astype(BF)
            gq[q, rows, :] = (cq[q, rows, :].astype(F32) + back.astype(F32)).astype(BF)

    for k in range(4):
        parts = jnp.concatenate([gq[q, 32 * k : 32 * k + 64, :] for q in range(4)], axis=0)
        gn[WRP * k : WRP * k + WRP, :] = dot(pi_ref[k], parts).astype(BF)

    stores = []

    def store(src, dst):
        copy = pltpu.make_async_copy(src, dst, sems.at[9 + len(stores)])
        copy.start()
        stores.append(copy)

    def put(j, block):
        columns = slice(D * j, D * j + D)
        pairs = block.astype(BF).reshape(mine.shape[0], 2, mine.shape[1], D)
        even, odd = pairs[:, 0], pairs[:, 1]
        mine[:, :, columns] = jnp.where(core == 0, even, odd)
        other[:, :, columns] = jnp.where(core == 0, odd, even)
        store(other.at[:, :, columns], other_hbm.at[:, :, columns])
        store(mine.at[:, :, columns], mine_hbm.at[:, :, columns])

    for load in loads[5:]:
        load.wait()
    inner = slice(0, 4 * WRP)
    store(gn, gn_hbm)
    put(3, dot_tn(attn[inner, :], gn[...]))

    for j in range(2):
        columns = slice(256 * j, 256 * j + 256)
        d_attn[:, columns] = dot_nt(gn[...], wproj[columns, :]).astype(BF)

    def backward(k, carry):
        start = pl.multiple_of(k * WRP, 16)
        masked = masked_at(k)
        parts = [heads(qkv, start, w, hp, low) for w, hp in UNITS]
        do = [
            stacked(d_attn[win, 128 * hp : 128 * hp + 128], low)
            for (_, hp), (_, _, _, win) in zip(UNITS, parts)
        ]
        dp = [dot_nt(v2, d)[:WIN] for d, (_, _, v2, _) in zip(do, parts)]
        p = [probs[k, 4 * w + hp] for w, hp in UNITS]
        dv = [dot(padded_keys(v), d) for v, d in zip(p, do)]
        dp = [v.astype(BF).astype(F32) for v in dp]
        inner = [jnp.sum(a * b, axis=0, keepdims=True) for a, b in zip(dp, p)]
        ds = [b * (a - c) for a, b, c in zip(dp, p, inner)]
        ds = [padded_keys(jnp.where(masked, 0.0, v)) for v in ds]
        dk = [dot(v, qs) for v, (qs, _, _, _) in zip(ds, parts)]
        dq = [over_queries(v, k2, first_lane) * 0.125 for v, (_, k2, _, _) in zip(ds, parts)]
        for i, ((_, hp), (_, _, _, win)) in enumerate(zip(UNITS, parts)):
            lanes = slice(128 * hp, 128 * hp + 128)
            dqkv[win, lanes] = dq[i].astype(BF)
            dqkv[win, D + lanes.start : D + lanes.stop] = dk[i].astype(BF)
            dqkv[win, 2 * D + lanes.start : 2 * D + lanes.stop] = dv[i].astype(BF)
        return carry

    lax.fori_loop(0, 4, backward, 0, unroll=2)
    store(dqkv, dqkv_hbm)
    for j in range(3):
        put(j, dot_tn(normed[inner, :], dqkv[:, D * j : D * j + D]))
    for copy in stores:
        copy.wait()


def finish_kernel(early_ref, late_ref, gn_ref, dqkv_ref, wqkv_ref, ng_ref, px_ref, pxt_ref, dwork_ref, d_normed):
    for j in range(2):
        columns = slice(256 * j, 256 * j + 256)
        d_normed[:, columns] = dot_nt(dqkv_ref[...], wqkv_ref[columns, :]).astype(BF)

    for k in range(4):
        rows = slice(WRP * k, WRP * k + WRP)
        x = early_ref[WR * k : WR * k + WR, :] if k < EARLY else late_ref[:WR, :]
        hat, scale = norm_parts(dot(px_ref[...], x))
        back = norm_back(hat, scale, d_normed[rows, :].astype(F32) * ng_ref[...])
        d_work = (gn_ref[rows, :].astype(F32) + back).astype(BF)
        dwork_ref[WR * k : WR * k + WR, :] = dot(pxt_ref[...], d_work).astype(BF)


VMEM = pl.BlockSpec(memory_space=pltpu.VMEM)
HBM = pl.BlockSpec(memory_space=pl.ANY)


def start_early(x, norm_gain, w_qkv, w_proj):
    rows = EARLY * WRP
    shapes = [((rows, D), BF), ((rows, 3 * D), BF), ((EARLY, HEADS, WIN, 256), F32), ((rows, D), BF), ((rows, D), BF)]
    return pl.pallas_call(
        early_kernel,
        out_shape=tuple(jax.ShapeDtypeStruct(*one) for one in shapes),
        in_specs=[VMEM] * 5,
        out_specs=(VMEM,) * 5,
        scratch_shapes=[pltpu.VMEM((rows, D), BF)],
        compiler_params=pltpu.CompilerParams(vmem_limit_bytes=SMALL_GRANT),
        cost_estimate=pl.CostEstimate(flops=1_400_000_000, bytes_accessed=8_000_000, transcendentals=0),
        name="block_early",
    )(x, jnp.asarray(to_windows()), norm_gain[None], w_qkv, w_proj)


def compute(tiles, lats, early, x, c, norm_gain, w_qkv, w_proj, merge_gain, w_merge, w_expand, expand_gain):
    bf = lambda *shape: pltpu.VMEM(shape, BF)
    share = (tiles, D // (2 * tiles), 4 * D)
    return pl.pallas_call(
        functools.partial(kernel, lats),
        out_shape=tuple(
            jax.ShapeDtypeStruct(shape, BF) for shape in (share, share, (4 * WRP, D), (4 * WRP, 3 * D))
        ),
        in_specs=[VMEM] * 11 + [HBM] * 9,
        out_specs=(HBM,) * 4,
        scratch_shapes=[
            bf(D, 3 * D), bf(D, D), bf(4 * D, 2 * D), bf(2 * D, 4 * D),
            bf((NWR - EARLY) * WRP, D), bf(NWR * WRP, D), bf(NWR * WRP, 3 * D), pltpu.VMEM((EARLY + 1, HEADS, WIN, 256), F32),
            bf(NWR * WRP, D), bf(NWR * WRP, D),
            bf(4, QROWS, D), pltpu.VMEM((4, QROWS, D), F32), bf(4, QROWS, D), bf(QROWS, 4 * D), bf(QROWS, 4 * D), bf(4, QROWS, D),
            bf(4 * WRP, D), bf(4 * WRP, D), bf(4 * WRP, 3 * D), bf(*share), bf(*share),
            pltpu.SemaphoreType.DMA((19,)),
        ],
        compiler_params=pltpu.CompilerParams(vmem_limit_bytes=GRANT),
        cost_estimate=pl.CostEstimate(flops=7_000_000_000, bytes_accessed=18_000_000, transcendentals=0),
        name="block",
    )(
        x, c, norm_gain[None], merge_gain[None], expand_gain[None],
        jnp.asarray(to_windows()), jnp.asarray(to_windows(True)), jnp.asarray(fine_offsets()),
        jnp.asarray(cot_offsets(4, 48)), jnp.asarray(cot_offsets(1, 16)), jnp.asarray(from_offsets()),
        w_qkv, w_proj, w_merge, w_expand, *early,
    )


def finish_tokens(x_early, x, gn, dqkv, w_qkv, norm_gain):
    return pl.pallas_call(
        finish_kernel,
        out_shape=jax.ShapeDtypeStruct((4 * WR, D), BF),
        in_specs=[VMEM] * 8,
        out_specs=VMEM,
        scratch_shapes=[pltpu.VMEM((4 * WRP, D), BF)],
        compiler_params=pltpu.CompilerParams(vmem_limit_bytes=SMALL_GRANT),
        cost_estimate=pl.CostEstimate(flops=1_200_000_000, bytes_accessed=6_000_000, transcendentals=0),
        name="block_tokens",
    )(x_early, x, gn, dqkv, w_qkv, norm_gain[None], jnp.asarray(to_windows()), jnp.asarray(to_windows().T))


def add_kernel(a_ref, b_ref, out_ref):
    out_ref[...] = a_ref[...] + b_ref[...]


def pair_sum(a, b):
    return pl.pallas_call(
        add_kernel,
        out_shape=jax.ShapeDtypeStruct(a.shape, BF),
        in_specs=[VMEM, VMEM],
        out_specs=VMEM,
        compiler_params=pltpu.CompilerParams(vmem_limit_bytes=SMALL_GRANT),
        name="pair_sum",
    )(a, b)


def total_kernel(in_ref, qkv_ref, proj_ref):
    for j in range(4):
        columns = slice(D * j, D * j + D)
        total = in_ref[0, :, columns].astype(F32)
        for i in range(1, in_ref.shape[0]):
            total = total + in_ref[i, :, columns].astype(F32)
        if j < 3:
            qkv_ref[:, columns] = total
        else:
            proj_ref[...] = total


def total_sum(gathered):
    rows = gathered.shape[1]
    return pl.pallas_call(
        total_kernel,
        out_shape=(jax.ShapeDtypeStruct((rows, 3 * D), F32), jax.ShapeDtypeStruct((rows, D), F32)),
        in_specs=[VMEM],
        out_specs=(VMEM, VMEM),
        compiler_params=pltpu.CompilerParams(vmem_limit_bytes=SMALL_GRANT),
        name="total_sum",
    )(gathered)


def copies_kernel(in_ref, out_ref):
    for j in range(in_ref.shape[2] // D):
        columns = slice(D * j, D * j + D)
        total = in_ref[0, :, columns].astype(F32)
        for i in range(1, in_ref.shape[0]):
            total = total + in_ref[i, :, columns].astype(F32)
        for i in range(out_ref.shape[0]):
            out_ref[i, :, columns] = total.astype(BF)


def share_copies(spread, copies):
    return pl.pallas_call(
        copies_kernel,
        out_shape=jax.ShapeDtypeStruct((copies,) + spread.shape[1:], BF),
        in_specs=[VMEM],
        out_specs=VMEM,
        compiler_params=pltpu.CompilerParams(vmem_limit_bytes=SMALL_GRANT),
        name="share_copies",
    )(spread)


def body(tokens, cotangent, norm_gain, w_qkv, w_proj, merge_gain, w_merge, w_expand, expand_gain):
    lats, tiles, cores = lax.axis_size("lat"), lax.axis_size("tile"), lax.axis_size("core")
    lons = tiles * cores
    names = ("lat", "tile", "core")

    def moved(value, dlat, dlon):
        pairs = []
        for a in range(lats):
            for b in range(lons):
                pairs.append((a * lons + b, ((a + dlat) % lats) * lons + (b + dlon) % lons))
        return lax.ppermute(value, names, pairs)

    beside = moved(jnp.concatenate([tokens[:, :SLON], cotangent[:, :SLON]], axis=0), 0, -1)
    work = jnp.concatenate([tokens[:, SLON:], beside[:ROWS]], axis=1)
    cwork = jnp.concatenate([cotangent[:, SLON:], beside[ROWS:]], axis=1)
    first, last = SLAT, ROWS - SLAT
    below = moved(jnp.concatenate([work[:9], cwork[:4]], axis=0), -1, 0)
    above = moved(work[last:], 1, 0)

    x_early = work[first:last].reshape(EARLY * WR, D)
    early = start_early(x_early, norm_gain, w_qkv, w_proj)
    early, below, above = lax.optimization_barrier((early, below, above))

    x = jnp.concatenate([work[last:], below[:9], above, work[:first]], axis=0)
    x = x.reshape((NWR - EARLY) * WR, D)
    c = jnp.concatenate([cwork, below[9:]], axis=0).reshape(CROWS * COLS, D)

    mine, other, gn, dqkv = compute(
        tiles, lats, early, x, c, norm_gain, w_qkv, w_proj, merge_gain, w_merge, w_expand, expand_gain
    )

    theirs = lax.ppermute(other, "core", [(i, cores - 1 - i) for i in range(cores)])
    pair, dqkv = lax.optimization_barrier((pair_sum(mine, theirs), dqkv))
    spread = lax.all_to_all(pair, "tile", 0, 0, tiled=True)

    d_work = finish_tokens(x_early, x, gn, dqkv, w_qkv, norm_gain).reshape(ROWS, COLS, D)
    last_row, last_col = ROWS - SLAT, COLS - SLON
    rows = moved(d_work[last_row:, :last_col], 1, 0)
    corner = moved(d_work[last_row:, last_col:], 1, 1)
    edge = d_work[:last_row, last_col:]
    spread, rows, corner, edge = lax.optimization_barrier((spread, rows, corner, edge))
    columns = moved(edge, 0, 1)
    top = jnp.concatenate([corner, rows], axis=1)
    rest = jnp.concatenate([columns, d_work[:last_row, :last_col]], axis=1)
    d_tokens = jnp.concatenate([top, rest], axis=0)

    gathered = lax.all_to_all(share_copies(spread, lats), "lat", 0, 0, tiled=True)
    grad_qkv, grad_proj = total_sum(gathered)
    return (d_tokens, grad_qkv, grad_proj)


def solution(mesh):
    lats, lons = mesh.shape["lat"], mesh.shape["lon"]
    fine_mesh = Mesh(mesh.devices.reshape(lats, lons // 2, 2), ("lat", "tile", "core"))
    lon = ("tile", "core")
    in_specs = (P("lat", lon, None), P("lat", lon, None), P(), P(), P(), P(), P(), P(), P())
    out_specs = (P("lat", lon, None), P(lon, None), P(lon, None))
    return jax.shard_map(body, mesh=fine_mesh, in_specs=in_specs, out_specs=out_specs, check_vma=False)
```

```python
import functools

import jax
import jax.numpy as jnp
import numpy as np
from jax import lax
from jax.experimental import pallas as pl
from jax.experimental.pallas import tpu as pltpu
from jax.sharding import Mesh, PartitionSpec as P

HEADS = 8
HEAD = 64
WLAT = 6
WLON = 12
SLAT = 3
SLON = 6
D = 512
ROWS = 24
COLS = 24
WR = WLAT * COLS
WIN = WLAT * WLON
WP = 80
WRP = 2 * WP
NWR = 6
EARLY = 3
CROWS = 28
PAIRS = 13
QROWS = 160

EPSILON = 1e-05
GRANT = 40 * 1024 * 1024
SMALL_GRANT = 24 * 1024 * 1024
MASKED = -1000000000.0
OUTSIDE = -3.0e38
BF = jnp.bfloat16
F32 = jnp.float32


def window_row(i, col):
    return (col // WLON) * WP + i * WLON + col % WLON


def to_windows(upward=False):
    out = np.zeros((WRP, WR), np.float32)
    for t in range(WR):
        i = t // COLS
        out[window_row(WLAT - 1 - i if upward else i, t % COLS), t] = 1
    return out.astype(jnp.bfloat16)


def cot_offsets(pairs, padded):
    out = np.zeros((4 * padded, pairs * 2 * COLS), np.float32)
    for a in range(pairs):
        for rp in range(2):
            for col in range(COLS):
                q = (col % 2) * 2 + rp
                out[q * padded + a * 12 + col // 2, (2 * a + rp) * COLS + col] = 1
    return out.astype(jnp.bfloat16)


FINE_PARTS = ((0, 0), (0, 1), (0, 2), (1, 2), (1, 3), (2, 3), (2, 4), (3, 4), (3, 5))


def fine_offsets():
    out = np.zeros((len(FINE_PARTS), 4 * 48, WRP), np.float32)
    for n, (g, k) in enumerate(FINE_PARTS):
        padded = 48 if g < 3 else 16
        for a in range(4 * g, min(4 * g + 4, PAIRS)):
            for rp in range(2):
                f = 5 + 2 * a + rp
                if f // WLAT != k:
                    continue
                i = f % WLAT if k > 0 else WLAT - 1 - f
                for col in range(COLS):
                    q = (col % 2) * 2 + rp
                    out[n, q * padded + (a - 4 * g) * 12 + col // 2, window_row(i, col)] = 1
    return out.astype(jnp.bfloat16)


def from_offsets():
    out = np.zeros((4, WRP, 256), np.float32)
    for k in range(1, 5):
        for t in range(WR):
            f = WLAT * k + t // COLS
            col = t % COLS
            a, rp = divmod(f - 5, 2)
            q = (col % 2) * 2 + rp
            out[k - 1, window_row(t // COLS, col), q * 64 + 12 * a + col // 2 - 32 * (k - 1)] = 1
    return out.astype(jnp.bfloat16)


def dot(a, b):
    return jnp.dot(a, b, preferred_element_type=F32)


def dot_nt(a, b):
    return lax.dot_general(a, b, (((1,), (1,)), ((), ())), preferred_element_type=F32)


def dot_tn(a, b):
    return lax.dot_general(a, b, (((0,), (0,)), ((), ())), preferred_element_type=F32)


def norm_parts(values):
    average = jnp.mean(values, axis=-1, keepdims=True)
    centred = values - average
    spread = jnp.mean(centred * centred, axis=-1, keepdims=True)
    scale = lax.rsqrt(spread + EPSILON)
    return centred * scale, scale


def norm_back(hat, scale, dy):
    mean_dy = jnp.mean(dy, axis=-1, keepdims=True)
    mean_dyh = jnp.mean(dy * hat, axis=-1, keepdims=True)
    return scale * (dy - mean_dy - hat * mean_dyh)


def stacked(two, low):
    gap = jnp.zeros((128 - WP, 2 * HEAD), BF)
    return jnp.concatenate([two * low, gap, two * (1 - low), gap], axis=0)


def over_queries(keys_by_queries, rows, first_lane):
    both = [dot_tn(keys_by_queries[:, 128 * i : 128 * i + WP], rows) for i in range(2)]
    return jnp.where(first_lane, both[0], both[1])


def padded_keys(values):
    return jnp.concatenate([values, jnp.zeros((WP - WIN, 256), F32)], axis=0).astype(BF)


UNITS = [(w, hp) for w in range(2) for hp in range(HEADS // 2)]


def lane_halves():
    first_lane = lax.broadcasted_iota(jnp.int32, (1, 2 * HEAD), 1) < HEAD
    return first_lane, first_lane.astype(F32).astype(BF)


def rows_of(start, size):
    return pl.ds(pl.multiple_of(start, 16), size)


def heads(qkv, start, w, hp, low):
    win = rows_of(start + WP * w, WP)
    q2 = qkv[win, 128 * hp : 128 * hp + 128]
    k2 = qkv[win, D + 128 * hp : D + 128 * hp + 128]
    v2 = qkv[win, 2 * D + 128 * hp : 2 * D + 128 * hp + 128]
    return stacked(q2 * 0.125, low), k2, v2, win


def first_row_attention(qkv, attn, start, masked):
    win, top = slice(start, start + WP), slice(start, start + 16)
    head = lax.broadcasted_iota(jnp.int32, (1, D), 1) // HEAD
    mine = [head == h for h in range(HEADS)]
    q = qkv[top, :D] * 0.125
    qs = jnp.concatenate([q * m.astype(F32).astype(BF) for m in mine], axis=0)
    s = dot_nt(qkv[win, D : 2 * D], qs)[:WIN]
    if masked is not None:
        s = jnp.where(masked, MASKED, s)
    e = jnp.exp(s - jnp.max(s, axis=0, keepdims=True))
    p = e * (1.0 / jnp.sum(e, axis=0, keepdims=True))
    p = jnp.concatenate([p, jnp.zeros((WP - WIN, p.shape[1]), F32)], axis=0).astype(BF)
    o = dot_tn(p, qkv[win, 2 * D :])
    total = jnp.zeros((16, D), F32)
    for h, m in enumerate(mine):
        total = jnp.where(m, o[16 * h : 16 * h + 16], total)
    attn[top, :] = total.astype(BF)
    attn[start + 16 : start + WP, :] = jnp.zeros((WP - 16, D), BF)


def attention(first, whole, mask, edge, x_ref, px, gain, wqkv, wproj, xw, normed, qkv, probs, attn, fine):
    first_lane, low = lane_halves()
    base = WRP * first
    span = slice(base, base + 3 * WRP)
    for k in range(3):
        rows = slice(base + WRP * k, base + WRP * k + WRP)
        x = dot(px[k][...], x_ref[WR * k : WR * k + WR, :])
        xw[WRP * k : WRP * k + WRP, :] = x.astype(BF)
        hat, _ = norm_parts(x)
        normed[rows, :] = (hat * gain[...]).astype(BF)
    for j in range(6):
        columns = slice(256 * j, 256 * j + 256)
        qkv[span, columns] = dot(normed[span, :], wqkv[:, columns]).astype(BF)

    def window_row(k, carry):
        masked = None if mask is None else mask(k)
        parts = [heads(qkv, k * WRP, w, hp, low) for w, hp in UNITS]
        s = [dot_nt(k2, qs)[:WIN] for qs, k2, _, _ in parts]
        if masked is not None:
            s = [jnp.where(masked, MASKED, v) for v in s]
        top = [jnp.max(v, axis=0, keepdims=True) for v in s]
        e = [jnp.exp(v - t) for v, t in zip(s, top)]
        total = [jnp.sum(v, axis=0, keepdims=True) for v in e]
        p = [v * (1.0 / t) for v, t in zip(e, total)]
        for (w, hp), v in zip(UNITS, p):
            probs[k, 4 * w + hp] = v
        o = [over_queries(padded_keys(v), v2, first_lane) for v, (_, _, v2, _) in zip(p, parts)]
        for (w, hp), v, (_, _, _, win) in zip(UNITS, o, parts):
            attn[win, 128 * hp : 128 * hp + 128] = v.astype(BF)
        return carry

    lax.fori_loop(first, first + whole, window_row, 0)
    for k in range(first + whole, first + 3):
        for w in range(2):
            first_row_attention(qkv, attn, WRP * k + WP * w, edge if k == NWR - 1 else None)
    for j in range(2):
        columns = slice(256 * j, 256 * j + 256)
        fine[span, columns] = (
            xw[:, columns].astype(F32) + dot(attn[span, :], wproj[:, columns])
        ).astype(BF)


def early_kernel(x_ref, px_ref, ng_ref, wqkv, wproj, normed, qkv, probs, attn, fine, xw):
    attention(0, 3, None, None, x_ref, (px_ref,) * 3, ng_ref, wqkv, wproj, xw, normed, qkv, probs, attn, fine)


def kernel(
    lat_size, x_ref, c_ref, ng_ref, mg_ref, eg_ref, px_ref, pxu_ref, pf_hbm, pc_ref, pc3_ref, pi_ref,
    wqkv_hbm, wproj_hbm, wm_hbm, we_hbm, normed_hbm, qkv_hbm, probs_hbm, attn_hbm, fine_hbm,
    mine_hbm, other_hbm, gn_hbm, dqkv_hbm,
    pf_ref, wqkv, wproj, wm, we, xw, normed, qkv, probs, attn, fine, fq, hats, cq, mg, dw, gq, gn, d_attn, dqkv, mine, other, sems,
):
    lat = lax.axis_index("lat")
    core = lax.axis_index("core")
    done = slice(0, EARLY * WRP)
    sources = (
        (wqkv_hbm, wqkv), (wproj_hbm, wproj), (fine_hbm, fine.at[done]), (wm_hbm, wm), (we_hbm, we),
        (probs_hbm, probs.at[0:EARLY]), (qkv_hbm, qkv.at[done]),
        (attn_hbm, attn.at[done]), (normed_hbm, normed.at[done]), (pf_hbm, pf_ref),
    )
    loads = [pltpu.make_async_copy(src, dst, sems.at[i]) for i, (src, dst) in enumerate(sources)]
    for load in loads:
        load.start()

    key = lax.broadcasted_iota(jnp.int32, (WIN, 256), 0)
    query = lax.broadcasted_iota(jnp.int32, (WIN, 256), 1) % 128
    apart = (key >= WIN // 2) != (query >= WIN // 2)
    first_lane, low = lane_halves()

    def masked_at(k):
        edge = (k == EARLY) & (lat == lat_size - 1)
        return apart & edge

    upper = (key[:, : 16 * HEADS] >= WIN // 2) & (lat == 0)

    loads[0].wait()
    loads[1].wait()
    attention(EARLY, 1, masked_at, upper, x_ref, (px_ref, px_ref, pxu_ref), ng_ref, wqkv, wproj, xw, normed, qkv, probs, attn, fine)
    loads[2].wait()
    loads[9].wait()

    for g in range(4):
        n = 48 if g < 3 else 16
        f = sum(
            dot(pf_ref[m, : 4 * n, :], fine[WRP * k : WRP * k + WRP, :])
            for m, (gg, k) in enumerate((g_, (k_ - 1) % NWR) for g_, k_ in FINE_PARTS)
            if gg == g
        ).astype(BF)
        if g < 3:
            c = dot(pc_ref[...], c_ref[48 + 192 * g : 48 + 192 * g + 192, :]).astype(BF)
        else:
            c = dot(pc3_ref[...], c_ref[624:672, :]).astype(BF)
        for q in range(4):
            fq[q, 48 * g : 48 * g + n, :] = f[n * q : n * q + n]
            cq[q, 48 * g : 48 * g + n, :] = c[n * q : n * q + n]

    def merge_stats(rows):
        total = jnp.zeros((32, 1), F32)
        for q in range(4):
            total = total + jnp.sum(fq[q, rows, :].astype(F32), axis=-1, keepdims=True)
        average = total * (1.0 / (4 * D))
        total = jnp.zeros((32, 1), F32)
        for q in range(4):
            centred = fq[q, rows, :].astype(F32) - average
            total = total + jnp.sum(centred * centred, axis=-1, keepdims=True)
        return average, lax.rsqrt(total * (1.0 / (4 * D)) + EPSILON)

    scales = []
    for r in range(QROWS // 32):
        rows = slice(32 * r, 32 * r + 32)
        average, scale = merge_stats(rows)
        scales.append(scale)
        for q in range(4):
            hat = (fq[q, rows, :].astype(F32) - average) * scale
            hats[q, rows, :] = hat
            mg[rows, D * q : D * q + D] = (hat * mg_ref[:, D * q : D * q + D]).astype(BF)

    loads[3].wait()
    loads[4].wait()
    coarse = dot(mg[...], wm[...]).astype(BF)
    for q in range(4):
        qq = (0, 2, 1, 3)[q]
        wide = dot(coarse, we[:, D * qq : D * qq + D])
        hat, scale = norm_parts(wide)
        dy = cq[q].astype(F32) * eg_ref[...]
        dw[:, D * qq : D * qq + D] = norm_back(hat, scale, dy).astype(BF)
    d_coarse = dot_nt(dw[...], we[...]).astype(BF)
    mg[...] = dot_nt(d_coarse, wm[...]).astype(BF)

    for r in range(QROWS // 32):
        rows = slice(32 * r, 32 * r + 32)
        scale = scales[r]
        sum_dy = jnp.zeros((32, 1), F32)
        sum_dyh = jnp.zeros((32, 1), F32)
        for q in range(4):
            hat = hats[q, rows, :]
            dy = mg[rows, D * q : D * q + D].astype(F32) * mg_ref[:, D * q : D * q + D]
            sum_dy = sum_dy + jnp.sum(dy, axis=-1, keepdims=True)
            sum_dyh = sum_dyh + jnp.sum(dy * hat, axis=-1, keepdims=True)
        mean_dy = sum_dy * (1.0 / (4 * D))
        mean_dyh = sum_dyh * (1.0 / (4 * D))
        for q in range(4):
            hat = hats[q, rows, :]
            dy = mg[rows, D * q : D * q + D].astype(F32) * mg_ref[:, D * q : D * q + D]
            back = (scale * (dy - mean_dy - hat * mean_dyh)).astype(BF)
            gq[q, rows, :] = (cq[q, rows, :].astype(F32) + back.astype(F32)).astype(BF)

    for k in range(4):
        parts = jnp.concatenate([gq[q, 32 * k : 32 * k + 64, :] for q in range(4)], axis=0)
        gn[WRP * k : WRP * k + WRP, :] = dot(pi_ref[k], parts).astype(BF)

    stores = []

    def store(src, dst):
        copy = pltpu.make_async_copy(src, dst, sems.at[10 + len(stores)])
        copy.start()
        stores.append(copy)

    def put(j, block):
        columns = slice(D * j, D * j + D)
        pairs = block.astype(BF).reshape(mine.shape[0], 2, mine.shape[1], D)
        even, odd = pairs[:, 0], pairs[:, 1]
        mine[:, :, columns] = jnp.where(core == 0, even, odd)
        other[:, :, columns] = jnp.where(core == 0, odd, even)
        store(other.at[:, :, columns], other_hbm.at[:, :, columns])
        store(mine.at[:, :, columns], mine_hbm.at[:, :, columns])

    for load in loads[5:9]:
        load.wait()
    inner = slice(0, 4 * WRP)
    store(gn, gn_hbm)
    put(3, dot_tn(attn[inner, :], gn[...]))

    for j in range(2):
        columns = slice(256 * j, 256 * j + 256)
        d_attn[:, columns] = dot_nt(gn[...], wproj[columns, :]).astype(BF)

    def backward(k, carry):
        start = pl.multiple_of(k * WRP, 16)
        masked = masked_at(k)
        parts = [heads(qkv, start, w, hp, low) for w, hp in UNITS]
        do = [
            stacked(d_attn[win, 128 * hp : 128 * hp + 128], low)
            for (_, hp), (_, _, _, win) in zip(UNITS, parts)
        ]
        dp = [dot_nt(v2, d)[:WIN] for d, (_, _, v2, _) in zip(do, parts)]
        p = [probs[k, 4 * w + hp] for w, hp in UNITS]
        dv = [dot(padded_keys(v), d) for v, d in zip(p, do)]
        dp = [v.astype(BF).astype(F32) for v in dp]
        inner = [jnp.sum(a * b, axis=0, keepdims=True) for a, b in zip(dp, p)]
        ds = [b * (a - c) for a, b, c in zip(dp, p, inner)]
        ds = [padded_keys(jnp.where(masked, 0.0, v)) for v in ds]
        dk = [dot(v, qs) for v, (qs, _, _, _) in zip(ds, parts)]
        dq = [over_queries(v, k2, first_lane) * 0.125 for v, (_, k2, _, _) in zip(ds, parts)]
        for i, ((_, hp), (_, _, _, win)) in enumerate(zip(UNITS, parts)):
            lanes = slice(128 * hp, 128 * hp + 128)
            dqkv[win, lanes] = dq[i].astype(BF)
            dqkv[win, D + lanes.start : D + lanes.stop] = dk[i].astype(BF)
            dqkv[win, 2 * D + lanes.start : 2 * D + lanes.stop] = dv[i].astype(BF)
        return carry

    lax.fori_loop(0, 4, backward, 0, unroll=2)
    store(dqkv, dqkv_hbm)
    for j in range(3):
        put(j, dot_tn(normed[inner, :], dqkv[:, D * j : D * j + D]))
    for copy in stores:
        copy.wait()


def finish_kernel(early_ref, late_ref, gn_ref, dqkv_ref, wqkv_ref, ng_ref, px_ref, pxt_ref, dwork_ref, d_normed):
    for j in range(2):
        columns = slice(256 * j, 256 * j + 256)
        d_normed[:, columns] = dot_nt(dqkv_ref[...], wqkv_ref[columns, :]).astype(BF)

    for k in range(4):
        rows = slice(WRP * k, WRP * k + WRP)
        x = early_ref[WR * k : WR * k + WR, :] if k < EARLY else late_ref[:WR, :]
        hat, scale = norm_parts(dot(px_ref[...], x))
        back = norm_back(hat, scale, d_normed[rows, :].astype(F32) * ng_ref[...])
        d_work = (gn_ref[rows, :].astype(F32) + back).astype(BF)
        dwork_ref[WR * k : WR * k + WR, :] = dot(pxt_ref[...], d_work).astype(BF)


VMEM = pl.BlockSpec(memory_space=pltpu.VMEM)
HBM = pl.BlockSpec(memory_space=pl.ANY)


def start_early(x, norm_gain, w_qkv, w_proj):
    rows = EARLY * WRP
    shapes = [((rows, D), BF), ((rows, 3 * D), BF), ((EARLY, HEADS, WIN, 256), F32), ((rows, D), BF), ((rows, D), BF)]
    return pl.pallas_call(
        early_kernel,
        out_shape=tuple(jax.ShapeDtypeStruct(*one) for one in shapes),
        in_specs=[VMEM] * 5,
        out_specs=(VMEM,) * 5,
        scratch_shapes=[pltpu.VMEM((rows, D), BF)],
        compiler_params=pltpu.CompilerParams(vmem_limit_bytes=SMALL_GRANT),
        cost_estimate=pl.CostEstimate(flops=1_400_000_000, bytes_accessed=8_000_000, transcendentals=0),
        name="block_early",
    )(x, jnp.asarray(to_windows()), norm_gain[None], w_qkv, w_proj)


def compute(tiles, lats, early, x, c, norm_gain, w_qkv, w_proj, merge_gain, w_merge, w_expand, expand_gain):
    bf = lambda *shape: pltpu.VMEM(shape, BF)
    share = (tiles, D // (2 * tiles), 4 * D)
    return pl.pallas_call(
        functools.partial(kernel, lats),
        out_shape=tuple(
            jax.ShapeDtypeStruct(shape, BF) for shape in (share, share, (4 * WRP, D), (4 * WRP, 3 * D))
        ),
        in_specs=[VMEM] * 7 + [HBM] + [VMEM] * 3 + [HBM] * 9,
        out_specs=(HBM,) * 4,
        scratch_shapes=[
            bf(len(FINE_PARTS), 4 * 48, WRP),
            bf(D, 3 * D), bf(D, D), bf(4 * D, 2 * D), bf(2 * D, 4 * D),
            bf((NWR - EARLY) * WRP, D), bf(NWR * WRP, D), bf(NWR * WRP, 3 * D), pltpu.VMEM((EARLY + 1, HEADS, WIN, 256), F32),
            bf(NWR * WRP, D), bf(NWR * WRP, D),
            bf(4, QROWS, D), pltpu.VMEM((4, QROWS, D), F32), bf(4, QROWS, D), bf(QROWS, 4 * D), bf(QROWS, 4 * D), bf(4, QROWS, D),
            bf(4 * WRP, D), bf(4 * WRP, D), bf(4 * WRP, 3 * D), bf(*share), bf(*share),
            pltpu.SemaphoreType.DMA((20,)),
        ],
        compiler_params=pltpu.CompilerParams(vmem_limit_bytes=GRANT),
        cost_estimate=pl.CostEstimate(flops=7_000_000_000, bytes_accessed=18_000_000, transcendentals=0),
        name="block",
    )(
        x, c, norm_gain[None], merge_gain[None], expand_gain[None],
        jnp.asarray(to_windows()), jnp.asarray(to_windows(True)), jnp.asarray(fine_offsets()),
        jnp.asarray(cot_offsets(4, 48)), jnp.asarray(cot_offsets(1, 16)), jnp.asarray(from_offsets()),
        w_qkv, w_proj, w_merge, w_expand, *early,
    )


def finish_tokens(x_early, x, gn, dqkv, w_qkv, norm_gain):
    return pl.pallas_call(
        finish_kernel,
        out_shape=jax.ShapeDtypeStruct((4 * WR, D), BF),
        in_specs=[VMEM] * 8,
        out_specs=VMEM,
        scratch_shapes=[pltpu.VMEM((4 * WRP, D), BF)],
        compiler_params=pltpu.CompilerParams(vmem_limit_bytes=SMALL_GRANT),
        cost_estimate=pl.CostEstimate(flops=1_200_000_000, bytes_accessed=6_000_000, transcendentals=0),
        name="block_tokens",
    )(x_early, x, gn, dqkv, w_qkv, norm_gain[None], jnp.asarray(to_windows()), jnp.asarray(to_windows().T))


def add_kernel(a_ref, b_ref, out_ref):
    out_ref[...] = a_ref[...] + b_ref[...]


def pair_sum(a, b):
    return pl.pallas_call(
        add_kernel,
        out_shape=jax.ShapeDtypeStruct(a.shape, BF),
        in_specs=[VMEM, VMEM],
        out_specs=VMEM,
        compiler_params=pltpu.CompilerParams(vmem_limit_bytes=SMALL_GRANT),
        name="pair_sum",
    )(a, b)


def total_kernel(in_ref, qkv_ref, proj_ref):
    for j in range(4):
        columns = slice(D * j, D * j + D)
        total = in_ref[0, :, columns].astype(F32)
        for i in range(1, in_ref.shape[0]):
            total = total + in_ref[i, :, columns].astype(F32)
        if j < 3:
            qkv_ref[:, columns] = total
        else:
            proj_ref[...] = total


def total_sum(gathered):
    rows = gathered.shape[1]
    return pl.pallas_call(
        total_kernel,
        out_shape=(jax.ShapeDtypeStruct((rows, 3 * D), F32), jax.ShapeDtypeStruct((rows, D), F32)),
        in_specs=[VMEM],
        out_specs=(VMEM, VMEM),
        compiler_params=pltpu.CompilerParams(vmem_limit_bytes=SMALL_GRANT),
        name="total_sum",
    )(gathered)


def copies_kernel(in_ref, out_ref):
    for j in range(in_ref.shape[2] // D):
        columns = slice(D * j, D * j + D)
        total = in_ref[0, :, columns].astype(F32)
        for i in range(1, in_ref.shape[0]):
            total = total + in_ref[i, :, columns].astype(F32)
        for i in range(out_ref.shape[0]):
            out_ref[i, :, columns] = total.astype(BF)


def share_copies(spread, copies):
    return pl.pallas_call(
        copies_kernel,
        out_shape=jax.ShapeDtypeStruct((copies,) + spread.shape[1:], BF),
        in_specs=[VMEM],
        out_specs=VMEM,
        compiler_params=pltpu.CompilerParams(vmem_limit_bytes=SMALL_GRANT),
        name="share_copies",
    )(spread)


def body(tokens, cotangent, norm_gain, w_qkv, w_proj, merge_gain, w_merge, w_expand, expand_gain):
    lats, tiles, cores = lax.axis_size("lat"), lax.axis_size("tile"), lax.axis_size("core")
    lons = tiles * cores
    names = ("lat", "tile", "core")

    def moved(value, dlat, dlon):
        pairs = []
        for a in range(lats):
            for b in range(lons):
                pairs.append((a * lons + b, ((a + dlat) % lats) * lons + (b + dlon) % lons))
        return lax.ppermute(value, names, pairs)

    beside = moved(jnp.concatenate([tokens[:, :SLON], cotangent[:, :SLON]], axis=0), 0, -1)
    work = jnp.concatenate([tokens[:, SLON:], beside[:ROWS]], axis=1)
    cwork = jnp.concatenate([cotangent[:, SLON:], beside[ROWS:]], axis=1)
    first, last = SLAT, ROWS - SLAT
    below = moved(jnp.concatenate([work[:9], cwork[:4]], axis=0), -1, 0)
    above = moved(work[last:], 1, 0)

    x_early = work[first:last].reshape(EARLY * WR, D)
    early = start_early(x_early, norm_gain, w_qkv, w_proj)
    early, below, above = lax.optimization_barrier((early, below, above))

    x = jnp.concatenate([work[last:], below[:9], above, work[:first]], axis=0)
    x = x.reshape((NWR - EARLY) * WR, D)
    c = jnp.concatenate([cwork, below[9:]], axis=0).reshape(CROWS * COLS, D)

    mine, other, gn, dqkv = compute(
        tiles, lats, early, x, c, norm_gain, w_qkv, w_proj, merge_gain, w_merge, w_expand, expand_gain
    )

    theirs = lax.ppermute(other, "core", [(i, cores - 1 - i) for i in range(cores)])
    pair, dqkv = lax.optimization_barrier((pair_sum(mine, theirs), dqkv))
    spread = lax.all_to_all(pair, "tile", 0, 0, tiled=True)

    d_work = finish_tokens(x_early, x, gn, dqkv, w_qkv, norm_gain).reshape(ROWS, COLS, D)
    last_row, last_col = ROWS - SLAT, COLS - SLON
    rows = moved(d_work[last_row:, :last_col], 1, 0)
    corner = moved(d_work[last_row:, last_col:], 1, 1)
    edge = d_work[:last_row, last_col:]
    spread, rows, corner, edge = lax.optimization_barrier((spread, rows, corner, edge))
    columns = moved(edge, 0, 1)
    top = jnp.concatenate([corner, rows], axis=1)
    rest = jnp.concatenate([columns, d_work[:last_row, :last_col]], axis=1)
    d_tokens = jnp.concatenate([top, rest], axis=0)

    gathered = lax.all_to_all(share_copies(spread, lats), "lat", 0, 0, tiled=True)
    grad_qkv, grad_proj = total_sum(gathered)
    return (d_tokens, grad_qkv, grad_proj)


def solution(mesh):
    lats, lons = mesh.shape["lat"], mesh.shape["lon"]
    fine_mesh = Mesh(mesh.devices.reshape(lats, lons // 2, 2), ("lat", "tile", "core"))
    lon = ("tile", "core")
    in_specs = (P("lat", lon, None), P("lat", lon, None), P(), P(), P(), P(), P(), P(), P())
    out_specs = (P("lat", lon, None), P(lon, None), P(lon, None))
    return jax.shard_map(body, mesh=fine_mesh, in_specs=in_specs, out_specs=out_specs, check_vma=False)
```
